32 devices in a mesh: tensor: 2 (over x), ctx: 4 (over z), dp: 4 (over y, core).
Axes of the slice: x: 2, y: 2, z: 4, core: 2. Of those that a mesh axis runs over, the one named last changes fastest.
Arguments:
- states: bfloat16 [4, 512, 2048], P('dp', 'ctx'), may hold values from -6 to 6
- lengths: int32 [4], P('dp'), may hold values from 1 to 512, 1280 in all
- first_gain: bfloat16 [2048], P(('ctx', 'dp')), may hold values from 0.25 to 1.75
- w_query: bfloat16 [2048, 2048], P(('ctx', 'dp'), 'tensor'), may hold values from -0.125 to 0.125
- key_matrix: bfloat16 [2048, 256], P(('ctx', 'dp'), 'tensor'), may hold values from -0.125 to 0.125
- value_matrix: bfloat16 [2048, 256], P(('ctx', 'dp'), 'tensor'), may hold values from -0.125 to 0.125
- w_out: bfloat16 [2048, 2048], P('tensor', ('ctx', 'dp')), may hold values from -1 to 1
- second_gain: bfloat16 [2048], P(('ctx', 'dp')), may hold values from 0.25 to 1.75
- w_gate: bfloat16 [2048, 5632], P(('ctx', 'dp'), 'tensor'), may hold values from -0.125 to 0.125
- w_up: bfloat16 [2048, 5632], P(('ctx', 'dp'), 'tensor'), may hold values from -0.125 to 0.125
- w_down: bfloat16 [5632, 2048], P('tensor', ('ctx', 'dp')), may hold values from -0.078125 to 0.078125
- cotangent: bfloat16 [4, 512, 2048], P('dp', 'ctx'), may hold values from -6 to 6
Outputs:
- layer_out: bfloat16 [4, 512, 2048], P('dp', 'ctx')
- grad_states: float32 [4, 512, 2048], P('dp', 'ctx')
- grad_first_gain: float32 [2048], P(('ctx', 'dp'))
- grad_query: float32 [2048, 2048], P(('ctx', 'dp'), 'tensor')
- grad_key: float32 [2048, 256], P(('ctx', 'dp'), 'tensor')
- grad_value: float32 [2048, 256], P(('ctx', 'dp'), 'tensor')
- grad_out: float32 [2048, 2048], P('tensor', ('ctx', 'dp'))
- grad_second_gain: float32 [2048], P(('ctx', 'dp'))
- grad_gate: float32 [2048, 5632], P(('ctx', 'dp'), 'tensor')
- grad_up: float32 [2048, 5632], P(('ctx', 'dp'), 'tensor')
- grad_down: float32 [5632, 2048], P('tensor', ('ctx', 'dp'))
The draws below stay inside these ranges and needn't reach their ends.
Inputs may be any that keep to these rules, and one draw needn't show every extreme that they name: Slot s holds lengths[s] real tokens followed by padding; one slot is full, and the lengths add up to 1280.
All inputs are finite; a program needn't handle non-finite values. No bound on the sum of `lengths` on one device may be relied on, other than what follows from the above.
Results may differ from the reference program's by a relative error of at most 0.015.
Values may be sent and summed in bfloat16 or wider, within the bound.
A program may use at most 256 MiB of HBM per device.

```python
import math
import jax
import jax.numpy as jnp
import numpy as np
from jax import lax

MODEL_WIDTH = 2048
QUERY_HEADS = 32
KEY_VALUE_HEADS = 4
HEAD_SIZE = 64
FF = 5632
SLOT_LEN = 512
SLOTS = 4


def block_levels(rng, shape, cuts, low, largest):
    def one(position, blocks):
        steps = jax.random.uniform(jax.random.fold_in(jax.random.fold_in(rng, 6), position), (blocks,), jnp.float32, low / len(cuts), largest / len(cuts))
        return jnp.repeat(jnp.exp(steps), shape[position] // blocks).reshape((-1,) + (1,) * (len(shape) - position - 1))

    factor_of = one(*cuts[0])
    for cut in cuts[1:]:
        factor_of = factor_of * one(*cut)
    return factor_of


def split_up(number_of, total, limit, lean):
    loads = [(1 << 20) // math.isqrt(grade ** lean) + 1 for grade in range(2, number_of + 1)]
    surplus, given = total - limit - (number_of - 1), [1] * (number_of - 1)
    while surplus > 0:
        free = [i for i in range(number_of - 1) if given[i] < limit]
        pool, left = sum([loads[i] for i in free]), surplus
        for i in free:
            addition = min(limit - given[i], max(1, left * loads[i] // pool), surplus)
            given[i] = given[i] + addition
            surplus = surplus - addition
    return np.array([limit] + given)


def ragged_sizes(rng, count, total, limit, skew):
    if count == 2:
        one = jax.random.randint(rng, (), max(1, total - limit), min(limit, total - 1) + 1)
        return jnp.stack([one, total - one])
    sizes = jnp.asarray(split_up(count, total, limit, skew), jnp.int32)
    couples = (count - 1) // 2
    donor, taker = sizes[1:1 + 2 * couples:2], sizes[2:2 + 2 * couples:2]
    margin = jnp.minimum(donor - 1, limit - taker)
    passed = jax.random.randint(jax.random.fold_in(rng, 1), (couples,), 0, 1 << 20) % (margin + 1)
    sizes = sizes.at[1:1 + 2 * couples:2].set(donor - passed).at[2:2 + 2 * couples:2].set(taker + passed)
    return sizes[jax.random.permutation(jax.random.fold_in(rng, 2), count)]


def gaussian(rng, extent, spread, most, cuts=(), held_as=jnp.bfloat16):
    result = jax.random.normal(rng, extent, jnp.float32) * spread
    if len(cuts) > 0:
        result = block_levels(rng, extent, cuts, -0.22, 0.18) * result
    return jnp.clip(result, min=-most, max=most).astype(held_as)


def setup_inputs(seed: int = 0) -> dict:
    splits = jax.random.split(jax.random.key(seed), 13)
    return {
        "states": gaussian(splits[0], (SLOTS, SLOT_LEN, MODEL_WIDTH), 1.0, 6.0, ((0, 4), (1, 4))),
        "lengths": ragged_sizes(splits[1], SLOTS, 5 * SLOT_LEN // 2, SLOT_LEN, 1).astype(jnp.int32),
        "first_gain": jnp.clip(1.0 + 0.15 * jax.random.normal(splits[2], (MODEL_WIDTH,), jnp.float32), 0.25, 1.75).astype(jnp.bfloat16),
        "w_query": gaussian(splits[3], (MODEL_WIDTH, QUERY_HEADS * HEAD_SIZE), MODEL_WIDTH ** -0.5, 0.125, ((0, 16), (1, 2))),
        "key_matrix": gaussian(splits[4], (MODEL_WIDTH, KEY_VALUE_HEADS * HEAD_SIZE), MODEL_WIDTH ** -0.5, 0.125, ((0, 16), (1, 2))),
        "value_matrix": gaussian(splits[5], (MODEL_WIDTH, KEY_VALUE_HEADS * HEAD_SIZE), MODEL_WIDTH ** -0.5, 0.125, ((0, 16), (1, 2))),
        "w_out": gaussian(splits[6], (QUERY_HEADS * HEAD_SIZE, MODEL_WIDTH), (max(QUERY_HEADS * HEAD_SIZE // 64, 1)) ** -0.5, 1.0, ((0, 2), (1, 16))),
        "second_gain": jnp.clip(1.0 + 0.15 * jax.random.normal(splits[7], (MODEL_WIDTH,), jnp.float32), 0.25, 1.75).astype(jnp.bfloat16),
        "w_gate": gaussian(splits[8], (MODEL_WIDTH, FF), MODEL_WIDTH ** -0.5, 0.125, ((0, 16), (1, 2))),
        "w_up": gaussian(splits[9], (MODEL_WIDTH, FF), MODEL_WIDTH ** -0.5, 0.125, ((0, 16), (1, 2))),
        "w_down": gaussian(splits[10], (FF, MODEL_WIDTH), FF ** -0.5, 0.078125, ((0, 2), (1, 16))),
        "cotangent": gaussian(splits[11], (SLOTS, SLOT_LEN, MODEL_WIDTH), 1.0, 6.0, ((0, 4), (1, 4))),
    }


EPS = 1e-05
THETA = 10000.0
NEGATIVE = -1e+30
HIGH = lax.Precision.HIGHEST

@jax.custom_vjp
def lower_precision(v):
    return lax.optimization_barrier(v.astype(jnp.bfloat16)).astype(jnp.float32)

@jax.custom_vjp
def lower_precision_back(v):
    return v

def low_keep(v):
    return (lower_precision(v), None)

def low_pass(kept, grad):
    return (grad,)

def back_keep(v):
    return (v, None)

def back_low(kept, grad):
    return (lower_precision(grad),)
lower_precision.defvjp(low_keep, low_pass)
lower_precision_back.defvjp(back_keep, back_low)

def matrix_multiply(left, right):
    return jnp.dot(left, right, precision=HIGH, preferred_element_type=jnp.float32)

def rope_tables(positions, half_width):
    inverse = jnp.exp(-jnp.log(THETA) * jnp.arange(half_width).astype(jnp.float32) / half_width)
    angles = positions.astype(jnp.float32)[:, None] * inverse[None, :]
    return (jnp.cos(angles)[:, None, :], jnp.sin(angles)[:, None, :])

def apply_rotation(vectors, cosine_table, sine_table):
    half_width = vectors.shape[-1] // 2
    first_half = vectors[..., :half_width]
    second_half = vectors[..., half_width:]
    return jnp.concatenate([first_half * cosine_table - second_half * sine_table, second_half * cosine_table + first_half * sine_table], axis=-1)

def layer(inputs, seq_length, gain_one, w_query, key_matrix, value_matrix, w_out, gain_two, w_gate, w_up, w_down):
    combined_length = inputs.shape[0]
    group_factor = QUERY_HEADS // KEY_VALUE_HEADS
    scale = HEAD_SIZE ** (-0.5)
    positions = jnp.arange(combined_length, dtype=jnp.int32)
    cosine_table, sine_table = rope_tables(positions, HEAD_SIZE // 2)
    rms_one = lax.rsqrt(lax.optimization_barrier(jnp.mean(inputs * inputs, axis=-1, keepdims=True)) + EPS)
    first_normed = lower_precision(inputs * rms_one * gain_one)
    query_rows = lower_precision_back(matrix_multiply(first_normed, w_query)).reshape(combined_length, QUERY_HEADS, HEAD_SIZE)
    fresh_keys = lower_precision_back(matrix_multiply(first_normed, key_matrix)).reshape(combined_length, KEY_VALUE_HEADS, HEAD_SIZE)
    value_lower = lower_precision(lower_precision_back(matrix_multiply(first_normed, value_matrix))).reshape(combined_length, KEY_VALUE_HEADS, HEAD_SIZE)
    query_rotated = lower_precision(apply_rotation(query_rows, cosine_table, sine_table)).reshape(combined_length, KEY_VALUE_HEADS, group_factor, HEAD_SIZE)
    key_rot = lower_precision(apply_rotation(fresh_keys, cosine_table, sine_table))
    query_block = min(512, combined_length)

    def attend(begin_at):
        query_piece = lax.dynamic_slice_in_dim(query_rotated, begin_at, query_block, 0)
        scores = lower_precision_back(jnp.einsum('qkgd,pkd->kgqp', query_piece, key_rot, precision=HIGH) * scale)
        query_pos = begin_at + jnp.arange(query_block, dtype=jnp.int32)
        allowed = (positions[None, :] <= query_pos[:, None]) & (positions[None, :] < seq_length)
        scores = jnp.where(allowed, scores, NEGATIVE)
        shifted = jnp.exp(scores - lax.optimization_barrier(jnp.max(scores, axis=-1, keepdims=True)))
        probs = shifted / lax.optimization_barrier(jnp.sum(shifted, axis=-1, keepdims=True))
        return jnp.einsum('kgqp,pkd->qkgd', lower_precision(probs), value_lower, precision=HIGH)
    starts = jnp.arange(combined_length // query_block, dtype=jnp.int32) * query_block
    mixed = lax.map(jax.checkpoint(attend), starts).reshape(combined_length, QUERY_HEADS * HEAD_SIZE)
    mixed_low = lower_precision(lower_precision_back(mixed))
    hidden = inputs + lower_precision_back(matrix_multiply(mixed_low, w_out))
    rms_two = lax.rsqrt(lax.optimization_barrier(jnp.mean(hidden * hidden, axis=-1, keepdims=True)) + EPS)
    normed_two = lower_precision(hidden * rms_two * gain_two)
    gate = lower_precision_back(matrix_multiply(normed_two, w_gate))
    up_proj = lower_precision_back(matrix_multiply(normed_two, w_up))
    activated = lower_precision(gate * jax.nn.sigmoid(gate) * up_proj)
    return hidden + lower_precision_back(matrix_multiply(activated, w_down))

def reference(states, lengths, first_gain, w_query, key_matrix, value_matrix, w_out, second_gain, w_gate, w_up, w_down, cotangent):
    weights = tuple((entry.astype(jnp.float32) for entry in (first_gain, w_query, key_matrix, value_matrix, w_out, second_gain, w_gate, w_up, w_down)))
    slot_len = states.shape[1]

    def one_slot(totals, entry):
        inputs, seq_length, upstream = entry
        valid = (jnp.arange(slot_len, dtype=jnp.int32) < seq_length)[:, None]

        def forward(inputs_f, *params):
            return layer(inputs_f, seq_length, *params)
        output, pull = jax.vjp(forward, inputs.astype(jnp.float32), *weights)
        grads = pull(jnp.where(valid, upstream.astype(jnp.float32), 0.0))
        totals = tuple((left + right for left, right in zip(totals, grads[1:])))
        return (totals, (output.astype(jnp.bfloat16), grads[0]))
    zeros = tuple((jnp.zeros_like(entry) for entry in weights))
    totals, (outputs, grad_states) = lax.scan(one_slot, zeros, (states, lengths, cotangent))
    return (outputs, grad_states, totals[0], totals[1], totals[2], totals[3], totals[4], totals[5], totals[6], totals[7], totals[8])
```

```python
import functools

import jax
import jax.numpy as jnp
from jax import lax
from jax.experimental import pallas as pl
from jax.experimental.pallas import tpu as pltpu
from jax.sharding import PartitionSpec as P

HEAD_SIZE = 64


EPS = 1e-05
THETA = 10000.0
NEGATIVE = -1e30


def rope_tables(positions, half_width):
    inverse = jnp.exp(-jnp.log(THETA) * jnp.arange(half_width).astype(jnp.float32) / half_width)
    angles = positions.astype(jnp.float32)[:, None] * inverse[None, :]
    return (jnp.cos(angles)[:, None, :], jnp.sin(angles)[:, None, :])


def apply_rotation(vectors, cosine_table, sine_table):
    half_width = vectors.shape[-1] // 2
    first_half = vectors[..., :half_width]
    second_half = vectors[..., half_width:]
    return jnp.concatenate(
        [
            first_half * cosine_table - second_half * sine_table,
            second_half * cosine_table + first_half * sine_table,
        ],
        axis=-1,
    )


def rotate_back(grads, cosine_table, sine_table):
    half_width = grads.shape[-1] // 2
    first_half = grads[..., :half_width]
    second_half = grads[..., half_width:]
    return jnp.concatenate(
        [
            first_half * cosine_table + second_half * sine_table,
            second_half * cosine_table - first_half * sine_table,
        ],
        axis=-1,
    )


def times_transposed(left, right):
    return lax.dot_general(
        left, right, (((1,), (1,)), ((), ())), preferred_element_type=jnp.float32
    )


def transposed_times(left, right):
    return lax.dot_general(
        left, right, (((0,), (0,)), ((), ())), preferred_element_type=jnp.float32
    )


def norm_back(upstream, inputs, inverse_rms, gain):
    scaled = upstream * gain
    gain_grad = jnp.sum(upstream * inputs * inverse_rms, axis=0)
    inner = jnp.mean(scaled * inputs, axis=-1, keepdims=True)
    return (inverse_rms * scaled - inputs * inverse_rms**3 * inner, gain_grad)


def shards(
    states,
    lengths,
    first_gain,
    w_query,
    key_matrix,
    value_matrix,
    w_out,
    second_gain,
    w_gate,
    w_up,
    w_down,
    cotangent,
):
    low_type = jnp.bfloat16
    wide_type = jnp.float32
    gathered = (
        lax.all_gather(first_gain, ("ctx", "dp"), axis=0, tiled=True),
        lax.all_gather(w_query, ("ctx", "dp"), axis=0, tiled=True),
        lax.all_gather(key_matrix, ("ctx", "dp"), axis=0, tiled=True),
        lax.all_gather(value_matrix, ("ctx", "dp"), axis=0, tiled=True),
        lax.all_gather(w_out, ("ctx", "dp"), axis=1, tiled=True),
        lax.all_gather(second_gain, ("ctx", "dp"), axis=0, tiled=True),
        lax.all_gather(w_gate, ("ctx", "dp"), axis=0, tiled=True),
        lax.all_gather(w_up, ("ctx", "dp"), axis=0, tiled=True),
        lax.all_gather(w_down, ("ctx", "dp"), axis=1, tiled=True),
    )
    (
        gain_one,
        full_query,
        full_key,
        full_value,
        full_out,
        gain_two,
        full_gate,
        full_up,
        full_down,
    ) = gathered
    gain_one = gain_one.astype(wide_type)
    gain_two = gain_two.astype(wide_type)
    tokens = states.shape[1]
    inputs = states[0].astype(wide_type)
    seq_length = lengths[0]
    first_pos = lax.axis_index("ctx") * tokens
    positions = first_pos + jnp.arange(tokens, dtype=jnp.int32)
    cosine_table, sine_table = rope_tables(positions, HEAD_SIZE // 2)
    heads = full_query.shape[1] // HEAD_SIZE
    kv_heads = full_key.shape[1] // HEAD_SIZE
    group_factor = heads // kv_heads
    scale = HEAD_SIZE ** (-0.5)
    rms_one = lax.rsqrt(jnp.mean(inputs * inputs, axis=-1, keepdims=True) + EPS)
    first_normed = (inputs * rms_one * gain_one).astype(low_type)
    query_rows = jnp.dot(first_normed, full_query, preferred_element_type=wide_type)
    fresh_keys = jnp.dot(first_normed, full_key, preferred_element_type=wide_type)
    values_new = jnp.dot(first_normed, full_value, preferred_element_type=wide_type)
    query_rotated = (
        apply_rotation(query_rows.reshape(tokens, heads, HEAD_SIZE), cosine_table, sine_table)
        .astype(low_type)
        .reshape(tokens, kv_heads, group_factor, HEAD_SIZE)
    )
    key_rot = (
        apply_rotation(fresh_keys.reshape(tokens, kv_heads, HEAD_SIZE), cosine_table, sine_table)
        .astype(low_type)
        .reshape(tokens, kv_heads * HEAD_SIZE)
    )
    value_lower = values_new.astype(low_type)
    keys_all, values_all = (
        lax.all_gather(key_rot, "ctx", axis=0, tiled=True),
        lax.all_gather(value_lower, "ctx", axis=0, tiled=True),
    )
    total_keys = keys_all.shape[0]
    key_block = min(512, total_keys)
    block_count = total_keys // key_block

    def block_scores(begin_at):
        key_piece = lax.dynamic_slice_in_dim(keys_all, begin_at, key_block, 0).reshape(
            key_block, kv_heads, HEAD_SIZE
        )
        value_piece = lax.dynamic_slice_in_dim(values_all, begin_at, key_block, 0).reshape(
            key_block, kv_heads, HEAD_SIZE
        )
        scores = (
            jnp.einsum("qkgd,pkd->kgqp", query_rotated, key_piece, preferred_element_type=wide_type)
            * scale
        )
        key_pos = begin_at + jnp.arange(key_block, dtype=jnp.int32)
        allowed = (key_pos[None, :] <= positions[:, None]) & (key_pos[None, :] < seq_length)
        return (jnp.where(allowed, scores, NEGATIVE), key_piece, value_piece)

    def max_pass(index, carry):
        running, total = carry
        scores = block_scores(index * key_block)[0]
        newest = jnp.maximum(running, jnp.max(scores, axis=-1))
        total = total * jnp.exp(running - newest) + jnp.sum(
            jnp.exp(scores - newest[..., None]), axis=-1
        )
        return (newest, total)

    start_max = jnp.full((kv_heads, group_factor, tokens), NEGATIVE, wide_type)
    running, total = lax.fori_loop(0, block_count, max_pass, (start_max, jnp.zeros_like(start_max)))
    log_total = running + jnp.log(total)

    def mix_pass(index, carry):
        scores, key_piece, value_piece = block_scores(index * key_block)
        weights = jnp.exp(scores - log_total[..., None]).astype(low_type)
        return carry + jnp.einsum(
            "kgqp,pkd->qkgd", weights, value_piece, preferred_element_type=wide_type
        )

    mixed = lax.fori_loop(
        0, block_count, mix_pass, jnp.zeros((tokens, kv_heads, group_factor, HEAD_SIZE), wide_type)
    )
    mixed_low = mixed.reshape(tokens, heads * HEAD_SIZE).astype(low_type)
    attention = lax.psum(jnp.dot(mixed_low, full_out, preferred_element_type=wide_type), "tensor")
    hidden = inputs + attention
    rms_two = lax.rsqrt(jnp.mean(hidden * hidden, axis=-1, keepdims=True) + EPS)
    normed_two = (hidden * rms_two * gain_two).astype(low_type)
    gate = jnp.dot(normed_two, full_gate, preferred_element_type=wide_type)
    up_proj = jnp.dot(normed_two, full_up, preferred_element_type=wide_type)
    sigma = jax.nn.sigmoid(gate)
    swish = gate * sigma
    activated = (swish * up_proj).astype(low_type)
    branch = lax.psum(
        jnp.dot(activated, full_down, preferred_element_type=wide_type).astype(jnp.bfloat16),
        "tensor",
    ).astype(jnp.float32)
    layer_out = (hidden + branch).astype(low_type)
    valid = (positions < seq_length)[:, None]
    grad_y = jnp.where(valid, cotangent[0].astype(wide_type), 0.0)
    grad_y_low = grad_y.astype(low_type)
    grad_down = transposed_times(activated, grad_y_low)
    grad_act = times_transposed(grad_y_low, full_down)
    grad_gate_low = (grad_act * up_proj * (sigma * (1.0 + gate * (1.0 - sigma)))).astype(low_type)
    grad_up_low = (grad_act * swish).astype(low_type)
    grad_gate = transposed_times(normed_two, grad_gate_low)
    grad_up = transposed_times(normed_two, grad_up_low)
    grad_normed_two = lax.psum(
        times_transposed(grad_gate_low, full_gate) + times_transposed(grad_up_low, full_up),
        "tensor",
    )
    norm_part, grad_gain_two = norm_back(grad_normed_two, hidden, rms_two, gain_two)
    grad_hidden = grad_y + norm_part
    grad_hidden_low = grad_hidden.astype(low_type)
    grad_out = transposed_times(mixed_low, grad_hidden_low)
    grad_mixed = (
        times_transposed(grad_hidden_low, full_out)
        .astype(low_type)
        .reshape(tokens, kv_heads, group_factor, HEAD_SIZE)
    )

    def delta_pass(index, carry):
        scores, key_piece, value_piece = block_scores(index * key_block)
        probs = jnp.exp(scores - log_total[..., None])
        dprob = jnp.einsum(
            "qkgd,pkd->kgqp", grad_mixed, value_piece, preferred_element_type=wide_type
        )
        return carry + jnp.sum(probs * dprob, axis=-1)

    delta = lax.fori_loop(
        0, block_count, delta_pass, jnp.zeros((kv_heads, group_factor, tokens), wide_type)
    )

    def grad_pass(index, carry):
        grad_queries, key_grads, value_grads = carry
        begin_at = index * key_block
        scores, key_piece, value_piece = block_scores(begin_at)
        probs = jnp.exp(scores - log_total[..., None])
        dprob = jnp.einsum(
            "qkgd,pkd->kgqp", grad_mixed, value_piece, preferred_element_type=wide_type
        )
        grad_scores = (probs * (dprob - delta[..., None])).astype(low_type)
        grad_queries = (
            grad_queries
            + jnp.einsum("kgqp,pkd->qkgd", grad_scores, key_piece, preferred_element_type=wide_type)
            * scale
        )
        key_part = (
            jnp.einsum(
                "kgqp,qkgd->pkd", grad_scores, query_rotated, preferred_element_type=wide_type
            )
            * scale
        )
        value_part = jnp.einsum(
            "kgqp,qkgd->pkd", probs.astype(low_type), grad_mixed, preferred_element_type=wide_type
        )
        key_grads = lax.dynamic_update_slice_in_dim(
            key_grads, key_part.reshape(key_block, kv_heads * HEAD_SIZE), begin_at, 0
        )
        value_grads = lax.dynamic_update_slice_in_dim(
            value_grads, value_part.reshape(key_block, kv_heads * HEAD_SIZE), begin_at, 0
        )
        return (grad_queries, key_grads, value_grads)

    empty_keys = jnp.zeros((total_keys, kv_heads * HEAD_SIZE), wide_type)
    start_state = (
        jnp.zeros((tokens, kv_heads, group_factor, HEAD_SIZE), wide_type),
        empty_keys,
        empty_keys,
    )
    grad_queries, key_grads, value_grads = lax.fori_loop(0, block_count, grad_pass, start_state)
    key_local, value_local = (
        lax.psum_scatter(key_grads, "ctx", scatter_dimension=0, tiled=True),
        lax.psum_scatter(value_grads, "ctx", scatter_dimension=0, tiled=True),
    )
    grad_query_low = (
        rotate_back(grad_queries.reshape(tokens, heads, HEAD_SIZE), cosine_table, sine_table)
        .reshape(tokens, heads * HEAD_SIZE)
        .astype(low_type)
    )
    grad_key_low = (
        rotate_back(key_local.reshape(tokens, kv_heads, HEAD_SIZE), cosine_table, sine_table)
        .reshape(tokens, kv_heads * HEAD_SIZE)
        .astype(low_type)
    )
    grad_value_low = value_local.astype(low_type)
    grad_query = transposed_times(first_normed, grad_query_low)
    grad_key = transposed_times(first_normed, grad_key_low)
    grad_value = transposed_times(first_normed, grad_value_low)
    grad_normed_one = lax.psum(
        (
            times_transposed(grad_query_low, full_query)
            + times_transposed(grad_key_low, full_key)
            + times_transposed(grad_value_low, full_value)
        ).astype(jnp.bfloat16),
        "tensor",
    ).astype(jnp.float32)
    first_part, grad_gain_one = norm_back(grad_normed_one, inputs, rms_one, gain_one)
    grad_states = grad_hidden + first_part
    summed = tuple(
        (
            lax.psum_scatter(grad_gain_one, ("ctx", "dp"), scatter_dimension=0, tiled=True),
            lax.psum_scatter(grad_query, ("ctx", "dp"), scatter_dimension=0, tiled=True),
            lax.psum_scatter(grad_key, ("ctx", "dp"), scatter_dimension=0, tiled=True),
            lax.psum_scatter(grad_value, ("ctx", "dp"), scatter_dimension=0, tiled=True),
            lax.psum_scatter(grad_out, ("ctx", "dp"), scatter_dimension=1, tiled=True),
            lax.psum_scatter(grad_gain_two, ("ctx", "dp"), scatter_dimension=0, tiled=True),
            lax.psum_scatter(grad_gate, ("ctx", "dp"), scatter_dimension=0, tiled=True),
            lax.psum_scatter(grad_up, ("ctx", "dp"), scatter_dimension=0, tiled=True),
            lax.psum_scatter(grad_down, ("ctx", "dp"), scatter_dimension=1, tiled=True),
        )
    )
    return (
        layer_out[None],
        grad_states[None],
        summed[0],
        summed[1],
        summed[2],
        summed[3],
        summed[4],
        summed[5],
        summed[6],
        summed[7],
        summed[8],
    )


MESH = pl.DeviceIdType.MESH
HBM = pltpu.MemorySpace.HBM
VMEM = pltpu.MemorySpace.VMEM
STEPS = [(1, -1), (1, 1), (2, -1), (2, 1), (3, -1), (3, 1)]


def position():
    t, c, d = lax.axis_index("tensor"), lax.axis_index("ctx"), lax.axis_index("dp")
    return t, c, d // 2, d % 2


def only(cond, act):
    if cond is True:
        act()
    else:
        pl.when(cond)(act)


class Wires:
    def __init__(self, send, recv):
        self.send, self.recv, self.used, self.sent = send, recv, 0, []

    def index(self):
        self.used += 1
        return self.used - 1

    def copy(self, i, src, dst, device, lands=None):
        return pltpu.make_async_remote_copy(
            src_ref=src,
            dst_ref=dst,
            send_sem=self.send.at[i],
            recv_sem=self.recv.at[i if lands is None else lands],
            device_id=device,
            device_id_type=MESH,
        )

    def push(self, i, src, dst, device, cond=True, lands=None):
        only(cond, lambda: self.copy(i, src(), dst(), device, lands).start())
        self.sent.append((cond, lambda: self.copy(i, src(), dst(), device).wait_send()))

    def owe(self, i, src, cond=True):
        self.sent.append((cond, lambda: self.copy(i, src(), src(), position_id()).wait_send()))

    def arrive(self, i, dst, cond=True):
        def act():
            place = dst()
            self.copy(i, place, place, position_id()).wait_recv()

        only(cond, act)

    def local(self, i, src, dst):
        def make():
            return pltpu.make_async_copy(src(), dst(), self.send.at[i])

        make().start()
        self.sent.append((True, lambda: make().wait()))

    def fetch(self, i, src, dst):
        copy = pltpu.make_async_copy(src, dst, self.recv.at[i])
        copy.start()
        return copy

    def drain(self):
        for cond, act in self.sent:
            only(cond, act)
        self.sent = []


def position_id():
    t, c, y, e = position()
    return (t, c, y * 2 + e)


def greet(peers):
    barrier = pltpu.get_barrier_semaphore()
    count = 0
    for cond, device in peers:
        only(
            cond,
            functools.partial(
                pl.semaphore_signal, barrier, inc=1, device_id=device, device_id_type=MESH
            ),
        )
        count = count + (1 if cond is True else cond.astype(jnp.int32))
    pl.semaphore_wait(barrier, count)


def around(pos, chain=True, x=False, y=False, core=True, row=False):
    t, c, yy, e = pos
    d = yy * 2 + e
    peers = []
    if chain:
        peers += [(c < 3, (t, c + 1, d)), (c > 0, (t, c - 1, d))]
    if x:
        peers.append((True, (1 - t, c, d)))
    if y:
        peers.append((True, (t, c, (1 - yy) * 2 + e)))
    if core:
        peers.append((True, (t, c, yy * 2 + 1 - e)))
    return peers


def reach(c, s, sign):
    k = c + sign * s
    return k, ((k >= 0) if sign < 0 else (k <= 3))


def plane_gather(wires, pos, src, at):
    t, c, y, e = pos
    d, d_y, d_e = y * 2 + e, (1 - y) * 2 + e, y * 2 + 1 - e
    z_id = {key: wires.index() for key in STEPS}
    y_id = {key: wires.index() for key in [(0, 0)] + STEPS}
    e_id = {key: wires.index() for key in [(0, 0)] + STEPS}
    f_id = {key: wires.index() for key in [(0, 0)] + STEPS}
    fetch = wires.fetch(wires.index(), src(), at(c, d))

    def spread(key, block, place, cond):
        s, sign = key
        if s < 3:
            for way in ((-1, 1) if s == 0 else (sign,)):
                nxt = c - way
                here = (nxt >= 0) if way > 0 else (nxt <= 3)
                wires.push(
                    z_id[(s + 1, way)], block, place, (t, nxt, d),
                    here if cond is True else (cond & here),
                )
        wires.push(y_id[key], block, place, (t, c, d_y), cond)
        wires.push(e_id[key], block, place, (t, c, d_e), cond)

    def relay(key, cond):
        k = c + key[0] * key[1]
        place = lambda: at(k, d_y)
        wires.arrive(y_id[key], place, cond)
        wires.push(f_id[key], place, place, (t, c, d_e), cond)

    spread((0, 0), src, lambda: at(c, d), True)
    yield
    late = [((0, 0), True)]
    for key in STEPS:
        k, cond = reach(c, *key)
        place = lambda k=k: at(k, d)
        wires.arrive(z_id[key], place, cond)
        spread(key, place, place, cond)
        if key[1] > 0:
            for old in late:
                relay(*old)
            late = []
            yield
        late.append((key, cond))
    for old in late:
        relay(*old)
    yield
    for key in [(0, 0)] + STEPS:
        k, cond = (c, True) if key[0] == 0 else reach(c, *key)
        wires.arrive(e_id[key], lambda: at(k, d_e), cond)
        wires.arrive(f_id[key], lambda: at(k, (1 - y) * 2 + 1 - e), cond)
    fetch.wait()


def token_gather(wires, pos, src, at, half):
    t, c, y, e = pos
    d, d_e = y * 2 + e, y * 2 + 1 - e
    z_id = {key: wires.index() for key in STEPS}
    x_id = {key: wires.index() for key in STEPS}
    e_id = {key: wires.index() for key in STEPS}
    f_id = {key: wires.index() for key in STEPS}
    own = wires.index(), wires.index()
    here = wires.index(), wires.index()
    for way in (-1, 1):
        nxt = c - way
        wires.push(
            z_id[(1, way)], lambda: half(t), lambda: at(e, c, t), (t, nxt, d),
            (nxt >= 0) if way > 0 else (nxt <= 3),
        )
    for i in (0, 1):
        wires.push(own[i], lambda i=i: half(i), lambda i=i: at(e, c, i), (t, c, d_e))
    fetch = [wires.fetch(here[i], half(i), at(e, c, i)) for i in (0, 1)]
    yield

    def relay(key, cond):
        k = c + key[0] * key[1]
        place = lambda: at(e, k, 1 - t)
        wires.arrive(x_id[key], place, cond)
        wires.push(f_id[key], place, place, (t, c, d_e), cond)

    late = []
    for key in STEPS:
        k, cond = reach(c, *key)
        place = lambda k=k: at(e, k, t)
        wires.arrive(z_id[key], place, cond)
        s, sign = key
        if s < 3:
            nxt = c - sign
            ok = (nxt >= 0) if sign > 0 else (nxt <= 3)
            wires.push(z_id[(s + 1, sign)], place, place, (t, nxt, d), cond & ok)
        wires.push(x_id[key], place, place, (1 - t, c, d), cond)
        wires.push(e_id[key], place, place, (t, c, d_e), cond)
        if sign > 0:
            for old in late:
                relay(*old)
            late = []
            yield
        late.append((key, cond))
    for old in late:
        relay(*old)
    yield
    for i in (0, 1):
        wires.arrive(own[i], lambda i=i: at(1 - e, c, i))
    for key in STEPS:
        k, cond = reach(c, *key)
        wires.arrive(e_id[key], lambda: at(1 - e, k, t), cond)
        wires.arrive(f_id[key], lambda: at(1 - e, k, 1 - t), cond)
    for copy in fetch:
        copy.wait()


def unit_scatter(wires, pos, piece, place):
    t, c, y, e = pos
    me = c * 2 + e
    first = [wires.index() for _ in range(8)]
    second = [wires.index() for _ in range(8)]
    fetch = wires.fetch(first[0], piece(me), place(c, y * 2 + e))
    for i in range(1, 8):
        q = lax.rem(me + i, 8)
        wires.push(
            first[i], lambda q=q: piece(q), lambda: place(c, y * 2 + e), (t, q // 2, y * 2 + q % 2)
        )
    wires.push(
        second[0], lambda: piece(me), lambda: place(c, y * 2 + e), (t, c, (1 - y) * 2 + e)
    )
    yield
    for i in range(1, 8):
        q = lax.rem(me + 8 - i, 8)
        block = lambda q=q: place(q // 2, y * 2 + q % 2)
        wires.arrive(first[i], block)
        wires.push(second[i], block, block, (t, c, (1 - y) * 2 + e))
        yield
    yield
    for i in range(8):
        q = lax.rem(me + 8 - i, 8)
        wires.arrive(second[i], lambda q=q: place(q // 2, (1 - y) * 2 + q % 2))
    fetch.wait()


def run_all(parts):
    parts = list(parts)
    while parts:
        for part in list(parts):
            try:
                next(part)
            except StopIteration:
                parts.remove(part)


def rows(ref, start, size):
    return ref.at[pl.ds(pl.multiple_of(start, 16), size)]


def dot_nn(a, b):
    return lax.dot_general(a, b, (((1,), (0,)), ((), ())), preferred_element_type=jnp.float32)


def by_rows(count, step, act):
    def body(i, carry):
        act(pl.ds(pl.multiple_of(i * step, step), step))
        return carry

    lax.fori_loop(0, count // step, body, 0)


ORDER = (3, 0, 2, 1)


def chain_sum(wires, pos, height, value, keep, came, extra, done):
    t, c, y, e = pos
    d = y * 2 + e
    wide = jnp.float32
    r_id = [wires.index() for _ in range(4)]
    l_id = [wires.index() for _ in range(4)]

    def hop(k):
        place = keep(k)
        for go, edge, number, way in ((c < k, 0, r_id[k], 1), (c > k, 3, l_id[k], -1)):
            if (k == 0 and way > 0) or (k == 3 and way < 0):
                continue
            wires.arrive(number, lambda: came.at[k], go & (c != edge))

            def act():
                def first(r):
                    place[r] = value(k, r).astype(place.dtype)

                def later(r):
                    place[r] = (value(k, r) + came[k, r].astype(wide)).astype(place.dtype)

                pl.when(c == edge)(lambda: by_rows(height, 16, first))
                pl.when(c != edge)(lambda: by_rows(height, 16, later))

            pl.when(go)(act)
            target = (t, c + way, d)
            if way > 0:
                wires.push(number, lambda: keep(k), lambda: came.at[k], target, go)
            else:
                wires.push(number, lambda: keep(k), lambda: extra, target, go & (c == k + 1))
                wires.push(number, lambda: keep(k), lambda: came.at[k], target, go & (c > k + 1))

    def finish():
        for k in range(4):

            def act(k=k):
                if k > 0:
                    wires.arrive(r_id[k], lambda: came.at[k])
                if k < 3:
                    wires.arrive(l_id[k], lambda: extra)

                def add(r):
                    total = value(k, r)
                    if k > 0:
                        total = total + came[k, r].astype(wide)
                    if k < 3:
                        total = total + extra[r].astype(wide)
                    done(r, total)

                by_rows(height, 16, add)

            pl.when(c == k)(act)

    return hop, finish


def token_scatter(wires, pos, part, out, scratch):
    t, c, y, e = pos
    near, own, x_in, came, extra = scratch
    wide = jnp.float32
    tokens, half = x_in.shape[1], x_in.shape[2]
    d_e = y * 2 + 1 - e
    e_id = [wires.index() for _ in range(4)]
    x_id = [wires.index() for _ in range(4)]
    last = wires.index()
    mine = pl.ds(pl.multiple_of(t * half, 128), half)
    other = pl.ds(pl.multiple_of((1 - t) * half, 128), half)

    def begin(k, f):
        return pl.multiple_of((k * 2 + f) * tokens, 16)

    for k in ORDER:
        wires.push(
            e_id[k], lambda k=k: part.at[pl.ds(begin(k, 1 - e), tokens)],
            lambda k=k: near.at[k], (t, c, d_e),
        )
    fetch = [
        wires.fetch(wires.index(), part.at[pl.ds(begin(k, e), tokens)], own.at[k]) for k in range(4)
    ]
    yield
    for k in ORDER:
        fetch[k].wait()
        wires.arrive(e_id[k], lambda: near.at[k])

        def away(r):
            total = own[k, r, other].astype(wide) + near[k, r, other].astype(wide)
            near[k, r, other] = total.astype(near.dtype)

        by_rows(tokens, 16, away)
        wires.push(
            x_id[k], lambda k=k: near.at[k, :, other], lambda k=k: x_in.at[k], (1 - t, c, y * 2 + e)
        )
    yield

    def value(k, r):
        return (
            own[k, r, mine].astype(wide)
            + near[k, r, mine].astype(wide)
            + x_in[k, r].astype(wide)
        )

    def done(r, total):
        out[r, mine] = total.astype(out.dtype)

    hop, finish = chain_sum(
        wires, pos, tokens, value, lambda k: near.at[k, :, mine], came, extra, done
    )
    for k in ORDER:
        wires.arrive(x_id[k], lambda: x_in.at[k])
        hop(k)
        yield
    finish()
    wires.push(last, lambda: out.at[:, mine], lambda: out.at[:, mine], (1 - t, c, y * 2 + e))
    yield
    wires.arrive(last, lambda: out.at[:, other])


def token_scratch(tokens, width):
    low, half = jnp.bfloat16, width // 2
    return [
        pltpu.VMEM((4, tokens, width), low),
        pltpu.VMEM((4, tokens, width), low),
        pltpu.VMEM((4, tokens, half), low),
        pltpu.VMEM((4, tokens, half), low),
        pltpu.VMEM((tokens, half), low),
    ]


def plane_scatter(wires, pos, out_block, own_block, height, scratch, done):
    t, c, y, e = pos
    near, y_in, came, extra = scratch
    wide = jnp.float32
    d_y, d_e = (1 - y) * 2 + e, y * 2 + 1 - e
    e_id = {(k, f): wires.index() for k in range(4) for f in range(2)}
    y_id = [wires.index() for _ in range(4)]
    for f in range(2):
        yy = (1 - y) if f == 0 else y
        for k in ORDER:
            wires.push(
                e_id[k, f], lambda k=k, yy=yy: out_block(k, yy),
                lambda k=k, f=f: near.at[f * 4 + k], (t, c, d_e),
            )
    yield
    for k in ORDER:
        wires.arrive(e_id[k, 0], lambda: near.at[k])
        block = own_block(k, 1 - y)

        def away(r):
            total = block[r].astype(wide) + near[k, r].astype(wide)
            near[k, r] = total.astype(near.dtype)

        by_rows(height, 16, away)
        wires.push(y_id[k], lambda k=k: near.at[k], lambda k=k: y_in.at[k], (t, c, d_y))
        yield

    def value(k, r):
        return (
            own_block(k, y)[r].astype(wide)
            + near[4 + k, r].astype(wide)
            + y_in[k, r].astype(wide)
        )

    hop, finish = chain_sum(
        wires, pos, height, value, lambda k: near.at[4 + k], came, extra, done
    )
    for k in ORDER:
        wires.arrive(e_id[k, 1], lambda: near.at[4 + k])
        wires.arrive(y_id[k], lambda: y_in.at[k])
        hop(k)
        yield
    finish()


def plane_scratch(shape):
    low = jnp.bfloat16
    return [
        pltpu.VMEM((8,) + shape, low),
        pltpu.VMEM((4,) + shape, low),
        pltpu.VMEM((4,) + shape, low),
        pltpu.VMEM(shape, low),
    ]


def unit_gather(wires, pos, sums, out):
    t, c, y, e = pos
    units, lanes = sums.shape[2], out.shape[2]
    me = c * 2 + e
    o_id = [wires.index() for _ in range(8)]
    here = pl.ds(pl.multiple_of(me * units, 16), units)
    for i in range(1, 8):
        q = lax.rem(me + i, 8)
        wires.push(
            o_id[i],
            lambda q=q: sums.at[q // 2, :, :, pl.ds(pl.multiple_of((q % 2) * lanes, 128), lanes)],
            lambda: out.at[:, here], (t, q // 2, y * 2 + q % 2),
        )
    fetch = wires.fetch(
        wires.index(), sums.at[c, :, :, pl.ds(pl.multiple_of(e * lanes, 128), lanes)], out.at[:, here]
    )
    yield
    for i in range(1, 8):
        q = lax.rem(me + 8 - i, 8)
        wires.arrive(o_id[i], lambda: out.at[:, pl.ds(pl.multiple_of(q * units, 16), units)])
    fetch.wait()


def swap_halves(x):
    lane = lax.broadcasted_iota(jnp.int32, x.shape, 1)
    ahead, behind = pltpu.roll(x, x.shape[1] - 32, 1), pltpu.roll(x, 32, 1)
    return jnp.where(lax.rem(lane, 64) < 32, ahead, behind)


def head_probs(query, keys, allowed):
    scores = times_transposed(query, keys) * (HEAD_SIZE ** (-0.5))
    scores = jnp.where(allowed, scores, NEGATIVE)
    shifted = jnp.exp(scores - jnp.max(scores, axis=-1, keepdims=True))
    return shifted * (1.0 / jnp.sum(shifted, axis=-1, keepdims=True))


def norm_rows(upstream, inputs, gain):
    rms = lax.rsqrt(jnp.mean(inputs * inputs, axis=-1, keepdims=True) + EPS)
    gain_grad = jnp.sum(upstream * inputs * rms, axis=0, keepdims=True)
    scaled = upstream * gain
    inner = jnp.mean(scaled * inputs, axis=-1, keepdims=True)
    return rms * scaled - inputs * (rms * rms * rms * inner), gain_grad


def advance(parts, count=1):
    for _ in range(count):
        for part in list(parts):
            try:
                next(part)
            except StopIteration:
                parts.remove(part)


def backward_kernel(
    lengths, gn, part_b, g3, qkv_hbm, out_hbm, gain_all, hidden, states, gy, normed_one, q_rot, kv_all,
    mixed, cosine, sine,
    layer_out, grad_states, g3_out, gq_out, go_out, gain_out,
    send, recv, grad_low, branch, grad_hidden, mixed_t, go_part, grad_mixed, gqkv, normed_t, gq_part,
    dk, dv, kv_part, kv_in, pair_out, pair_in, gains, gain_in, qkv_all, out_all, *scratch,
):
    pos = position()
    t, c, y, e = pos
    low, wide = jnp.bfloat16, jnp.float32
    wires = Wires(send, recv)
    d = y * 2 + e
    me = c * 4 + d
    peers = [(True, (1 - t, c, d))]
    for i in range(1, 16):
        q = lax.rem(me + i, 16)
        peers.append((True, (t, q // 4, lax.rem(q, 4))))
    greet(peers)
    tokens, width = states.shape
    n_query = q_rot.shape[1]
    n_key = kv_all.shape[1] // 2
    lanes = go_out.shape[1]
    rows_out = go_out.shape[0]
    t_b, s_q, s_k, s_o = scratch[:5], scratch[5:9], scratch[9:13], scratch[13:17]
    load_out = wires.fetch(wires.index(), out_hbm, out_all)
    load_qkv = wires.fetch(wires.index(), qkv_hbm, qkv_all)

    units = [unit_gather(wires, pos, g3, g3_out)]
    second = [token_scatter(wires, pos, part_b, branch, t_b)]
    advance(units)
    mixed_t[...] = mixed[...].T
    normed_t[...] = normed_one[...].T
    advance(second)

    gains[...] = jnp.zeros_like(gains)
    gain_one = gain_all[...].astype(wide)[0:1]
    gain_two = gain_all[...].astype(wide)[1:2]

    def norm_two(r):
        value, grad = norm_rows(gn[r].astype(wide), hidden[r], gain_two)
        total = gy[r].astype(wide) + value
        grad_hidden[r] = total
        grad_low[r] = total.astype(low)
        gains[1:2] += grad

    by_rows(tokens, 16, norm_two)

    def out_grad(j, carry):
        where = pl.ds(pl.multiple_of(j * 2 * lanes, 256), 2 * lanes)
        go_part[j] = dot_nn(mixed_t[...], grad_low[:, where]).astype(low)
        return carry

    lax.fori_loop(0, 8, out_grad, 0)
    outs = [
        plane_scatter(
            wires, pos,
            lambda k, yy: go_part.at[k * 2 + yy, :, pl.ds(pl.multiple_of((1 - e) * lanes, 128), lanes)],
            lambda k, yy: go_part.at[k * 2 + yy, :, pl.ds(pl.multiple_of(e * lanes, 128), lanes)],
            rows_out, s_o, lambda r, v: go_out.__setitem__(r, v),
        )
    ]
    advance(outs)

    load_out.wait()

    def mix_grad(j, carry):
        where = pl.ds(pl.multiple_of(j * 256, 256), 256)
        grad_mixed[:, where] = times_transposed(grad_low[...], out_all[where, :]).astype(low)
        return carry

    lax.fori_loop(0, n_query // 256, mix_grad, 0)

    q_pos = c * tokens + lax.broadcasted_iota(jnp.int32, (tokens, kv_all.shape[0]), 0)
    k_pos = lax.broadcasted_iota(jnp.int32, (tokens, kv_all.shape[0]), 1)
    allowed = (k_pos <= q_pos) & (k_pos < lengths[0])
    scale = HEAD_SIZE ** (-0.5)
    pairs = n_query // 256
    for g in range(2):
        keys = kv_all[:, g * HEAD_SIZE : (g + 1) * HEAD_SIZE]
        values = kv_all[:, n_key + g * HEAD_SIZE : n_key + (g + 1) * HEAD_SIZE]
        dk[...] = jnp.zeros_like(dk)
        dv[...] = jnp.zeros_like(dv)

        def pair(j, carry, g=g, keys=keys, values=values):
            slab = pl.ds(pl.multiple_of((g * pairs + j) * 128, 128), 128)
            q_two, m_two = q_rot[:, slab], grad_mixed[:, slab]
            both = []
            for h in range(2):
                query = q_two[:, h * HEAD_SIZE : (h + 1) * HEAD_SIZE]
                upstream = m_two[:, h * HEAD_SIZE : (h + 1) * HEAD_SIZE]
                probs = head_probs(query, keys, allowed)
                dprob = times_transposed(upstream, values)
                delta = jnp.sum(probs * dprob, axis=-1, keepdims=True)
                grad_scores = (probs * (dprob - delta)).astype(low)
                both.append(dot_nn(grad_scores, keys))
                dk[...] += transposed_times(grad_scores, query)
                dv[...] += transposed_times(probs.astype(low), upstream)
            grads = jnp.concatenate(both, axis=1) * scale
            back = grads * cosine[...] - swap_halves(grads) * sine[...]
            gqkv[:, slab] = back.astype(low)
            return carry

        lax.fori_loop(0, pairs, pair, 0)
        for k in range(4):
            block = slice(k * tokens, (k + 1) * tokens)
            kv_part[k, :, g * HEAD_SIZE : (g + 1) * HEAD_SIZE] = (dk[block] * scale).astype(low)
            kv_part[k, :, n_key + g * HEAD_SIZE : n_key + (g + 1) * HEAD_SIZE] = dv[block].astype(low)
        advance(outs)

    kv_id = [wires.index() for _ in range(3)]
    for i in range(3):
        k = lax.rem(c + i + 1, 4)
        wires.push(kv_id[i], lambda k=k: kv_part.at[k], lambda i=i: kv_in.at[i], (t, k, d))

    def q_grad(core, where):
        def act(j, carry):
            owner = j * 2 + core
            here = pl.ds(pl.multiple_of(owner * lanes, 128), lanes)
            gq_part[owner, :, where] = dot_nn(normed_t[here, :], gqkv[:, where]).astype(low)
            return carry

        lax.fori_loop(0, 8, act, 0)

    def q_sums(where, scratches):
        def done(r, value):
            gq_out[r, where] = value

        return plane_scatter(
            wires, pos,
            lambda k, yy: gq_part.at[k * 4 + yy * 2 + 1 - e, :, where],
            lambda k, yy: gq_part.at[k * 4 + yy * 2 + e, :, where],
            gq_out.shape[0], scratches, done,
        )

    first, rest = slice(0, n_query), slice(n_query, n_query + 2 * n_key)
    q_grad(1 - e, first)
    queries = [q_sums(first, s_q)]
    advance(queries)
    q_grad(e, first)
    for _ in range(4):
        advance(queries)
    total = kv_part[c].astype(wide)
    for i in range(3):
        wires.arrive(kv_id[i], lambda: kv_in.at[i])
        total = total + kv_in[i].astype(wide)
    key_grads = total[:, :n_key]
    key_grads = key_grads * cosine[...] - swap_halves(key_grads) * sine[...]
    gqkv[:, n_query : n_query + n_key] = key_grads.astype(low)
    gqkv[:, n_query + n_key :] = total[:, n_key:].astype(low)
    q_grad(1 - e, rest)
    others = [q_sums(rest, s_k)]
    advance(others)
    q_grad(e, rest)
    load_qkv.wait()

    def normed_grad(j, carry):
        where = pl.ds(pl.multiple_of(j * 256, 256), 256)
        pair_out[:, where] = times_transposed(gqkv[...], qkv_all[where, :]).astype(low)
        return carry

    lax.fori_loop(0, width // 256, normed_grad, 0)
    p_id = wires.index()
    wires.push(p_id, lambda: pair_out, lambda: pair_in, (1 - t, c, d))
    for _ in range(4):
        advance(others)
    advance(second)
    wires.arrive(p_id, lambda: pair_in)

    def norm_one(r):
        upstream = pair_out[r].astype(wide) + pair_in[r].astype(wide)
        value, grad = norm_rows(upstream, states[r].astype(wide), gain_one)
        grad_states[r] = grad_hidden[r] + value
        gains[0:1] += grad

    by_rows(tokens, 16, norm_one)
    g_id = [wires.index() for _ in range(16)]

    def gain_block(q):
        return gains.at[:, pl.ds(pl.multiple_of(q * lanes, 128), lanes)]

    for i in range(1, 16):
        q = lax.rem(me + i, 16)
        wires.push(
            g_id[i], lambda q=q: gain_block(q), lambda i=i: gain_in.at[i],
            (t, q // 4, lax.rem(q, 4)),
        )
    while second or outs or queries or others:
        advance(outs)
        advance(queries)
        advance(others)
        advance(second)
    advance(units)

    def finish(r):
        layer_out[r] = (hidden[r] + branch[r].astype(wide)).astype(low)

    by_rows(tokens, 16, finish)
    gain = gains[:, pl.ds(pl.multiple_of(me * lanes, 128), lanes)]
    for i in range(1, 16):
        wires.arrive(g_id[i], lambda: gain_in.at[i])
        gain = gain + gain_in[i]
    gain_out[...] = gain
    wires.drain()


def backward_call(
    lengths, gn, part_b, g3, qkv_all, out_all, gain_all, hidden, states, gy, normed_one, q_rot, kv_all,
    mixed, cosine, sine,
):
    shape = jax.ShapeDtypeStruct
    low, wide = jnp.bfloat16, jnp.float32
    units = g3.shape[2]
    tokens, width = states.shape
    n_query, keys = q_rot.shape[1], kv_all.shape[0]
    n_all = qkv_all.shape[1]
    lanes = width // 16
    vm = pltpu.VMEM
    return pl.pallas_call(
        backward_kernel,
        name="backward",
        out_shape=(
            shape((tokens, width), low),
            shape((tokens, width), wide),
            shape((3, units * 8, lanes), low),
            shape((lanes, n_all), wide),
            shape((n_query, lanes), wide),
            shape((8, lanes), wide),
        ),
        in_specs=[pl.BlockSpec(memory_space=pltpu.MemorySpace.SMEM)]
        + [pl.BlockSpec(memory_space=VMEM)]
        + [pl.BlockSpec(memory_space=HBM)] * 4
        + [pl.BlockSpec(memory_space=VMEM)] * 10,
        out_specs=[
            pl.BlockSpec(memory_space=VMEM),
            pl.BlockSpec(memory_space=VMEM),
            pl.BlockSpec(memory_space=HBM),
            pl.BlockSpec(memory_space=VMEM),
            pl.BlockSpec(memory_space=VMEM),
            pl.BlockSpec(memory_space=VMEM),
        ],
        scratch_shapes=[
            pltpu.SemaphoreType.DMA((128,)),
            pltpu.SemaphoreType.DMA((128,)),
            vm((tokens, width), low),
            vm((tokens, width), low),
            vm((tokens, width), wide),
            vm((n_query, tokens), low),
            vm((8, n_query, 2 * lanes), low),
            vm((tokens, n_query), low),
            vm((tokens, n_all), low),
            vm((width, tokens), low),
            vm((16, lanes, n_all), low),
            vm((keys, HEAD_SIZE), wide),
            vm((keys, HEAD_SIZE), wide),
            vm((4, tokens, kv_all.shape[1]), low),
            vm((3, tokens, kv_all.shape[1]), low),
            vm((tokens, width), low),
            vm((tokens, width), low),
            vm((8, width), wide),
            vm((16, 8, lanes), wide),
            vm((width, n_all), low),
            vm((n_query, width), low),
        ]
        + token_scratch(tokens, width)
        + plane_scratch((lanes, n_query))
        + plane_scratch((lanes, n_all - n_query))
        + plane_scratch((n_query, lanes)),
        compiler_params=pltpu.CompilerParams(
            collective_id=3, has_side_effects=True, vmem_limit_bytes=63 << 20
        ),
    )(
        lengths, gn, part_b, g3, qkv_all, out_all, gain_all, hidden, states, gy, normed_one, q_rot,
        kv_all, mixed, cosine, sine,
    )


def pick(c, table):
    value = table[0]
    for i in range(1, 4):
        value = jnp.where(c == i, table[i], value)
    return value


NEAREST = ((0, 1, 2, 3), (1, 0, 2, 3), (2, 3, 1, 0), (3, 2, 1, 0))


def forward_kernel(
    lengths, states, gains, qkv, out_w, w3, gy, cosine, sine,
    qkv_out, out_out, gain_out, hidden_out, normed_out, q_out, kv_out, mixed_out, part_out, g3, gn,
    send, recv, qkv_all, out_all, gain_all, hidden, normed_one, q_rot, kv_all, mixed, part_b, gn_own,
    unit_out, unit_in, unit_own, scaled, w3_all, gy_all, nt_all, act, both, act_t, both_t, part_g,
    kv_own, pair_out, pair_in, nt, near, x_in, came,
):
    pos = position()
    t, c, y, e = pos
    low, wide = jnp.bfloat16, jnp.float32
    wires = Wires(send, recv)
    d = y * 2 + e
    me = c * 4 + d
    here, beside, over = (t, c, d), (t, c, y * 2 + 1 - e), (1 - t, c, d)
    peers = [(True, over)]
    for i in range(1, 16):
        q = lax.rem(me + i, 16)
        peers.append((True, (t, q // 4, lax.rem(q, 4))))
    greet(peers)
    tokens, width = states.shape
    half = width // 2
    block, n_all = qkv.shape
    n_query = q_rot.shape[1]
    n_key = (n_all - n_query) // 2
    lanes = out_w.shape[1]
    units = g3.shape[2]
    kept_out = []

    def save(src, dst):
        kept_out.append(wires.fetch(wires.index(), src, dst))

    def lane_block(q, size=lanes):
        return pl.ds(pl.multiple_of(q * size, 128), size)

    gain_id = [wires.index() for _ in range(16)]
    for i in range(1, 16):
        q = lax.rem(me + i, 16)
        wires.push(
            gain_id[i], lambda: gains, lambda: gain_all.at[:, lane_block(me)],
            (t, q // 4, lax.rem(q, 4)),
        )
    fetch_gain = wires.fetch(wires.index(), gains, gain_all.at[:, lane_block(me)])
    g_qkv = [
        plane_gather(wires, pos, lambda: qkv, lambda k, f: rows(qkv_all, (k * 4 + f) * block, block))
    ]
    g_out = [
        plane_gather(
            wires, pos, lambda: out_w, lambda k, f: out_all.at[:, lane_block(k * 4 + f)]
        )
    ]
    g_unit = [
        unit_scatter(
            wires, pos,
            lambda q: w3.at[:, pl.ds(pl.multiple_of(q * units, 16), units)],
            lambda k, f: w3_all.at[:, pl.ds(0, units), lane_block(k * 4 + f)],
        )
    ]

    def spot(ref):
        return lambda f, k, h: ref.at[
            pl.ds(pl.multiple_of((k * 2 + f) * tokens, 16), tokens), lane_block(h, half)
        ]

    g_gy = [token_gather(wires, pos, None, spot(gy_all), lambda h: gy.at[:, lane_block(h, half)])]
    advance(g_qkv)
    advance(g_gy)
    w3_all[:, units:, :] = jnp.zeros_like(w3_all[:, units:, :])

    def scale_rows(r):
        x = states[r].astype(wide)
        scaled[r] = x * lax.rsqrt(jnp.mean(x * x, axis=-1, keepdims=True) + EPS)

    by_rows(tokens, 16, scale_rows)
    advance(g_qkv)
    advance(g_out)
    advance(g_gy)
    advance(g_qkv)
    advance(g_out)
    advance(g_gy)
    advance(g_qkv)
    advance(g_out)
    advance(g_gy)
    while g_qkv:
        advance(g_qkv)
    fetch_gain.wait()
    for i in range(1, 16):
        q = lax.rem(me + 16 - i, 16)
        wires.arrive(gain_id[i], lambda: gain_all.at[:, lane_block(q)])
    gain_one = gain_all[...].astype(wide)[0:1]
    gain_two = gain_all[...].astype(wide)[1:2]

    save(qkv_all, qkv_out)
    save(gain_all, gain_out)

    def norm_one(r):
        normed_one[r] = (scaled[r] * gain_one).astype(low)

    by_rows(tokens, 16, norm_one)

    def turned(x):
        return x * cosine[...] + swap_halves(x) * sine[...]

    tail = dot_nn(normed_one[...], qkv_all[:, n_query:])
    kv_own[:, :n_key] = turned(tail[:, :n_key]).astype(low)
    kv_own[:, n_key:] = tail[:, n_key:].astype(low)
    kv_all[pl.ds(pl.multiple_of(c * tokens, 16), tokens)] = kv_own[...]
    kv_id = [wires.index() for _ in range(3)]
    for i in range(3):
        k = lax.rem(c + i + 1, 4)
        wires.push(kv_id[i], lambda: kv_own, lambda: rows(kv_all, c * tokens, tokens), (t, k, d))
    advance(g_unit)

    def project(j, carry):
        where = pl.ds(pl.multiple_of(j * 256, 256), 256)
        two = dot_nn(normed_one[...], qkv_all[:, where])
        for h in range(2):
            slab = pl.ds(pl.multiple_of(j * 256 + h * 128, 128), 128)
            q_rot[:, slab] = turned(two[:, h * 128 : (h + 1) * 128]).astype(low)
        return carry

    lax.fori_loop(0, n_query // 256, project, 0)
    advance(g_out)
    for i in range(3):
        k = lax.rem(c + 3 - i, 4)
        wires.arrive(kv_id[i], lambda: rows(kv_all, k * tokens, tokens))
    q_pos = c * tokens + lax.broadcasted_iota(jnp.int32, (tokens, kv_all.shape[0]), 0)
    k_pos = lax.broadcasted_iota(jnp.int32, (tokens, kv_all.shape[0]), 1)
    allowed = (k_pos <= q_pos) & (k_pos < lengths[0])
    pairs = n_query // 256
    for g in range(2):
        keys = kv_all[:, g * HEAD_SIZE : (g + 1) * HEAD_SIZE]
        values = kv_all[:, n_key + g * HEAD_SIZE : n_key + (g + 1) * HEAD_SIZE]

        def pair(j, carry, g=g, keys=keys, values=values):
            slab = pl.ds(pl.multiple_of((g * pairs + j) * 128, 128), 128)
            q_two = q_rot[:, slab]
            both_heads = []
            for h in range(2):
                probs = head_probs(q_two[:, h * HEAD_SIZE : (h + 1) * HEAD_SIZE], keys, allowed)
                both_heads.append(dot_nn(probs.astype(low), values))
            mixed[:, slab] = jnp.concatenate(both_heads, axis=1).astype(low)
            return carry

        lax.fori_loop(0, pairs, pair, 0)
        if g == 0:
            advance(g_out)
    save(kv_all, kv_out)
    save(q_rot, q_out)
    save(mixed, mixed_out)
    save(normed_one, normed_out)
    while g_out:
        advance(g_out)
    advance(g_unit)
    save(out_all, out_out)
    pair_id = [wires.index() for _ in range(4)]
    for i in range(4):
        for j in range(2):
            where = pl.ds(i * (width // 4) + j * (width // 8), width // 8)
            pair_out[:, where] = dot_nn(mixed[...], out_all[:, where]).astype(low)
        piece = pl.ds(i * (width // 4), width // 4)
        wires.push(pair_id[i], lambda p=piece: pair_out.at[:, p], lambda p=piece: pair_in.at[:, p], over)
    advance(g_unit, 2)
    for i in range(4):
        piece = pl.ds(i * (width // 4), width // 4)
        wires.arrive(pair_id[i], lambda: pair_in.at[:, piece])

    def norm_two(r):
        total = states[r].astype(wide) + (pair_out[r].astype(wide) + pair_in[r].astype(wide))
        hidden[r] = total
        factor = lax.rsqrt(jnp.mean(total * total, axis=-1, keepdims=True) + EPS)
        nt[r] = (total * factor * gain_two).astype(low)

    by_rows(tokens, 16, norm_two)
    save(hidden, hidden_out)

    gathers = []
    for source, target in ((nt, nt_all),):
        at = spot(target)
        z_id, x_id, e_id, f_id = [[wires.index() for _ in range(4)][0] for _ in range(4)]
        gathers.append((at, z_id, x_id, e_id, f_id))
        own_half = lambda h, source=source: source.at[:, lane_block(h, half)]
        for i in (3, 1, 2):
            k = lax.rem(c + i, 4)
            wires.push(
                wires.index(), lambda own=own_half: own(t), lambda at=at: at(e, c, t), (t, k, d),
                lands=z_id + c,
            )
        wires.push(e_id + c, lambda own=own_half: own(t), lambda at=at: at(e, c, t), beside)
        wires.push(f_id + c, lambda own=own_half: own(1 - t), lambda at=at: at(e, c, 1 - t), beside)
    at_home = pl.ds(pl.multiple_of((c * 2 + e) * tokens, 16), tokens)
    nt_all[at_home] = nt[...]
    advance(g_unit, 4)
    while g_gy:
        advance(g_gy)

    def nearest(j):
        return pick(c, [sum_of(j, NEAREST[i]) for i in range(4)])

    def sum_of(j, order):
        value = order[0]
        for i in range(1, 4):
            value = jnp.where(j == i, order[i], value)
        return value

    def stage_one(j):
        k = nearest(j)
        for at, z_id, x_id, e_id, f_id in gathers:
            wires.arrive(z_id + k, lambda: at(e, k, t))
            wires.copy(x_id + k, at(e, k, t), at(e, k, t), over).start()
            wires.copy(e_id + k, at(e, k, t), at(e, k, t), beside).start()

    def stage_two(j):
        k = nearest(j)
        for at, z_id, x_id, e_id, f_id in gathers:

            def act():
                wires.arrive(x_id + k, lambda: at(e, k, 1 - t))
                wires.copy(f_id + k, at(e, k, 1 - t), at(e, k, 1 - t), beside).start()

            pl.when(j > 0)(act)
        for at, z_id, x_id, e_id, f_id in gathers:
            wires.arrive(e_id + k, lambda: at(1 - e, k, t))
            wires.arrive(f_id + k, lambda: at(1 - e, k, 1 - t))

    n_id = [wires.index() for _ in range(4)][0]
    r_id = [wires.index() for _ in range(4)][0]

    def part_rows(k, f):
        return part_g.at[pl.ds(pl.multiple_of((k * 2 + f) * tokens, 16), tokens)]

    mine, other = lane_block(t, half), lane_block(1 - t, half)

    def stage_three(j):
        k = nearest(j)
        wires.arrive(n_id + k, lambda: near.at[k])
        ours = part_rows(k, e)

        def away(r):
            total = ours[r, other].astype(wide) + near[k, r, other].astype(wide)
            near[k, r, other] = total.astype(low)

        by_rows(tokens, 16, away)
        wires.copy(r_id + k, near.at[k, :, other], x_in.at[k], over).start()

    def kept(k, r):
        return (
            part_rows(k, e)[r, mine].astype(wide)
            + near[k, r, mine].astype(wide)
            + x_in[k, r].astype(wide)
        )

    s_id = [wires.index() for _ in range(4)][0]

    def stage_four(j):
        k = nearest(j)
        wires.arrive(r_id + k, lambda: x_in.at[k])

        def add(r):
            near[k, r, mine] = kept(k, r).astype(low)

        by_rows(tokens, 16, add)
        i = lax.rem(k - c + 4, 4)
        wires.copy(s_id + i, near.at[k, :, mine], came.at[i - 1], (t, k, d)).start()

    def swiglu(j, carry):
        stage_two(j)
        k = nearest(j)
        where = pl.ds(pl.multiple_of(k * 2 * tokens, 16), 2 * tokens)
        x = nt_all[where]
        gate = times_transposed(x, w3_all[0])
        up = times_transposed(x, w3_all[1])
        grad_act = times_transposed(gy_all[where], w3_all[2])
        sigma = jax.nn.sigmoid(gate)
        swish = gate * sigma
        act[where] = (swish * up).astype(low)
        wide_units = gate.shape[1]
        both[where, :wide_units] = (
            grad_act * up * (sigma * (1.0 + gate * (1.0 - sigma)))
        ).astype(low)
        both[where, wide_units:] = (grad_act * swish).astype(low)
        for i in range(4):
            piece = slice(i * (width // 4), (i + 1) * (width // 4))
            part_g[where, piece] = (
                dot_nn(both[where, :wide_units], w3_all[0, :, piece])
                + dot_nn(both[where, wide_units:], w3_all[1, :, piece])
            ).astype(low)
        wires.copy(n_id + k, part_rows(k, 1 - e), near.at[k], beside).start()
        for i in range(4):
            piece = slice(i * (width // 4), (i + 1) * (width // 4))
            part_b[where, piece] = dot_nn(act[where], w3_all[2, :, piece]).astype(low)
        pl.when(j > 0)(lambda: stage_three(j - 1))
        pl.when(j > 2)(lambda: stage_four(j - 2))
        return carry

    for j in range(1, 4):
        stage_one(j)
    while g_unit:
        advance(g_unit)
    lax.fori_loop(0, 4, swiglu, 0)
    save(part_b, part_out)
    stage_three(3)
    for k in range(4):
        away = c != k
        for at, z_id, x_id, e_id, f_id in gathers:
            half_at = lambda h, k=k, at=at: at(e, k, h)
            wires.owe(x_id + k, lambda f=half_at: f(t), away)
            wires.owe(e_id + k, lambda f=half_at: f(t), away)
            wires.owe(f_id + k, lambda f=half_at: f(1 - t), away)
        wires.owe(n_id + k, lambda k=k: part_rows(k, 1 - e))
        wires.owe(r_id + k, lambda k=k: near.at[k, :, other])
    for i in (1, 2, 3):
        k = lax.rem(c + i, 4)
        wires.owe(s_id + i, lambda k=k: near.at[k, :, mine])
    stage_four(2)
    act_t[...] = act[...].T
    both_t[...] = both[...].T

    def unit_grads(k, yy, place):
        where = lane_block(k * 2 + yy, 256)
        wide_units = act_t.shape[0]
        two = dot_nn(both_t[...], nt_all[:, where]).astype(low)
        place[k, 0] = two[:units]
        place[k, 1] = two[wide_units : wide_units + units]
        place[k, 2] = dot_nn(act_t[...], gy_all[:, where]).astype(low)[:units]

    u_id = [wires.index() for _ in range(4)][0]
    across = (t, c, (1 - y) * 2 + e)

    def send_units(k, carry):
        unit_grads(k, 1 - y, unit_out)
        wires.copy(u_id + k, unit_out.at[k], unit_in.at[k], across).start()
        return carry

    lax.fori_loop(0, 2, send_units, 0)
    stage_four(3)
    lax.fori_loop(2, 4, send_units, 0)
    for k in range(4):
        wires.owe(u_id + k, lambda k=k: unit_out.at[k])

    def keep_units(k, carry):
        unit_grads(k, y, unit_own)
        return carry

    lax.fori_loop(0, 2, keep_units, 0)
    wires.arrive(r_id + c, lambda: x_in.at[c])
    for i in (3, 1, 2):
        wires.arrive(s_id + i, lambda: came.at[i - 1])

    def done(r):
        total = kept(c, r)
        for i in range(3):
            total = total + came[i, r].astype(wide)
        gn_own[r, mine] = total.astype(low)

    by_rows(tokens, 16, done)
    last = wires.index()
    wires.push(last, lambda: gn_own.at[:, mine], lambda: gn_own.at[:, mine], over)
    lax.fori_loop(2, 4, keep_units, 0)
    g_save = wires.index(), wires.index(), wires.index(), wires.index()
    saves = []
    for k in range(4):
        wires.arrive(u_id + k, lambda: unit_in.at[k])
        for m in range(3):

            def add(r):
                both_y = unit_own[k, m, r].astype(wide) + unit_in[k, m, r].astype(wide)
                unit_own[k, m, r] = both_y.astype(low)

            by_rows(units, 16, add)
        saves.append(wires.fetch(g_save[k], unit_own.at[k], g3.at[k]))
    wires.arrive(last, lambda: gn_own.at[:, other])
    saves.append(wires.fetch(wires.index(), gn_own, gn))
    for copy in saves + kept_out:
        copy.wait()
    wires.drain()


def forward_call(lengths, states, gains, qkv, out_w, w3, gy, cosine, sine):
    shape = jax.ShapeDtypeStruct
    low, wide = jnp.bfloat16, jnp.float32
    tokens, width = states.shape
    n_query, lanes = out_w.shape
    n_all = qkv.shape[1]
    units = w3.shape[1] // 8
    padded = -(-units // 128) * 128
    all_tokens = tokens * 8
    half = width // 2
    vm = pltpu.VMEM
    return pl.pallas_call(
        forward_kernel,
        name="forward",
        out_shape=(
            shape((width, n_all), low),
            shape((n_query, width), low),
            shape((16, width), low),
            shape((tokens, width), wide),
            shape((tokens, width), low),
            shape((tokens, n_query), low),
            shape((tokens * 4, n_all - n_query), low),
            shape((tokens, n_query), low),
            shape((all_tokens, width), low),
            shape((4, 3, units, width // 8), low),
            shape((tokens, width), low),
        ),
        in_specs=[pl.BlockSpec(memory_space=pltpu.MemorySpace.SMEM), pl.BlockSpec(memory_space=VMEM)]
        + [pl.BlockSpec(memory_space=HBM)] * 5
        + [pl.BlockSpec(memory_space=VMEM)] * 2,
        out_specs=[pl.BlockSpec(memory_space=HBM)] * 11,
        scratch_shapes=[
            pltpu.SemaphoreType.DMA((200,)),
            pltpu.SemaphoreType.DMA((200,)),
            vm((width, n_all), low),
            vm((n_query, width), low),
            vm((16, width), low),
            vm((tokens, width), wide),
            vm((tokens, width), low),
            vm((tokens, n_query), low),
            vm((tokens * 4, n_all - n_query), low),
            vm((tokens, n_query), low),
            vm((all_tokens, width), low),
            vm((tokens, width), low),
            vm((4, 3, units, width // 8), low),
            vm((4, 3, units, width // 8), low),
            vm((4, 3, units, width // 8), low),
            vm((tokens, width), wide),
            vm((3, padded, width), low),
            vm((all_tokens, width), low),
            vm((all_tokens, width), low),
            vm((all_tokens, padded), low),
            vm((all_tokens, 2 * padded), low),
            vm((padded, all_tokens), low),
            vm((2 * padded, all_tokens), low),
            vm((all_tokens, width), low),
            vm((tokens, n_all - n_query), low),
            vm((tokens, width), low),
            vm((tokens, width), low),
            vm((tokens, width), low),
            vm((4, tokens, width), low),
            vm((4, tokens, half), low),
            vm((3, tokens, half), low),
        ],
        compiler_params=pltpu.CompilerParams(
            collective_id=1, has_side_effects=True, vmem_limit_bytes=63 << 20
        ),
    )(lengths, states, gains, qkv, out_w, w3, gy, cosine, sine)


def plane_shards(
    states, lengths, first_gain, w_query, key_matrix, value_matrix, w_out, second_gain,
    w_gate, w_up, w_down, cotangent,
):
    low, wide = jnp.bfloat16, jnp.float32
    tokens = states.shape[1]
    positions = lax.axis_index("ctx") * tokens + jnp.arange(tokens, dtype=jnp.int32)
    cosine, sine = rope_tables(positions, HEAD_SIZE // 2)
    lane = jnp.arange(2 * HEAD_SIZE)
    turn = jnp.where((lane % HEAD_SIZE) < HEAD_SIZE // 2, -1.0, 1.0)
    cosine = jnp.tile(cosine[:, 0], (1, 4))
    sine = jnp.tile(sine[:, 0], (1, 4)) * turn[None, :]
    valid = (positions < lengths[0])[:, None]
    grad_y = jnp.where(valid, cotangent[0], jnp.zeros((), low))
    n_query, n_key = w_query.shape[1], key_matrix.shape[1]
    lanes = w_out.shape[1]
    qkv = jnp.concatenate([w_query, key_matrix, value_matrix], axis=1)
    gains = jnp.concatenate(
        [first_gain[None], second_gain[None], jnp.zeros((14, lanes), low)], axis=0
    )
    w3 = jnp.stack([w_gate.T, w_up.T, w_down])
    qkv_all, out_all, gain_all, hidden, normed_one, q_rot, kv_all, mixed, part_b, g3, gn = (
        forward_call(lengths, states[0], gains, qkv, w_out, w3, grad_y, cosine, sine)
    )
    layer_out, grad_states, g3, gq, go, gain = backward_call(
        lengths, gn, part_b, g3, qkv_all, out_all, gain_all, hidden, states[0], grad_y,
        normed_one, q_rot, kv_all, mixed, cosine, sine,
    )
    return (
        layer_out[None],
        grad_states[None],
        gain[0],
        gq[:, :n_query],
        gq[:, n_query : n_query + n_key],
        gq[:, n_query + n_key :],
        go,
        gain[1],
        g3[0].T.astype(wide),
        g3[1].T.astype(wide),
        g3[2].astype(wide),
    )


def fits(mesh):
    return dict(mesh.shape) == {"tensor": 2, "ctx": 4, "dp": 4}


def solution(mesh):
    placed = (
        P("dp", "ctx", None),
        P("dp"),
        P(("ctx", "dp")),
        P(("ctx", "dp"), "tensor"),
        P(("ctx", "dp"), "tensor"),
        P(("ctx", "dp"), "tensor"),
        P("tensor", ("ctx", "dp")),
        P(("ctx", "dp")),
        P(("ctx", "dp"), "tensor"),
        P(("ctx", "dp"), "tensor"),
        P("tensor", ("ctx", "dp")),
        P("dp", "ctx", None),
    )
    return jax.shard_map(
        plane_shards if fits(mesh) else shards,
        mesh=mesh,
        in_specs=placed,
        out_specs=(
            P("dp", "ctx", None),
            P("dp", "ctx", None),
            P(("ctx", "dp")),
            P(("ctx", "dp"), "tensor"),
            P(("ctx", "dp"), "tensor"),
            P(("ctx", "dp"), "tensor"),
            P("tensor", ("ctx", "dp")),
            P(("ctx", "dp")),
            P(("ctx", "dp"), "tensor"),
            P(("ctx", "dp"), "tensor"),
            P("tensor", ("ctx", "dp")),
        ),
        check_vma=False,
    )
```

```python
import functools

import jax
import jax.numpy as jnp
from jax import lax
from jax.experimental import pallas as pl
from jax.experimental.pallas import tpu as pltpu
from jax.sharding import PartitionSpec as P

HEAD_SIZE = 64


EPS = 1e-05
THETA = 10000.0
NEGATIVE = -1e30


def rope_tables(positions, half_width):
    inverse = jnp.exp(-jnp.log(THETA) * jnp.arange(half_width).astype(jnp.float32) / half_width)
    angles = positions.astype(jnp.float32)[:, None] * inverse[None, :]
    return (jnp.cos(angles)[:, None, :], jnp.sin(angles)[:, None, :])


def apply_rotation(vectors, cosine_table, sine_table):
    half_width = vectors.shape[-1] // 2
    first_half = vectors[..., :half_width]
    second_half = vectors[..., half_width:]
    return jnp.concatenate(
        [
            first_half * cosine_table - second_half * sine_table,
            second_half * cosine_table + first_half * sine_table,
        ],
        axis=-1,
    )


def rotate_back(grads, cosine_table, sine_table):
    half_width = grads.shape[-1] // 2
    first_half = grads[..., :half_width]
    second_half = grads[..., half_width:]
    return jnp.concatenate(
        [
            first_half * cosine_table + second_half * sine_table,
            second_half * cosine_table - first_half * sine_table,
        ],
        axis=-1,
    )


def times_transposed(left, right):
    return lax.dot_general(
        left, right, (((1,), (1,)), ((), ())), preferred_element_type=jnp.float32
    )


def transposed_times(left, right):
    return lax.dot_general(
        left, right, (((0,), (0,)), ((), ())), preferred_element_type=jnp.float32
    )


def norm_back(upstream, inputs, inverse_rms, gain):
    scaled = upstream * gain
    gain_grad = jnp.sum(upstream * inputs * inverse_rms, axis=0)
    inner = jnp.mean(scaled * inputs, axis=-1, keepdims=True)
    return (inverse_rms * scaled - inputs * inverse_rms**3 * inner, gain_grad)


def shards(
    states,
    lengths,
    first_gain,
    w_query,
    key_matrix,
    value_matrix,
    w_out,
    second_gain,
    w_gate,
    w_up,
    w_down,
    cotangent,
):
    low_type = jnp.bfloat16
    wide_type = jnp.float32
    gathered = (
        lax.all_gather(first_gain, ("ctx", "dp"), axis=0, tiled=True),
        lax.all_gather(w_query, ("ctx", "dp"), axis=0, tiled=True),
        lax.all_gather(key_matrix, ("ctx", "dp"), axis=0, tiled=True),
        lax.all_gather(value_matrix, ("ctx", "dp"), axis=0, tiled=True),
        lax.all_gather(w_out, ("ctx", "dp"), axis=1, tiled=True),
        lax.all_gather(second_gain, ("ctx", "dp"), axis=0, tiled=True),
        lax.all_gather(w_gate, ("ctx", "dp"), axis=0, tiled=True),
        lax.all_gather(w_up, ("ctx", "dp"), axis=0, tiled=True),
        lax.all_gather(w_down, ("ctx", "dp"), axis=1, tiled=True),
    )
    (
        gain_one,
        full_query,
        full_key,
        full_value,
        full_out,
        gain_two,
        full_gate,
        full_up,
        full_down,
    ) = gathered
    gain_one = gain_one.astype(wide_type)
    gain_two = gain_two.astype(wide_type)
    tokens = states.shape[1]
    inputs = states[0].astype(wide_type)
    seq_length = lengths[0]
    first_pos = lax.axis_index("ctx") * tokens
    positions = first_pos + jnp.arange(tokens, dtype=jnp.int32)
    cosine_table, sine_table = rope_tables(positions, HEAD_SIZE // 2)
    heads = full_query.shape[1] // HEAD_SIZE
    kv_heads = full_key.shape[1] // HEAD_SIZE
    group_factor = heads // kv_heads
    scale = HEAD_SIZE ** (-0.5)
    rms_one = lax.rsqrt(jnp.mean(inputs * inputs, axis=-1, keepdims=True) + EPS)
    first_normed = (inputs * rms_one * gain_one).astype(low_type)
    query_rows = jnp.dot(first_normed, full_query, preferred_element_type=wide_type)
    fresh_keys = jnp.dot(first_normed, full_key, preferred_element_type=wide_type)
    values_new = jnp.dot(first_normed, full_value, preferred_element_type=wide_type)
    query_rotated = (
        apply_rotation(query_rows.reshape(tokens, heads, HEAD_SIZE), cosine_table, sine_table)
        .astype(low_type)
        .reshape(tokens, kv_heads, group_factor, HEAD_SIZE)
    )
    key_rot = (
        apply_rotation(fresh_keys.reshape(tokens, kv_heads, HEAD_SIZE), cosine_table, sine_table)
        .astype(low_type)
        .reshape(tokens, kv_heads * HEAD_SIZE)
    )
    value_lower = values_new.astype(low_type)
    keys_all, values_all = (
        lax.all_gather(key_rot, "ctx", axis=0, tiled=True),
        lax.all_gather(value_lower, "ctx", axis=0, tiled=True),
    )
    total_keys = keys_all.shape[0]
    key_block = min(512, total_keys)
    block_count = total_keys // key_block

    def block_scores(begin_at):
        key_piece = lax.dynamic_slice_in_dim(keys_all, begin_at, key_block, 0).reshape(
            key_block, kv_heads, HEAD_SIZE
        )
        value_piece = lax.dynamic_slice_in_dim(values_all, begin_at, key_block, 0).reshape(
            key_block, kv_heads, HEAD_SIZE
        )
        scores = (
            jnp.einsum("qkgd,pkd->kgqp", query_rotated, key_piece, preferred_element_type=wide_type)
            * scale
        )
        key_pos = begin_at + jnp.arange(key_block, dtype=jnp.int32)
        allowed = (key_pos[None, :] <= positions[:, None]) & (key_pos[None, :] < seq_length)
        return (jnp.where(allowed, scores, NEGATIVE), key_piece, value_piece)

    def max_pass(index, carry):
        running, total = carry
        scores = block_scores(index * key_block)[0]
        newest = jnp.maximum(running, jnp.max(scores, axis=-1))
        total = total * jnp.exp(running - newest) + jnp.sum(
            jnp.exp(scores - newest[..., None]), axis=-1
        )
        return (newest, total)

    start_max = jnp.full((kv_heads, group_factor, tokens), NEGATIVE, wide_type)
    running, total = lax.fori_loop(0, block_count, max_pass, (start_max, jnp.zeros_like(start_max)))
    log_total = running + jnp.log(total)

    def mix_pass(index, carry):
        scores, key_piece, value_piece = block_scores(index * key_block)
        weights = jnp.exp(scores - log_total[..., None]).astype(low_type)
        return carry + jnp.einsum(
            "kgqp,pkd->qkgd", weights, value_piece, preferred_element_type=wide_type
        )

    mixed = lax.fori_loop(
        0, block_count, mix_pass, jnp.zeros((tokens, kv_heads, group_factor, HEAD_SIZE), wide_type)
    )
    mixed_low = mixed.reshape(tokens, heads * HEAD_SIZE).astype(low_type)
    attention = lax.psum(jnp.dot(mixed_low, full_out, preferred_element_type=wide_type), "tensor")
    hidden = inputs + attention
    rms_two = lax.rsqrt(jnp.mean(hidden * hidden, axis=-1, keepdims=True) + EPS)
    normed_two = (hidden * rms_two * gain_two).astype(low_type)
    gate = jnp.dot(normed_two, full_gate, preferred_element_type=wide_type)
    up_proj = jnp.dot(normed_two, full_up, preferred_element_type=wide_type)
    sigma = jax.nn.sigmoid(gate)
    swish = gate * sigma
    activated = (swish * up_proj).astype(low_type)
    branch = lax.psum(
        jnp.dot(activated, full_down, preferred_element_type=wide_type).astype(jnp.bfloat16),
        "tensor",
    ).astype(jnp.float32)
    layer_out = (hidden + branch).astype(low_type)
    valid = (positions < seq_length)[:, None]
    grad_y = jnp.where(valid, cotangent[0].astype(wide_type), 0.0)
    grad_y_low = grad_y.astype(low_type)
    grad_down = transposed_times(activated, grad_y_low)
    grad_act = times_transposed(grad_y_low, full_down)
    grad_gate_low = (grad_act * up_proj * (sigma * (1.0 + gate * (1.0 - sigma)))).astype(low_type)
    grad_up_low = (grad_act * swish).astype(low_type)
    grad_gate = transposed_times(normed_two, grad_gate_low)
    grad_up = transposed_times(normed_two, grad_up_low)
    grad_normed_two = lax.psum(
        times_transposed(grad_gate_low, full_gate) + times_transposed(grad_up_low, full_up),
        "tensor",
    )
    norm_part, grad_gain_two = norm_back(grad_normed_two, hidden, rms_two, gain_two)
    grad_hidden = grad_y + norm_part
    grad_hidden_low = grad_hidden.astype(low_type)
    grad_out = transposed_times(mixed_low, grad_hidden_low)
    grad_mixed = (
        times_transposed(grad_hidden_low, full_out)
        .astype(low_type)
        .reshape(tokens, kv_heads, group_factor, HEAD_SIZE)
    )

    def delta_pass(index, carry):
        scores, key_piece, value_piece = block_scores(index * key_block)
        probs = jnp.exp(scores - log_total[..., None])
        dprob = jnp.einsum(
            "qkgd,pkd->kgqp", grad_mixed, value_piece, preferred_element_type=wide_type
        )
        return carry + jnp.sum(probs * dprob, axis=-1)

    delta = lax.fori_loop(
        0, block_count, delta_pass, jnp.zeros((kv_heads, group_factor, tokens), wide_type)
    )

    def grad_pass(index, carry):
        grad_queries, key_grads, value_grads = carry
        begin_at = index * key_block
        scores, key_piece, value_piece = block_scores(begin_at)
        probs = jnp.exp(scores - log_total[..., None])
        dprob = jnp.einsum(
            "qkgd,pkd->kgqp", grad_mixed, value_piece, preferred_element_type=wide_type
        )
        grad_scores = (probs * (dprob - delta[..., None])).astype(low_type)
        grad_queries = (
            grad_queries
            + jnp.einsum("kgqp,pkd->qkgd", grad_scores, key_piece, preferred_element_type=wide_type)
            * scale
        )
        key_part = (
            jnp.einsum(
                "kgqp,qkgd->pkd", grad_scores, query_rotated, preferred_element_type=wide_type
            )
            * scale
        )
        value_part = jnp.einsum(
            "kgqp,qkgd->pkd", probs.astype(low_type), grad_mixed, preferred_element_type=wide_type
        )
        key_grads = lax.dynamic_update_slice_in_dim(
            key_grads, key_part.reshape(key_block, kv_heads * HEAD_SIZE), begin_at, 0
        )
        value_grads = lax.dynamic_update_slice_in_dim(
            value_grads, value_part.reshape(key_block, kv_heads * HEAD_SIZE), begin_at, 0
        )
        return (grad_queries, key_grads, value_grads)

    empty_keys = jnp.zeros((total_keys, kv_heads * HEAD_SIZE), wide_type)
    start_state = (
        jnp.zeros((tokens, kv_heads, group_factor, HEAD_SIZE), wide_type),
        empty_keys,
        empty_keys,
    )
    grad_queries, key_grads, value_grads = lax.fori_loop(0, block_count, grad_pass, start_state)
    key_local, value_local = (
        lax.psum_scatter(key_grads, "ctx", scatter_dimension=0, tiled=True),
        lax.psum_scatter(value_grads, "ctx", scatter_dimension=0, tiled=True),
    )
    grad_query_low = (
        rotate_back(grad_queries.reshape(tokens, heads, HEAD_SIZE), cosine_table, sine_table)
        .reshape(tokens, heads * HEAD_SIZE)
        .astype(low_type)
    )
    grad_key_low = (
        rotate_back(key_local.reshape(tokens, kv_heads, HEAD_SIZE), cosine_table, sine_table)
        .reshape(tokens, kv_heads * HEAD_SIZE)
        .astype(low_type)
    )
    grad_value_low = value_local.astype(low_type)
    grad_query = transposed_times(first_normed, grad_query_low)
    grad_key = transposed_times(first_normed, grad_key_low)
    grad_value = transposed_times(first_normed, grad_value_low)
    grad_normed_one = lax.psum(
        (
            times_transposed(grad_query_low, full_query)
            + times_transposed(grad_key_low, full_key)
            + times_transposed(grad_value_low, full_value)
        ).astype(jnp.bfloat16),
        "tensor",
    ).astype(jnp.float32)
    first_part, grad_gain_one = norm_back(grad_normed_one, inputs, rms_one, gain_one)
    grad_states = grad_hidden + first_part
    summed = tuple(
        (
            lax.psum_scatter(grad_gain_one, ("ctx", "dp"), scatter_dimension=0, tiled=True),
            lax.psum_scatter(grad_query, ("ctx", "dp"), scatter_dimension=0, tiled=True),
            lax.psum_scatter(grad_key, ("ctx", "dp"), scatter_dimension=0, tiled=True),
            lax.psum_scatter(grad_value, ("ctx", "dp"), scatter_dimension=0, tiled=True),
            lax.psum_scatter(grad_out, ("ctx", "dp"), scatter_dimension=1, tiled=True),
            lax.psum_scatter(grad_gain_two, ("ctx", "dp"), scatter_dimension=0, tiled=True),
            lax.psum_scatter(grad_gate, ("ctx", "dp"), scatter_dimension=0, tiled=True),
            lax.psum_scatter(grad_up, ("ctx", "dp"), scatter_dimension=0, tiled=True),
            lax.psum_scatter(grad_down, ("ctx", "dp"), scatter_dimension=1, tiled=True),
        )
    )
    return (
        layer_out[None],
        grad_states[None],
        summed[0],
        summed[1],
        summed[2],
        summed[3],
        summed[4],
        summed[5],
        summed[6],
        summed[7],
        summed[8],
    )


MESH = pl.DeviceIdType.MESH
HBM = pltpu.MemorySpace.HBM
VMEM = pltpu.MemorySpace.VMEM
STEPS = [(1, -1), (1, 1), (2, -1), (2, 1), (3, -1), (3, 1)]


def position():
    t, c, d = lax.axis_index("tensor"), lax.axis_index("ctx"), lax.axis_index("dp")
    return t, c, d // 2, d % 2


def only(cond, act):
    if cond is True:
        act()
    else:
        pl.when(cond)(act)


class Wires:
    def __init__(self, send, recv):
        self.send, self.recv, self.used, self.sent = send, recv, 0, []

    def index(self):
        self.used += 1
        return self.used - 1

    def copy(self, i, src, dst, device, lands=None):
        return pltpu.make_async_remote_copy(
            src_ref=src,
            dst_ref=dst,
            send_sem=self.send.at[i],
            recv_sem=self.recv.at[i if lands is None else lands],
            device_id=device,
            device_id_type=MESH,
        )

    def push(self, i, src, dst, device, cond=True, lands=None):
        only(cond, lambda: self.copy(i, src(), dst(), device, lands).start())
        self.sent.append((cond, lambda: self.copy(i, src(), dst(), device).wait_send()))

    def owe(self, i, src, cond=True):
        self.sent.append((cond, lambda: self.copy(i, src(), src(), position_id()).wait_send()))

    def arrive(self, i, dst, cond=True):
        def act():
            place = dst()
            self.copy(i, place, place, position_id()).wait_recv()

        only(cond, act)

    def local(self, i, src, dst):
        def make():
            return pltpu.make_async_copy(src(), dst(), self.send.at[i])

        make().start()
        self.sent.append((True, lambda: make().wait()))

    def fetch(self, i, src, dst):
        copy = pltpu.make_async_copy(src, dst, self.recv.at[i])
        copy.start()
        return copy

    def drain(self):
        for cond, act in self.sent:
            only(cond, act)
        self.sent = []


def position_id():
    t, c, y, e = position()
    return (t, c, y * 2 + e)


def greet(peers):
    barrier = pltpu.get_barrier_semaphore()
    count = 0
    for cond, device in peers:
        only(
            cond,
            functools.partial(
                pl.semaphore_signal, barrier, inc=1, device_id=device, device_id_type=MESH
            ),
        )
        count = count + (1 if cond is True else cond.astype(jnp.int32))
    pl.semaphore_wait(barrier, count)


def around(pos, chain=True, x=False, y=False, core=True, row=False):
    t, c, yy, e = pos
    d = yy * 2 + e
    peers = []
    if chain:
        peers += [(c < 3, (t, c + 1, d)), (c > 0, (t, c - 1, d))]
    if x:
        peers.append((True, (1 - t, c, d)))
    if y:
        peers.append((True, (t, c, (1 - yy) * 2 + e)))
    if core:
        peers.append((True, (t, c, yy * 2 + 1 - e)))
    return peers


def reach(c, s, sign):
    k = c + sign * s
    return k, ((k >= 0) if sign < 0 else (k <= 3))


def plane_gather(wires, pos, src, at):
    t, c, y, e = pos
    d, d_y, d_e = y * 2 + e, (1 - y) * 2 + e, y * 2 + 1 - e
    z_id = {key: wires.index() for key in STEPS}
    y_id = {key: wires.index() for key in [(0, 0)] + STEPS}
    e_id = {key: wires.index() for key in [(0, 0)] + STEPS}
    f_id = {key: wires.index() for key in [(0, 0)] + STEPS}
    fetch = wires.fetch(wires.index(), src(), at(c, d))

    def spread(key, block, place, cond):
        s, sign = key
        if s < 3:
            for way in ((-1, 1) if s == 0 else (sign,)):
                nxt = c - way
                here = (nxt >= 0) if way > 0 else (nxt <= 3)
                wires.push(
                    z_id[(s + 1, way)], block, place, (t, nxt, d),
                    here if cond is True else (cond & here),
                )
        wires.push(y_id[key], block, place, (t, c, d_y), cond)
        wires.push(e_id[key], block, place, (t, c, d_e), cond)

    def relay(key, cond):
        k = c + key[0] * key[1]
        place = lambda: at(k, d_y)
        wires.arrive(y_id[key], place, cond)
        wires.push(f_id[key], place, place, (t, c, d_e), cond)

    spread((0, 0), src, lambda: at(c, d), True)
    yield
    late = [((0, 0), True)]
    for key in STEPS:
        k, cond = reach(c, *key)
        place = lambda k=k: at(k, d)
        wires.arrive(z_id[key], place, cond)
        spread(key, place, place, cond)
        if key[1] > 0:
            for old in late:
                relay(*old)
            late = []
            yield
        late.append((key, cond))
    for old in late:
        relay(*old)
    yield
    for key in [(0, 0)] + STEPS:
        k, cond = (c, True) if key[0] == 0 else reach(c, *key)
        wires.arrive(e_id[key], lambda: at(k, d_e), cond)
        wires.arrive(f_id[key], lambda: at(k, (1 - y) * 2 + 1 - e), cond)
    fetch.wait()


def token_gather(wires, pos, src, at, half):
    t, c, y, e = pos
    d, d_e = y * 2 + e, y * 2 + 1 - e
    z_id = {key: wires.index() for key in STEPS}
    x_id = {key: wires.index() for key in STEPS}
    e_id = {key: wires.index() for key in STEPS}
    f_id = {key: wires.index() for key in STEPS}
    own = wires.index(), wires.index()
    here = wires.index(), wires.index()
    for way in (-1, 1):
        nxt = c - way
        wires.push(
            z_id[(1, way)], lambda: half(t), lambda: at(e, c, t), (t, nxt, d),
            (nxt >= 0) if way > 0 else (nxt <= 3),
        )
    for i in (0, 1):
        wires.push(own[i], lambda i=i: half(i), lambda i=i: at(e, c, i), (t, c, d_e))
    fetch = [wires.fetch(here[i], half(i), at(e, c, i)) for i in (0, 1)]
    yield

    def relay(key, cond):
        k = c + key[0] * key[1]
        place = lambda: at(e, k, 1 - t)
        wires.arrive(x_id[key], place, cond)
        wires.push(f_id[key], place, place, (t, c, d_e), cond)

    late = []
    for key in STEPS:
        k, cond = reach(c, *key)
        place = lambda k=k: at(e, k, t)
        wires.arrive(z_id[key], place, cond)
        s, sign = key
        if s < 3:
            nxt = c - sign
            ok = (nxt >= 0) if sign > 0 else (nxt <= 3)
            wires.push(z_id[(s + 1, sign)], place, place, (t, nxt, d), cond & ok)
        wires.push(x_id[key], place, place, (1 - t, c, d), cond)
        wires.push(e_id[key], place, place, (t, c, d_e), cond)
        if sign > 0:
            for old in late:
                relay(*old)
            late = []
            yield
        late.append((key, cond))
    for old in late:
        relay(*old)
    yield
    for i in (0, 1):
        wires.arrive(own[i], lambda i=i: at(1 - e, c, i))
    for key in STEPS:
        k, cond = reach(c, *key)
        wires.arrive(e_id[key], lambda: at(1 - e, k, t), cond)
        wires.arrive(f_id[key], lambda: at(1 - e, k, 1 - t), cond)
    for copy in fetch:
        copy.wait()


def unit_scatter(wires, pos, piece, place):
    t, c, y, e = pos
    me = c * 2 + e
    first = [wires.index() for _ in range(8)]
    second = [wires.index() for _ in range(8)]
    fetch = wires.fetch(first[0], piece(me), place(c, y * 2 + e))
    for i in range(1, 8):
        q = lax.rem(me + i, 8)
        wires.push(
            first[i], lambda q=q: piece(q), lambda: place(c, y * 2 + e), (t, q // 2, y * 2 + q % 2)
        )
    wires.push(
        second[0], lambda: piece(me), lambda: place(c, y * 2 + e), (t, c, (1 - y) * 2 + e)
    )
    yield
    for i in range(1, 8):
        q = lax.rem(me + 8 - i, 8)
        block = lambda q=q: place(q // 2, y * 2 + q % 2)
        wires.arrive(first[i], block)
        wires.push(second[i], block, block, (t, c, (1 - y) * 2 + e))
        yield
    yield
    for i in range(8):
        q = lax.rem(me + 8 - i, 8)
        wires.arrive(second[i], lambda q=q: place(q // 2, (1 - y) * 2 + q % 2))
    fetch.wait()


def run_all(parts):
    parts = list(parts)
    while parts:
        for part in list(parts):
            try:
                next(part)
            except StopIteration:
                parts.remove(part)


def rows(ref, start, size):
    return ref.at[pl.ds(pl.multiple_of(start, 16), size)]


def dot_nn(a, b):
    return lax.dot_general(a, b, (((1,), (0,)), ((), ())), preferred_element_type=jnp.float32)


def by_rows(count, step, act):
    def body(i, carry):
        act(pl.ds(pl.multiple_of(i * step, step), step))
        return carry

    lax.fori_loop(0, count // step, body, 0)


ORDER = (3, 0, 2, 1)


def chain_sum(wires, pos, height, value, keep, came, extra, done):
    t, c, y, e = pos
    d = y * 2 + e
    wide = jnp.float32
    r_id = [wires.index() for _ in range(4)]
    l_id = [wires.index() for _ in range(4)]

    def hop(k):
        place = keep(k)
        for go, edge, number, way in ((c < k, 0, r_id[k], 1), (c > k, 3, l_id[k], -1)):
            if (k == 0 and way > 0) or (k == 3 and way < 0):
                continue
            wires.arrive(number, lambda: came.at[k], go & (c != edge))

            def act():
                def first(r):
                    place[r] = value(k, r).astype(place.dtype)

                def later(r):
                    place[r] = (value(k, r) + came[k, r].astype(wide)).astype(place.dtype)

                pl.when(c == edge)(lambda: by_rows(height, 16, first))
                pl.when(c != edge)(lambda: by_rows(height, 16, later))

            pl.when(go)(act)
            target = (t, c + way, d)
            if way > 0:
                wires.push(number, lambda: keep(k), lambda: came.at[k], target, go)
            else:
                wires.push(number, lambda: keep(k), lambda: extra, target, go & (c == k + 1))
                wires.push(number, lambda: keep(k), lambda: came.at[k], target, go & (c > k + 1))

    def finish():
        for k in range(4):

            def act(k=k):
                if k > 0:
                    wires.arrive(r_id[k], lambda: came.at[k])
                if k < 3:
                    wires.arrive(l_id[k], lambda: extra)

                def add(r):
                    total = value(k, r)
                    if k > 0:
                        total = total + came[k, r].astype(wide)
                    if k < 3:
                        total = total + extra[r].astype(wide)
                    done(r, total)

                by_rows(height, 16, add)

            pl.when(c == k)(act)

    return hop, finish


def token_scatter(wires, pos, part, out, scratch, credit):
    t, c, y, e = pos
    near, own, x_in, came, extra = scratch
    wide = jnp.float32
    tokens, half = x_in.shape[1], x_in.shape[2]
    d_e = y * 2 + 1 - e
    e_id = [wires.index() for _ in range(4)]
    x_id = [wires.index() for _ in range(4)]
    last = wires.index()
    mine = pl.ds(pl.multiple_of(t * half, 128), half)
    other = pl.ds(pl.multiple_of((1 - t) * half, 128), half)

    def begin(k, f):
        return pl.multiple_of((k * 2 + f) * tokens, 16)

    pl.semaphore_wait(credit.at[0], 1)
    for k in ORDER:
        wires.push(
            e_id[k], lambda k=k: part.at[pl.ds(begin(k, 1 - e), tokens)],
            lambda k=k: near.at[k], (t, c, d_e),
        )
    fetch = [
        wires.fetch(wires.index(), part.at[pl.ds(begin(k, e), tokens)], own(k)) for k in range(4)
    ]
    yield
    pl.semaphore_wait(credit.at[1], 1)
    for k in ORDER:
        fetch[k].wait()
        wires.arrive(e_id[k], lambda: near.at[k])

        def away(r):
            total = own(k)[r, other].astype(wide) + near[k, r, other].astype(wide)
            near[k, r, other] = total.astype(near.dtype)

        by_rows(tokens, 16, away)
        wires.push(
            x_id[k], lambda k=k: near.at[k, :, other], lambda k=k: x_in.at[k], (1 - t, c, y * 2 + e)
        )
    yield

    def value(k, r):
        return (
            own(k)[r, mine].astype(wide)
            + near[k, r, mine].astype(wide)
            + x_in[k, r].astype(wide)
        )

    def done(r, total):
        out[r, mine] = total.astype(out.dtype)

    hop, finish = chain_sum(
        wires, pos, tokens, value, lambda k: near.at[k, :, mine], came, extra, done
    )
    pl.when(c < 3)(lambda: pl.semaphore_wait(credit.at[2], 1))
    pl.when(c > 0)(lambda: pl.semaphore_wait(credit.at[3], 1))
    for k in ORDER:
        wires.arrive(x_id[k], lambda: x_in.at[k])
        hop(k)
        yield
    finish()
    wires.push(last, lambda: out.at[:, mine], lambda: out.at[:, mine], (1 - t, c, y * 2 + e))
    yield
    wires.arrive(last, lambda: out.at[:, other])


def plane_scatter(wires, pos, out_block, own_block, height, scratch, done):
    t, c, y, e = pos
    near, y_in, came, extra = scratch
    wide = jnp.float32
    d_y, d_e = (1 - y) * 2 + e, y * 2 + 1 - e
    e_id = {(k, f): wires.index() for k in range(4) for f in range(2)}
    y_id = [wires.index() for _ in range(4)]
    for f in range(2):
        yy = (1 - y) if f == 0 else y
        for k in ORDER:
            wires.push(
                e_id[k, f], lambda k=k, yy=yy: out_block(k, yy),
                lambda k=k, f=f: near.at[f * 4 + k], (t, c, d_e),
            )
    yield
    for k in ORDER:
        wires.arrive(e_id[k, 0], lambda: near.at[k])
        block = own_block(k, 1 - y)

        def away(r):
            total = block[r].astype(wide) + near[k, r].astype(wide)
            near[k, r] = total.astype(near.dtype)

        by_rows(height, 16, away)
        wires.push(y_id[k], lambda k=k: near.at[k], lambda k=k: y_in.at[k], (t, c, d_y))
        yield

    def value(k, r):
        return (
            own_block(k, y)[r].astype(wide)
            + near[4 + k, r].astype(wide)
            + y_in[k, r].astype(wide)
        )

    hop, finish = chain_sum(
        wires, pos, height, value, lambda k: near.at[4 + k], came, extra, done
    )
    for k in ORDER:
        wires.arrive(e_id[k, 1], lambda: near.at[4 + k])
        wires.arrive(y_id[k], lambda: y_in.at[k])
        hop(k)
        yield
    finish()


def plane_scratch(shape):
    low = jnp.bfloat16
    return [
        pltpu.VMEM((8,) + shape, low),
        pltpu.VMEM((4,) + shape, low),
        pltpu.VMEM((4,) + shape, low),
        pltpu.VMEM(shape, low),
    ]


def unit_gather(wires, pos, grads, came, y_id, out):
    t, c, y, e = pos
    wide = jnp.float32
    units, lanes = came.shape[2], out.shape[2]
    me = c * 2 + e
    o_id = [wires.index() for _ in range(8)]
    here = pl.ds(pl.multiple_of(me * units, 16), units)
    fetch = []
    for far in (1, 2, 3, 0):
        k = lax.rem(c + far, 4)
        wires.arrive(y_id + k, lambda: came.at[k])
        where = pl.ds(pl.multiple_of((k * 2 + y) * 2 * lanes, 256), 2 * lanes)
        for m in range(3):

            def add(r):
                both = grads[m, r, where].astype(wide) + came[k, m, r].astype(wide)
                grads[m, r, where] = both.astype(grads.dtype)

            by_rows(units, 16, add)
        for f in range(2):
            g = e if f == 0 else 1 - e
            src = lambda k=k, g=g: grads.at[
                :, pl.ds(0, units), pl.ds(pl.multiple_of(((k * 2 + y) * 2 + g) * lanes, 128), lanes)
            ]
            if far == 0 and f == 0:
                fetch.append(wires.fetch(wires.index(), src(), out.at[:, here]))
            else:
                wires.push(o_id[far * 2 + f], src, lambda: out.at[:, here], (t, k, y * 2 + g))
        yield
    for far in (1, 2, 3, 0):
        for f in range(2):
            if far == 0 and f == 0:
                continue
            k = lax.rem(c + 4 - far, 4)
            g = e if f == 0 else 1 - e
            wires.arrive(
                o_id[far * 2 + f],
                lambda: out.at[:, pl.ds(pl.multiple_of((k * 2 + g) * units, 16), units)],
            )
    fetch[0].wait()


def swap_halves(x):
    lane = lax.broadcasted_iota(jnp.int32, x.shape, 1)
    ahead, behind = pltpu.roll(x, x.shape[1] - 32, 1), pltpu.roll(x, 32, 1)
    return jnp.where(lax.rem(lane, 64) < 32, ahead, behind)


def head_probs(query, keys, allowed):
    scores = times_transposed(query, keys) * (HEAD_SIZE ** (-0.5))
    scores = jnp.where(allowed, scores, NEGATIVE)
    shifted = jnp.exp(scores - jnp.max(scores, axis=-1, keepdims=True))
    return shifted * (1.0 / jnp.sum(shifted, axis=-1, keepdims=True))


def norm_rows(upstream, inputs, gain):
    rms = lax.rsqrt(jnp.mean(inputs * inputs, axis=-1, keepdims=True) + EPS)
    gain_grad = jnp.sum(upstream * inputs * rms, axis=0, keepdims=True)
    scaled = upstream * gain
    inner = jnp.mean(scaled * inputs, axis=-1, keepdims=True)
    return rms * scaled - inputs * (rms * rms * rms * inner), gain_grad


def advance(parts, count=1):
    for _ in range(count):
        for part in list(parts):
            try:
                next(part)
            except StopIteration:
                parts.remove(part)


def pick(c, table):
    value = table[0]
    for i in range(1, 4):
        value = jnp.where(c == i, table[i], value)
    return value


NEAREST = ((0, 1, 2, 3), (1, 0, 2, 3), (2, 3, 1, 0), (3, 2, 1, 0))


def layer_kernel(
    lengths, states, gains, qkv, out_w, w3, gy, cosine, sine,
    layer_out, grad_states, g3_out, gq_out, go_out, gain_out, qkv_kept, part_b,
    send, recv, credit, qkv_all, out_all, gain_all, hidden, normed_one, q_rot, kv_all, mixed, gn_own,
    w3_all, gy_all, nt_all, act_t, part_g, stage_b, unit_in, kv_own, pair_out, pair_in, nt,
    near, x_in, came, grad_hidden, grad_low, branch, mixed_t, grad_mixed, gqkv, normed_t, gq_part,
    dk, dv, kv_part, kv_in, gains_sum, gain_in, *scratch,
):
    pos = position()
    t, c, y, e = pos
    low, wide = jnp.bfloat16, jnp.float32
    wires = Wires(send, recv)
    d = y * 2 + e
    me = c * 4 + d
    here, beside, over = (t, c, d), (t, c, y * 2 + 1 - e), (1 - t, c, d)
    peers = [(True, over)]
    for i in range(1, 16):
        q = lax.rem(me + i, 16)
        peers.append((True, (t, q // 4, lax.rem(q, 4))))
    greet(peers)
    tokens, width = states.shape
    half = width // 2
    block, n_all = qkv.shape
    n_query = q_rot.shape[1]
    n_key = (n_all - n_query) // 2
    lanes = out_w.shape[1]
    units = unit_in.shape[2]
    scaled = grad_hidden

    def lane_block(q, size=lanes):
        return pl.ds(pl.multiple_of(q * size, 128), size)

    gain_id = [wires.index() for _ in range(16)]
    for i in range(1, 16):
        q = lax.rem(me + i, 16)
        wires.push(
            gain_id[i], lambda: gains, lambda: gain_all.at[:, lane_block(me)],
            (t, q // 4, lax.rem(q, 4)),
        )
    fetch_gain = wires.fetch(wires.index(), gains, gain_all.at[:, lane_block(me)])
    g_qkv = [
        plane_gather(wires, pos, lambda: qkv, lambda k, f: rows(qkv_all, (k * 4 + f) * block, block))
    ]
    g_out = [
        plane_gather(
            wires, pos, lambda: out_w, lambda k, f: out_all.at[:, lane_block(k * 4 + f)]
        )
    ]
    g_unit = [
        unit_scatter(
            wires, pos,
            lambda q: w3.at[:, pl.ds(pl.multiple_of(q * units, 16), units)],
            lambda k, f: w3_all.at[:, pl.ds(0, units), lane_block(k * 4 + f)],
        )
    ]

    def spot(ref):
        return lambda f, k, h: ref.at[
            pl.ds(pl.multiple_of((k * 2 + f) * tokens, 16), tokens), lane_block(h, half)
        ]

    g_gy = [token_gather(wires, pos, None, spot(gy_all), lambda h: gy.at[:, lane_block(h, half)])]
    advance(g_qkv)
    advance(g_gy)
    w3_all[:, units:, :] = jnp.zeros_like(w3_all[:, units:, :])

    def scale_rows(r):
        x = states[r].astype(wide)
        scaled[r] = x * lax.rsqrt(jnp.mean(x * x, axis=-1, keepdims=True) + EPS)

    by_rows(tokens, 16, scale_rows)
    advance(g_qkv)
    advance(g_out)
    advance(g_gy)
    advance(g_qkv)
    advance(g_out)
    advance(g_gy)
    advance(g_qkv)
    advance(g_out)
    advance(g_gy)
    while g_qkv:
        advance(g_qkv)
    fetch_gain.wait()
    for i in range(1, 16):
        q = lax.rem(me + 16 - i, 16)
        wires.arrive(gain_id[i], lambda: gain_all.at[:, lane_block(q)])
    gain_one = gain_all[...].astype(wide)[0:1]
    gain_two = gain_all[...].astype(wide)[1:2]

    save_qkv = wires.fetch(wires.index(), qkv_all, qkv_kept)

    def norm_one(r):
        normed_one[r] = (scaled[r] * gain_one).astype(low)

    by_rows(tokens, 16, norm_one)

    def turned(x):
        return x * cosine[...] + swap_halves(x) * sine[...]

    tail = dot_nn(normed_one[...], qkv_all[:, n_query:])
    kv_own[:, :n_key] = turned(tail[:, :n_key]).astype(low)
    kv_own[:, n_key:] = tail[:, n_key:].astype(low)
    kv_all[pl.ds(pl.multiple_of(c * tokens, 16), tokens)] = kv_own[...]
    kv_id = [wires.index() for _ in range(3)]
    for i in range(3):
        k = lax.rem(c + i + 1, 4)
        wires.push(kv_id[i], lambda: kv_own, lambda: rows(kv_all, c * tokens, tokens), (t, k, d))
    advance(g_unit)

    def project(j, carry):
        where = pl.ds(pl.multiple_of(j * 256, 256), 256)
        two = dot_nn(normed_one[...], qkv_all[:, where])
        for h in range(2):
            slab = pl.ds(pl.multiple_of(j * 256 + h * 128, 128), 128)
            q_rot[:, slab] = turned(two[:, h * 128 : (h + 1) * 128]).astype(low)
        return carry

    lax.fori_loop(0, n_query // 256, project, 0)
    advance(g_out)
    for i in range(3):
        k = lax.rem(c + 3 - i, 4)
        wires.arrive(kv_id[i], lambda: rows(kv_all, k * tokens, tokens))
    q_pos = c * tokens + lax.broadcasted_iota(jnp.int32, (tokens, kv_all.shape[0]), 0)
    k_pos = lax.broadcasted_iota(jnp.int32, (tokens, kv_all.shape[0]), 1)
    allowed = (k_pos <= q_pos) & (k_pos < lengths[0])
    pairs = n_query // 256
    for g in range(2):
        keys = kv_all[:, g * HEAD_SIZE : (g + 1) * HEAD_SIZE]
        values = kv_all[:, n_key + g * HEAD_SIZE : n_key + (g + 1) * HEAD_SIZE]

        def pair(j, carry, g=g, keys=keys, values=values):
            slab = pl.ds(pl.multiple_of((g * pairs + j) * 128, 128), 128)
            q_two = q_rot[:, slab]
            both_heads = []
            for h in range(2):
                probs = head_probs(q_two[:, h * HEAD_SIZE : (h + 1) * HEAD_SIZE], keys, allowed)
                both_heads.append(dot_nn(probs.astype(low), values))
            mixed[:, slab] = jnp.concatenate(both_heads, axis=1).astype(low)
            return carry

        lax.fori_loop(0, pairs, pair, 0)
        if g == 0:
            advance(g_out)
    while g_out:
        advance(g_out)
    advance(g_unit)
    pair_id = [wires.index() for _ in range(4)]
    for i in range(4):
        for j in range(2):
            where = pl.ds(i * (width // 4) + j * (width // 8), width // 8)
            pair_out[:, where] = dot_nn(mixed[...], out_all[:, where]).astype(low)
        piece = pl.ds(i * (width // 4), width // 4)
        wires.push(pair_id[i], lambda p=piece: pair_out.at[:, p], lambda p=piece: pair_in.at[:, p], over)
    advance(g_unit, 2)
    for i in range(4):
        piece = pl.ds(i * (width // 4), width // 4)
        wires.arrive(pair_id[i], lambda: pair_in.at[:, piece])

    def norm_two(r):
        total = states[r].astype(wide) + (pair_out[r].astype(wide) + pair_in[r].astype(wide))
        hidden[r] = total
        factor = lax.rsqrt(jnp.mean(total * total, axis=-1, keepdims=True) + EPS)
        nt[r] = (total * factor * gain_two).astype(low)

    by_rows(tokens, 16, norm_two)

    gathers = []
    for source, target in ((nt, nt_all),):
        at = spot(target)
        z_id, x_id, e_id, f_id = [[wires.index() for _ in range(4)][0] for _ in range(4)]
        gathers.append((at, z_id, x_id, e_id, f_id))
        own_half = lambda h, source=source: source.at[:, lane_block(h, half)]
        for i in (3, 1, 2):
            k = lax.rem(c + i, 4)
            wires.push(
                wires.index(), lambda own=own_half: own(t), lambda at=at: at(e, c, t), (t, k, d),
                lands=z_id + c,
            )
        wires.push(e_id + c, lambda own=own_half: own(t), lambda at=at: at(e, c, t), beside)
        wires.push(f_id + c, lambda own=own_half: own(1 - t), lambda at=at: at(e, c, 1 - t), beside)
    at_home = pl.ds(pl.multiple_of((c * 2 + e) * tokens, 16), tokens)
    nt_all[at_home] = nt[...]
    advance(g_unit, 4)
    while g_gy:
        advance(g_gy)

    def nearest(j):
        return pick(c, [sum_of(j, NEAREST[i]) for i in range(4)])

    def sum_of(j, order):
        value = order[0]
        for i in range(1, 4):
            value = jnp.where(j == i, order[i], value)
        return value

    def stage_one(j):
        k = nearest(j)
        for at, z_id, x_id, e_id, f_id in gathers:
            wires.arrive(z_id + k, lambda: at(e, k, t))
            wires.copy(x_id + k, at(e, k, t), at(e, k, t), over).start()
            wires.copy(e_id + k, at(e, k, t), at(e, k, t), beside).start()

    def stage_two(j):
        k = nearest(j)
        for at, z_id, x_id, e_id, f_id in gathers:

            def act():
                wires.arrive(x_id + k, lambda: at(e, k, 1 - t))
                wires.copy(f_id + k, at(e, k, 1 - t), at(e, k, 1 - t), beside).start()

            pl.when(j > 0)(act)
        for at, z_id, x_id, e_id, f_id in gathers:
            wires.arrive(e_id + k, lambda: at(1 - e, k, t))
            wires.arrive(f_id + k, lambda: at(1 - e, k, 1 - t))

    n_id = [wires.index() for _ in range(4)][0]
    r_id = [wires.index() for _ in range(4)][0]

    def part_rows(k, f):
        return part_g.at[pl.ds(pl.multiple_of((k * 2 + f) * tokens, 16), tokens)]

    mine, other = lane_block(t, half), lane_block(1 - t, half)

    def stage_three(j):
        k = nearest(j)
        wires.arrive(n_id + k, lambda: near.at[k])
        ours = part_rows(k, e)

        def away(r):
            total = ours[r, other].astype(wide) + near[k, r, other].astype(wide)
            near[k, r, other] = total.astype(low)

        by_rows(tokens, 16, away)
        wires.copy(r_id + k, near.at[k, :, other], x_in.at[k], over).start()

    def kept(k, r):
        return (
            part_rows(k, e)[r, mine].astype(wide)
            + near[k, r, mine].astype(wide)
            + x_in[k, r].astype(wide)
        )

    s_id = [wires.index() for _ in range(4)][0]

    def stage_four(j):
        k = nearest(j)
        wires.arrive(r_id + k, lambda: x_in.at[k])

        def add(r):
            near[k, r, mine] = kept(k, r).astype(low)

        by_rows(tokens, 16, add)
        i = lax.rem(k - c + 4, 4)
        wires.copy(s_id + i, near.at[k, :, mine], came.at[i - 1], (t, k, d)).start()

    padded = act_t.shape[0]
    act = qkv_all.at[pl.ds(0, tokens * 8), pl.ds(0, padded)]
    both = qkv_all.at[pl.ds(0, tokens * 8), pl.ds(padded, 2 * padded)]
    both_t = qkv_all.at[pl.ds(tokens * 8, 2 * padded), pl.ds(0, tokens * 8)]
    b_id = wires.index()

    def stored(k):
        where = pl.ds(pl.multiple_of(k * 2 * tokens, 16), 2 * tokens)
        return pltpu.make_async_copy(stage_b, part_b.at[where], wires.recv.at[b_id])

    def swiglu(j, carry):
        stage_two(j)
        k = nearest(j)
        where = pl.ds(pl.multiple_of(k * 2 * tokens, 16), 2 * tokens)
        x = nt_all[where]
        gate = times_transposed(x, w3_all[0])
        up = times_transposed(x, w3_all[1])
        grad_act = times_transposed(gy_all[where], w3_all[2])
        sigma = jax.nn.sigmoid(gate)
        swish = gate * sigma
        act[where] = (swish * up).astype(low)
        wide_units = gate.shape[1]
        both[where, :wide_units] = (
            grad_act * up * (sigma * (1.0 + gate * (1.0 - sigma)))
        ).astype(low)
        both[where, wide_units:] = (grad_act * swish).astype(low)
        for i in range(4):
            piece = slice(i * (width // 4), (i + 1) * (width // 4))
            part_g[where, piece] = (
                dot_nn(both[where, :wide_units], w3_all[0, :, piece])
                + dot_nn(both[where, wide_units:], w3_all[1, :, piece])
            ).astype(low)
        wires.copy(n_id + k, part_rows(k, 1 - e), near.at[k], beside).start()
        pl.when(j > 0)(lambda: stored(0).wait())
        for i in range(4):
            piece = slice(i * (width // 4), (i + 1) * (width // 4))
            stage_b[:, piece] = dot_nn(act[where], w3_all[2, :, piece]).astype(low)
        stored(k).start()
        pl.when(j > 0)(lambda: stage_three(j - 1))
        pl.when(j > 2)(lambda: stage_four(j - 2))
        return carry

    for j in range(1, 4):
        stage_one(j)
    while g_unit:
        advance(g_unit)
    save_qkv.wait()
    wires.drain()
    lax.fori_loop(0, 4, swiglu, 0)
    stored(0).wait()
    stage_three(3)
    for k in range(4):
        away = c != k
        for at, z_id, x_id, e_id, f_id in gathers:
            half_at = lambda h, k=k, at=at: at(e, k, h)
            wires.owe(x_id + k, lambda f=half_at: f(t), away)
            wires.owe(e_id + k, lambda f=half_at: f(t), away)
            wires.owe(f_id + k, lambda f=half_at: f(1 - t), away)
        wires.owe(n_id + k, lambda k=k: part_rows(k, 1 - e))
        wires.owe(r_id + k, lambda k=k: near.at[k, :, other])
    for i in (1, 2, 3):
        k = lax.rem(c + i, 4)
        wires.owe(s_id + i, lambda k=k: near.at[k, :, mine])
    stage_four(2)
    act_t[...] = act[...].T
    both_t[...] = both[...].T

    def unit_grads(k, yy):
        where = lane_block(k * 2 + yy, 256)
        two = dot_nn(both_t[...], nt_all[:, where]).astype(low)
        w3_all[0, :units, where] = two[:units]
        w3_all[1, :units, where] = two[padded : padded + units]
        w3_all[2, :units, where] = dot_nn(act_t[...], gy_all[:, where]).astype(low)[:units]

    u_id = [wires.index() for _ in range(4)][0]
    across = (t, c, (1 - y) * 2 + e)

    def half_grads(k):
        return w3_all.at[:, pl.ds(0, units), lane_block(k * 2 + 1 - y, 256)]

    def send_units(k, carry):
        unit_grads(k, 1 - y)
        wires.copy(u_id + k, half_grads(k), unit_in.at[k], across).start()
        return carry

    lax.fori_loop(0, 2, send_units, 0)
    stage_four(3)
    lax.fori_loop(2, 4, send_units, 0)

    def keep_units(k, carry):
        unit_grads(k, y)
        return carry

    lax.fori_loop(0, 2, keep_units, 0)
    wires.arrive(r_id + c, lambda: x_in.at[c])
    for i in (3, 1, 2):
        wires.arrive(s_id + i, lambda: came.at[i - 1])

    def done(r):
        total = kept(c, r)
        for i in range(3):
            total = total + came[i, r].astype(wide)
        gn_own[r, mine] = total.astype(low)

    by_rows(tokens, 16, done)
    last = wires.index()
    wires.push(last, lambda: gn_own.at[:, mine], lambda: gn_own.at[:, mine], over)
    lax.fori_loop(2, 4, keep_units, 0)
    wires.arrive(last, lambda: gn_own.at[:, other])
    wires.drain()
    for k in range(4):
        wires.owe(u_id + k, lambda k=k: half_grads(k))
    for i, cond, device in (
        (0, True, beside), (1, True, over), (2, c > 0, (t, c - 1, d)), (3, c < 3, (t, c + 1, d))
    ):
        only(
            cond,
            functools.partial(
                pl.semaphore_signal, credit.at[i], inc=1, device_id=device, device_id_type=MESH
            ),
        )
    load_qkv = wires.fetch(wires.index(), qkv_kept, qkv_all)
    s_q, s_k, s_o = scratch[:4], scratch[4:8], scratch[8:12]
    t_b = (
        near, lambda k: part_g.at[pl.ds(k * tokens, tokens)], x_in, came.at[pl.ds(0, 4)], came.at[4]
    )
    g_unit = [unit_gather(wires, pos, w3_all, unit_in, u_id, g3_out)]
    second = [token_scatter(wires, pos, part_b, branch, t_b, credit)]
    mixed_t[...] = mixed[...].T
    normed_t[...] = normed_one[...].T
    gains_sum[...] = jnp.zeros_like(gains_sum)

    def norm_two_back(r):
        value, grad = norm_rows(gn_own[r].astype(wide), hidden[r], gain_two)
        home = pl.ds(pl.multiple_of((c * 2 + e) * tokens + r.start, 16), 16)
        total = gy_all[home].astype(wide) + value
        grad_hidden[r] = total
        grad_low[r] = total.astype(low)
        gains_sum[1:2] += grad

    by_rows(tokens, 16, norm_two_back)
    advance(g_unit)

    def out_grad(j, carry):
        where = pl.ds(pl.multiple_of(j * 2 * lanes, 256), 2 * lanes)
        nt_all[:, where] = dot_nn(mixed_t[...], grad_low[:, where]).astype(low)
        return carry

    lax.fori_loop(0, 8, out_grad, 0)
    outs = [
        plane_scatter(
            wires, pos,
            lambda k, yy: nt_all.at[:, lane_block(k * 4 + yy * 2 + 1 - e)],
            lambda k, yy: nt_all.at[:, lane_block(k * 4 + yy * 2 + e)],
            n_query, s_o, lambda r, v: go_out.__setitem__(r, v),
        )
    ]
    advance(outs)

    def mix_grad(j, carry):
        where = pl.ds(pl.multiple_of(j * 256, 256), 256)
        grad_mixed[:, where] = times_transposed(grad_low[...], out_all[where, :]).astype(low)
        return carry

    lax.fori_loop(0, n_query // 256, mix_grad, 0)
    advance(outs, 4)
    advance(second)
    advance(g_unit)

    scale = HEAD_SIZE ** (-0.5)
    pairs = n_query // 256
    for g in range(2):
        keys = kv_all[:, g * HEAD_SIZE : (g + 1) * HEAD_SIZE]
        values = kv_all[:, n_key + g * HEAD_SIZE : n_key + (g + 1) * HEAD_SIZE]
        dk[...] = jnp.zeros_like(dk)
        dv[...] = jnp.zeros_like(dv)

        def pair(j, carry, g=g, keys=keys, values=values):
            slab = pl.ds(pl.multiple_of((g * pairs + j) * 128, 128), 128)
            q_two, m_two = q_rot[:, slab], grad_mixed[:, slab]
            both = []
            for h in range(2):
                query = q_two[:, h * HEAD_SIZE : (h + 1) * HEAD_SIZE]
                upstream = m_two[:, h * HEAD_SIZE : (h + 1) * HEAD_SIZE]
                probs = head_probs(query, keys, allowed)
                dprob = times_transposed(upstream, values)
                delta = jnp.sum(probs * dprob, axis=-1, keepdims=True)
                grad_scores = (probs * (dprob - delta)).astype(low)
                both.append(dot_nn(grad_scores, keys))
                dk[...] += transposed_times(grad_scores, query)
                dv[...] += transposed_times(probs.astype(low), upstream)
            grads = jnp.concatenate(both, axis=1) * scale
            back = grads * cosine[...] - swap_halves(grads) * sine[...]
            gqkv[:, slab] = back.astype(low)
            return carry

        lax.fori_loop(0, pairs, pair, 0)
        for k in range(4):
            block = slice(k * tokens, (k + 1) * tokens)
            kv_part[k, :, g * HEAD_SIZE : (g + 1) * HEAD_SIZE] = (dk[block] * scale).astype(low)
            kv_part[k, :, n_key + g * HEAD_SIZE : n_key + (g + 1) * HEAD_SIZE] = dv[block].astype(low)
        advance(g_unit)
        advance(second)

    kvg_id = [wires.index() for _ in range(3)]
    for i in range(3):
        k = lax.rem(c + i + 1, 4)
        wires.push(kvg_id[i], lambda k=k: kv_part.at[k], lambda i=i: kv_in.at[i], (t, k, d))

    def q_grad(core, where):
        for h, place in ((0, gy_all), (1, gq_part)):

            def step(j, carry, h=h, place=place):
                owner = j * 2 + core
                here = lane_block(h * 8 + owner)
                place[pl.ds(pl.multiple_of(owner * lanes, 16), lanes), where] = dot_nn(
                    normed_t[here, :], gqkv[:, where]
                ).astype(low)
                return carry

            lax.fori_loop(0, 4, step, 0)

    def q_block(k, f, where):
        place = gy_all if k < 2 else gq_part
        return place.at[pl.ds(pl.multiple_of(((k % 2) * 4 + f) * lanes, 16), lanes), where]

    def q_sums(where, scratches):
        def done(r, value):
            gq_out[r, where] = value

        return plane_scatter(
            wires, pos,
            lambda k, yy: q_block(k, yy * 2 + 1 - e, where),
            lambda k, yy: q_block(k, yy * 2 + e, where),
            gq_out.shape[0], scratches, done,
        )

    first, rest = slice(0, n_query), slice(n_query, n_query + 2 * n_key)
    q_grad(1 - e, first)
    queries = [q_sums(first, s_q)]
    advance(queries)
    q_grad(e, first)
    advance(queries, 4)
    advance(g_unit)
    total = kv_part[c].astype(wide)
    for i in range(3):
        wires.arrive(kvg_id[i], lambda: kv_in.at[i])
        total = total + kv_in[i].astype(wide)
    key_grads = total[:, :n_key]
    key_grads = key_grads * cosine[...] - swap_halves(key_grads) * sine[...]
    gqkv[:, n_query : n_query + n_key] = key_grads.astype(low)
    gqkv[:, n_query + n_key :] = total[:, n_key:].astype(low)
    q_grad(1 - e, rest)
    others = [q_sums(rest, s_k)]
    advance(others)
    q_grad(e, rest)
    load_qkv.wait()

    def normed_grad(j, carry):
        where = pl.ds(pl.multiple_of(j * 256, 256), 256)
        pair_out[:, where] = times_transposed(gqkv[...], qkv_all[where, :]).astype(low)
        return carry

    lax.fori_loop(0, width // 256, normed_grad, 0)
    p_id = wires.index()
    wires.push(p_id, lambda: pair_out, lambda: pair_in, (1 - t, c, d))
    advance(others, 4)
    advance(g_unit)
    wires.arrive(p_id, lambda: pair_in)

    def norm_one_back(r):
        upstream = pair_out[r].astype(wide) + pair_in[r].astype(wide)
        value, grad = norm_rows(upstream, states[r].astype(wide), gain_one)
        grad_states[r] = grad_hidden[r] + value
        gains_sum[0:1] += grad

    by_rows(tokens, 16, norm_one_back)
    g_id = [wires.index() for _ in range(16)]

    def gain_block(q):
        return gains_sum.at[:, pl.ds(pl.multiple_of(q * lanes, 128), lanes)]

    for i in range(1, 16):
        q = lax.rem(me + i, 16)
        wires.push(
            g_id[i], lambda q=q: gain_block(q), lambda i=i: gain_in.at[i],
            (t, q // 4, lax.rem(q, 4)),
        )
    while second or outs or queries or others:
        advance(outs)
        advance(queries)
        advance(others)
        advance(second)
    while g_unit:
        advance(g_unit)

    def finish(r):
        layer_out[r] = (hidden[r] + branch[r].astype(wide)).astype(low)

    by_rows(tokens, 16, finish)
    gain = gains_sum[:, pl.ds(pl.multiple_of(me * lanes, 128), lanes)]
    for i in range(1, 16):
        wires.arrive(g_id[i], lambda: gain_in.at[i])
        gain = gain + gain_in[i]
    gain_out[...] = gain
    wires.drain()


def layer_call(lengths, states, gains, qkv, out_w, w3, gy, cosine, sine):
    shape = jax.ShapeDtypeStruct
    low, wide = jnp.bfloat16, jnp.float32
    tokens, width = states.shape
    n_query, lanes = out_w.shape
    n_all = qkv.shape[1]
    n_rest = n_all - n_query
    units = w3.shape[1] // 8
    padded = -(-units // 128) * 128
    all_tokens, keys = tokens * 8, tokens * 4
    half = width // 2
    vm = pltpu.VMEM
    return pl.pallas_call(
        layer_kernel,
        name="layer",
        out_shape=(
            shape((tokens, width), low),
            shape((tokens, width), wide),
            shape((3, units * 8, lanes), low),
            shape((lanes, n_all), wide),
            shape((n_query, lanes), wide),
            shape((8, lanes), wide),
            shape((width, n_all), low),
            shape((all_tokens, width), low),
        ),
        in_specs=[pl.BlockSpec(memory_space=pltpu.MemorySpace.SMEM), pl.BlockSpec(memory_space=VMEM)]
        + [pl.BlockSpec(memory_space=HBM)] * 5
        + [pl.BlockSpec(memory_space=VMEM)] * 2,
        out_specs=[
            pl.BlockSpec(memory_space=VMEM),
            pl.BlockSpec(memory_space=VMEM),
            pl.BlockSpec(memory_space=HBM),
            pl.BlockSpec(memory_space=VMEM),
            pl.BlockSpec(memory_space=VMEM),
            pl.BlockSpec(memory_space=VMEM),
            pl.BlockSpec(memory_space=HBM),
            pl.BlockSpec(memory_space=HBM),
        ],
        scratch_shapes=[
            pltpu.SemaphoreType.DMA((320,)),
            pltpu.SemaphoreType.DMA((320,)),
            pltpu.SemaphoreType.REGULAR((4,)),
            vm((width, n_all), low),
            vm((n_query, width), low),
            vm((16, width), low),
            vm((tokens, width), wide),
            vm((tokens, width), low),
            vm((tokens, n_query), low),
            vm((keys, n_rest), low),
            vm((tokens, n_query), low),
            vm((tokens, width), low),
            vm((3, padded, width), low),
            vm((all_tokens, width), low),
            vm((all_tokens, width), low),
            vm((padded, all_tokens), low),
            vm((all_tokens, width), low),
            vm((2 * tokens, width), low),
            vm((4, 3, units, width // 8), low),
            vm((tokens, n_rest), low),
            vm((tokens, width), low),
            vm((tokens, width), low),
            vm((tokens, width), low),
            vm((4, tokens, width), low),
            vm((4, tokens, half), low),
            vm((5, tokens, half), low),
            vm((tokens, width), wide),
            vm((tokens, width), low),
            vm((tokens, width), low),
            vm((n_query, tokens), low),
            vm((tokens, n_query), low),
            vm((tokens, n_all), low),
            vm((width, tokens), low),
            vm((8 * lanes, n_all), low),
            vm((keys, HEAD_SIZE), wide),
            vm((keys, HEAD_SIZE), wide),
            vm((4, tokens, n_rest), low),
            vm((3, tokens, n_rest), low),
            vm((8, width), wide),
            vm((16, 8, lanes), wide),
        ]
        + plane_scratch((lanes, n_query))
        + plane_scratch((lanes, n_rest))
        + plane_scratch((n_query, lanes)),
        compiler_params=pltpu.CompilerParams(
            collective_id=1, has_side_effects=True, vmem_limit_bytes=63 << 20
        ),
    )(lengths, states, gains, qkv, out_w, w3, gy, cosine, sine)


def plane_shards(
    states, lengths, first_gain, w_query, key_matrix, value_matrix, w_out, second_gain,
    w_gate, w_up, w_down, cotangent,
):
    low, wide = jnp.bfloat16, jnp.float32
    tokens = states.shape[1]
    positions = lax.axis_index("ctx") * tokens + jnp.arange(tokens, dtype=jnp.int32)
    cosine, sine = rope_tables(positions, HEAD_SIZE // 2)
    lane = jnp.arange(2 * HEAD_SIZE)
    turn = jnp.where((lane % HEAD_SIZE) < HEAD_SIZE // 2, -1.0, 1.0)
    cosine = jnp.tile(cosine[:, 0], (1, 4))
    sine = jnp.tile(sine[:, 0], (1, 4)) * turn[None, :]
    valid = (positions < lengths[0])[:, None]
    grad_y = jnp.where(valid, cotangent[0], jnp.zeros((), low))
    n_query, n_key = w_query.shape[1], key_matrix.shape[1]
    lanes = w_out.shape[1]
    qkv = jnp.concatenate([w_query, key_matrix, value_matrix], axis=1)
    gains = jnp.concatenate(
        [first_gain[None], second_gain[None], jnp.zeros((14, lanes), low)], axis=0
    )
    w3 = jnp.stack([w_gate.T, w_up.T, w_down])
    layer_out, grad_states, g3, gq, go, gain, _, _ = layer_call(
        lengths, states[0], gains, qkv, w_out, w3, grad_y, cosine, sine
    )
    return (
        layer_out[None],
        grad_states[None],
        gain[0],
        gq[:, :n_query],
        gq[:, n_query : n_query + n_key],
        gq[:, n_query + n_key :],
        go,
        gain[1],
        g3[0].T.astype(wide),
        g3[1].T.astype(wide),
        g3[2].astype(wide),
    )


def fits(mesh):
    return dict(mesh.shape) == {"tensor": 2, "ctx": 4, "dp": 4}


def solution(mesh):
    placed = (
        P("dp", "ctx", None),
        P("dp"),
        P(("ctx", "dp")),
        P(("ctx", "dp"), "tensor"),
        P(("ctx", "dp"), "tensor"),
        P(("ctx", "dp"), "tensor"),
        P("tensor", ("ctx", "dp")),
        P(("ctx", "dp")),
        P(("ctx", "dp"), "tensor"),
        P(("ctx", "dp"), "tensor"),
        P("tensor", ("ctx", "dp")),
        P("dp", "ctx", None),
    )
    return jax.shard_map(
        plane_shards if fits(mesh) else shards,
        mesh=mesh,
        in_specs=placed,
        out_specs=(
            P("dp", "ctx", None),
            P("dp", "ctx", None),
            P(("ctx", "dp")),
            P(("ctx", "dp"), "tensor"),
            P(("ctx", "dp"), "tensor"),
            P(("ctx", "dp"), "tensor"),
            P("tensor", ("ctx", "dp")),
            P(("ctx", "dp")),
            P(("ctx", "dp"), "tensor"),
            P(("ctx", "dp"), "tensor"),
            P("tensor", ("ctx", "dp")),
        ),
        check_vma=False,
    )
```

```python
import functools

import jax
import jax.numpy as jnp
from jax import lax
from jax.experimental import pallas as pl
from jax.experimental.pallas import tpu as pltpu
from jax.sharding import PartitionSpec as P

HEAD_SIZE = 64


EPS = 1e-05
THETA = 10000.0
NEGATIVE = -1e30


def rope_tables(positions, half_width):
    inverse = jnp.exp(-jnp.log(THETA) * jnp.arange(half_width).astype(jnp.float32) / half_width)
    angles = positions.astype(jnp.float32)[:, None] * inverse[None, :]
    return (jnp.cos(angles)[:, None, :], jnp.sin(angles)[:, None, :])


def apply_rotation(vectors, cosine_table, sine_table):
    half_width = vectors.shape[-1] // 2
    first_half = vectors[..., :half_width]
    second_half = vectors[..., half_width:]
    return jnp.concatenate(
        [
            first_half * cosine_table - second_half * sine_table,
            second_half * cosine_table + first_half * sine_table,
        ],
        axis=-1,
    )


def rotate_back(grads, cosine_table, sine_table):
    half_width = grads.shape[-1] // 2
    first_half = grads[..., :half_width]
    second_half = grads[..., half_width:]
    return jnp.concatenate(
        [
            first_half * cosine_table + second_half * sine_table,
            second_half * cosine_table - first_half * sine_table,
        ],
        axis=-1,
    )


def times_transposed(left, right):
    return lax.dot_general(
        left, right, (((1,), (1,)), ((), ())), preferred_element_type=jnp.float32
    )


def transposed_times(left, right):
    return lax.dot_general(
        left, right, (((0,), (0,)), ((), ())), preferred_element_type=jnp.float32
    )


def norm_back(upstream, inputs, inverse_rms, gain):
    scaled = upstream * gain
    gain_grad = jnp.sum(upstream * inputs * inverse_rms, axis=0)
    inner = jnp.mean(scaled * inputs, axis=-1, keepdims=True)
    return (inverse_rms * scaled - inputs * inverse_rms**3 * inner, gain_grad)


def shards(
    states,
    lengths,
    first_gain,
    w_query,
    key_matrix,
    value_matrix,
    w_out,
    second_gain,
    w_gate,
    w_up,
    w_down,
    cotangent,
):
    low_type = jnp.bfloat16
    wide_type = jnp.float32
    gathered = (
        lax.all_gather(first_gain, ("ctx", "dp"), axis=0, tiled=True),
        lax.all_gather(w_query, ("ctx", "dp"), axis=0, tiled=True),
        lax.all_gather(key_matrix, ("ctx", "dp"), axis=0, tiled=True),
        lax.all_gather(value_matrix, ("ctx", "dp"), axis=0, tiled=True),
        lax.all_gather(w_out, ("ctx", "dp"), axis=1, tiled=True),
        lax.all_gather(second_gain, ("ctx", "dp"), axis=0, tiled=True),
        lax.all_gather(w_gate, ("ctx", "dp"), axis=0, tiled=True),
        lax.all_gather(w_up, ("ctx", "dp"), axis=0, tiled=True),
        lax.all_gather(w_down, ("ctx", "dp"), axis=1, tiled=True),
    )
    (
        gain_one,
        full_query,
        full_key,
        full_value,
        full_out,
        gain_two,
        full_gate,
        full_up,
        full_down,
    ) = gathered
    gain_one = gain_one.astype(wide_type)
    gain_two = gain_two.astype(wide_type)
    tokens = states.shape[1]
    inputs = states[0].astype(wide_type)
    seq_length = lengths[0]
    first_pos = lax.axis_index("ctx") * tokens
    positions = first_pos + jnp.arange(tokens, dtype=jnp.int32)
    cosine_table, sine_table = rope_tables(positions, HEAD_SIZE // 2)
    heads = full_query.shape[1] // HEAD_SIZE
    kv_heads = full_key.shape[1] // HEAD_SIZE
    group_factor = heads // kv_heads
    scale = HEAD_SIZE ** (-0.5)
    rms_one = lax.rsqrt(jnp.mean(inputs * inputs, axis=-1, keepdims=True) + EPS)
    first_normed = (inputs * rms_one * gain_one).astype(low_type)
    query_rows = jnp.dot(first_normed, full_query, preferred_element_type=wide_type)
    fresh_keys = jnp.dot(first_normed, full_key, preferred_element_type=wide_type)
    values_new = jnp.dot(first_normed, full_value, preferred_element_type=wide_type)
    query_rotated = (
        apply_rotation(query_rows.reshape(tokens, heads, HEAD_SIZE), cosine_table, sine_table)
        .astype(low_type)
        .reshape(tokens, kv_heads, group_factor, HEAD_SIZE)
    )
    key_rot = (
        apply_rotation(fresh_keys.reshape(tokens, kv_heads, HEAD_SIZE), cosine_table, sine_table)
        .astype(low_type)
        .reshape(tokens, kv_heads * HEAD_SIZE)
    )
    value_lower = values_new.astype(low_type)
    keys_all, values_all = (
        lax.all_gather(key_rot, "ctx", axis=0, tiled=True),
        lax.all_gather(value_lower, "ctx", axis=0, tiled=True),
    )
    total_keys = keys_all.shape[0]
    key_block = min(512, total_keys)
    block_count = total_keys // key_block

    def block_scores(begin_at):
        key_piece = lax.dynamic_slice_in_dim(keys_all, begin_at, key_block, 0).reshape(
            key_block, kv_heads, HEAD_SIZE
        )
        value_piece = lax.dynamic_slice_in_dim(values_all, begin_at, key_block, 0).reshape(
            key_block, kv_heads, HEAD_SIZE
        )
        scores = (
            jnp.einsum("qkgd,pkd->kgqp", query_rotated, key_piece, preferred_element_type=wide_type)
            * scale
        )
        key_pos = begin_at + jnp.arange(key_block, dtype=jnp.int32)
        allowed = (key_pos[None, :] <= positions[:, None]) & (key_pos[None, :] < seq_length)
        return (jnp.where(allowed, scores, NEGATIVE), key_piece, value_piece)

    def max_pass(index, carry):
        running, total = carry
        scores = block_scores(index * key_block)[0]
        newest = jnp.maximum(running, jnp.max(scores, axis=-1))
        total = total * jnp.exp(running - newest) + jnp.sum(
            jnp.exp(scores - newest[..., None]), axis=-1
        )
        return (newest, total)

    start_max = jnp.full((kv_heads, group_factor, tokens), NEGATIVE, wide_type)
    running, total = lax.fori_loop(0, block_count, max_pass, (start_max, jnp.zeros_like(start_max)))
    log_total = running + jnp.log(total)

    def mix_pass(index, carry):
        scores, key_piece, value_piece = block_scores(index * key_block)
        weights = jnp.exp(scores - log_total[..., None]).astype(low_type)
        return carry + jnp.einsum(
            "kgqp,pkd->qkgd", weights, value_piece, preferred_element_type=wide_type
        )

    mixed = lax.fori_loop(
        0, block_count, mix_pass, jnp.zeros((tokens, kv_heads, group_factor, HEAD_SIZE), wide_type)
    )
    mixed_low = mixed.reshape(tokens, heads * HEAD_SIZE).astype(low_type)
    attention = lax.psum(jnp.dot(mixed_low, full_out, preferred_element_type=wide_type), "tensor")
    hidden = inputs + attention
    rms_two = lax.rsqrt(jnp.mean(hidden * hidden, axis=-1, keepdims=True) + EPS)
    normed_two = (hidden * rms_two * gain_two).astype(low_type)
    gate = jnp.dot(normed_two, full_gate, preferred_element_type=wide_type)
    up_proj = jnp.dot(normed_two, full_up, preferred_element_type=wide_type)
    sigma = jax.nn.sigmoid(gate)
    swish = gate * sigma
    activated = (swish * up_proj).astype(low_type)
    branch = lax.psum(
        jnp.dot(activated, full_down, preferred_element_type=wide_type).astype(jnp.bfloat16),
        "tensor",
    ).astype(jnp.float32)
    layer_out = (hidden + branch).astype(low_type)
    valid = (positions < seq_length)[:, None]
    grad_y = jnp.where(valid, cotangent[0].astype(wide_type), 0.0)
    grad_y_low = grad_y.astype(low_type)
    grad_down = transposed_times(activated, grad_y_low)
    grad_act = times_transposed(grad_y_low, full_down)
    grad_gate_low = (grad_act * up_proj * (sigma * (1.0 + gate * (1.0 - sigma)))).astype(low_type)
    grad_up_low = (grad_act * swish).astype(low_type)
    grad_gate = transposed_times(normed_two, grad_gate_low)
    grad_up = transposed_times(normed_two, grad_up_low)
    grad_normed_two = lax.psum(
        times_transposed(grad_gate_low, full_gate) + times_transposed(grad_up_low, full_up),
        "tensor",
    )
    norm_part, grad_gain_two = norm_back(grad_normed_two, hidden, rms_two, gain_two)
    grad_hidden = grad_y + norm_part
    grad_hidden_low = grad_hidden.astype(low_type)
    grad_out = transposed_times(mixed_low, grad_hidden_low)
    grad_mixed = (
        times_transposed(grad_hidden_low, full_out)
        .astype(low_type)
        .reshape(tokens, kv_heads, group_factor, HEAD_SIZE)
    )

    def delta_pass(index, carry):
        scores, key_piece, value_piece = block_scores(index * key_block)
        probs = jnp.exp(scores - log_total[..., None])
        dprob = jnp.einsum(
            "qkgd,pkd->kgqp", grad_mixed, value_piece, preferred_element_type=wide_type
        )
        return carry + jnp.sum(probs * dprob, axis=-1)

    delta = lax.fori_loop(
        0, block_count, delta_pass, jnp.zeros((kv_heads, group_factor, tokens), wide_type)
    )

    def grad_pass(index, carry):
        grad_queries, key_grads, value_grads = carry
        begin_at = index * key_block
        scores, key_piece, value_piece = block_scores(begin_at)
        probs = jnp.exp(scores - log_total[..., None])
        dprob = jnp.einsum(
            "qkgd,pkd->kgqp", grad_mixed, value_piece, preferred_element_type=wide_type
        )
        grad_scores = (probs * (dprob - delta[..., None])).astype(low_type)
        grad_queries = (
            grad_queries
            + jnp.einsum("kgqp,pkd->qkgd", grad_scores, key_piece, preferred_element_type=wide_type)
            * scale
        )
        key_part = (
            jnp.einsum(
                "kgqp,qkgd->pkd", grad_scores, query_rotated, preferred_element_type=wide_type
            )
            * scale
        )
        value_part = jnp.einsum(
            "kgqp,qkgd->pkd", probs.astype(low_type), grad_mixed, preferred_element_type=wide_type
        )
        key_grads = lax.dynamic_update_slice_in_dim(
            key_grads, key_part.reshape(key_block, kv_heads * HEAD_SIZE), begin_at, 0
        )
        value_grads = lax.dynamic_update_slice_in_dim(
            value_grads, value_part.reshape(key_block, kv_heads * HEAD_SIZE), begin_at, 0
        )
        return (grad_queries, key_grads, value_grads)

    empty_keys = jnp.zeros((total_keys, kv_heads * HEAD_SIZE), wide_type)
    start_state = (
        jnp.zeros((tokens, kv_heads, group_factor, HEAD_SIZE), wide_type),
        empty_keys,
        empty_keys,
    )
    grad_queries, key_grads, value_grads = lax.fori_loop(0, block_count, grad_pass, start_state)
    key_local, value_local = (
        lax.psum_scatter(key_grads, "ctx", scatter_dimension=0, tiled=True),
        lax.psum_scatter(value_grads, "ctx", scatter_dimension=0, tiled=True),
    )
    grad_query_low = (
        rotate_back(grad_queries.reshape(tokens, heads, HEAD_SIZE), cosine_table, sine_table)
        .reshape(tokens, heads * HEAD_SIZE)
        .astype(low_type)
    )
    grad_key_low = (
        rotate_back(key_local.reshape(tokens, kv_heads, HEAD_SIZE), cosine_table, sine_table)
        .reshape(tokens, kv_heads * HEAD_SIZE)
        .astype(low_type)
    )
    grad_value_low = value_local.astype(low_type)
    grad_query = transposed_times(first_normed, grad_query_low)
    grad_key = transposed_times(first_normed, grad_key_low)
    grad_value = transposed_times(first_normed, grad_value_low)
    grad_normed_one = lax.psum(
        (
            times_transposed(grad_query_low, full_query)
            + times_transposed(grad_key_low, full_key)
            + times_transposed(grad_value_low, full_value)
        ).astype(jnp.bfloat16),
        "tensor",
    ).astype(jnp.float32)
    first_part, grad_gain_one = norm_back(grad_normed_one, inputs, rms_one, gain_one)
    grad_states = grad_hidden + first_part
    summed = tuple(
        (
            lax.psum_scatter(grad_gain_one, ("ctx", "dp"), scatter_dimension=0, tiled=True),
            lax.psum_scatter(grad_query, ("ctx", "dp"), scatter_dimension=0, tiled=True),
            lax.psum_scatter(grad_key, ("ctx", "dp"), scatter_dimension=0, tiled=True),
            lax.psum_scatter(grad_value, ("ctx", "dp"), scatter_dimension=0, tiled=True),
            lax.psum_scatter(grad_out, ("ctx", "dp"), scatter_dimension=1, tiled=True),
            lax.psum_scatter(grad_gain_two, ("ctx", "dp"), scatter_dimension=0, tiled=True),
            lax.psum_scatter(grad_gate, ("ctx", "dp"), scatter_dimension=0, tiled=True),
            lax.psum_scatter(grad_up, ("ctx", "dp"), scatter_dimension=0, tiled=True),
            lax.psum_scatter(grad_down, ("ctx", "dp"), scatter_dimension=1, tiled=True),
        )
    )
    return (
        layer_out[None],
        grad_states[None],
        summed[0],
        summed[1],
        summed[2],
        summed[3],
        summed[4],
        summed[5],
        summed[6],
        summed[7],
        summed[8],
    )


MESH = pl.DeviceIdType.MESH
HBM = pltpu.MemorySpace.HBM
VMEM = pltpu.MemorySpace.VMEM
STEPS = [(1, -1), (1, 1), (2, -1), (2, 1), (3, -1), (3, 1)]


def position():
    t, c, d = lax.axis_index("tensor"), lax.axis_index("ctx"), lax.axis_index("dp")
    return t, c, d // 2, d % 2


def only(cond, act):
    if cond is True:
        act()
    else:
        pl.when(cond)(act)


class Wires:
    def __init__(self, send, recv):
        self.send, self.recv, self.used, self.sent = send, recv, 0, []

    def index(self):
        self.used += 1
        return self.used - 1

    def copy(self, i, src, dst, device, lands=None):
        return pltpu.make_async_remote_copy(
            src_ref=src,
            dst_ref=dst,
            send_sem=self.send.at[i],
            recv_sem=self.recv.at[i if lands is None else lands],
            device_id=device,
            device_id_type=MESH,
        )

    def push(self, i, src, dst, device, cond=True, lands=None):
        only(cond, lambda: self.copy(i, src(), dst(), device, lands).start())
        self.sent.append((cond, lambda: self.copy(i, src(), dst(), device).wait_send()))

    def owe(self, i, src, cond=True):
        self.sent.append((cond, lambda: self.copy(i, src(), src(), position_id()).wait_send()))

    def arrive(self, i, dst, cond=True):
        def act():
            place = dst()
            self.copy(i, place, place, position_id()).wait_recv()

        only(cond, act)

    def local(self, i, src, dst):
        def make():
            return pltpu.make_async_copy(src(), dst(), self.send.at[i])

        make().start()
        self.sent.append((True, lambda: make().wait()))

    def fetch(self, i, src, dst):
        copy = pltpu.make_async_copy(src, dst, self.recv.at[i])
        copy.start()
        return copy

    def drain(self):
        for cond, act in self.sent:
            only(cond, act)
        self.sent = []


def position_id():
    t, c, y, e = position()
    return (t, c, y * 2 + e)


def greet(peers):
    barrier = pltpu.get_barrier_semaphore()
    count = 0
    for cond, device in peers:
        only(
            cond,
            functools.partial(
                pl.semaphore_signal, barrier, inc=1, device_id=device, device_id_type=MESH
            ),
        )
        count = count + (1 if cond is True else cond.astype(jnp.int32))
    pl.semaphore_wait(barrier, count)


def around(pos, chain=True, x=False, y=False, core=True, row=False):
    t, c, yy, e = pos
    d = yy * 2 + e
    peers = []
    if chain:
        peers += [(c < 3, (t, c + 1, d)), (c > 0, (t, c - 1, d))]
    if x:
        peers.append((True, (1 - t, c, d)))
    if y:
        peers.append((True, (t, c, (1 - yy) * 2 + e)))
    if core:
        peers.append((True, (t, c, yy * 2 + 1 - e)))
    return peers


def reach(c, s, sign):
    k = c + sign * s
    return k, ((k >= 0) if sign < 0 else (k <= 3))


def plane_gather(wires, pos, src, at):
    t, c, y, e = pos
    d, d_y, d_e = y * 2 + e, (1 - y) * 2 + e, y * 2 + 1 - e
    z_id = {key: wires.index() for key in STEPS}
    y_id = {key: wires.index() for key in [(0, 0)] + STEPS}
    e_id = {key: wires.index() for key in [(0, 0)] + STEPS}
    f_id = {key: wires.index() for key in [(0, 0)] + STEPS}
    fetch = wires.fetch(wires.index(), src(), at(c, d))

    def spread(key, block, place, cond):
        s, sign = key
        if s < 3:
            for way in ((-1, 1) if s == 0 else (sign,)):
                nxt = c - way
                here = (nxt >= 0) if way > 0 else (nxt <= 3)
                wires.push(
                    z_id[(s + 1, way)], block, place, (t, nxt, d),
                    here if cond is True else (cond & here),
                )
        wires.push(y_id[key], block, place, (t, c, d_y), cond)
        wires.push(e_id[key], block, place, (t, c, d_e), cond)

    def relay(key, cond):
        k = c + key[0] * key[1]
        place = lambda: at(k, d_y)
        wires.arrive(y_id[key], place, cond)
        wires.push(f_id[key], place, place, (t, c, d_e), cond)

    spread((0, 0), src, lambda: at(c, d), True)
    yield
    late = [((0, 0), True)]
    for key in STEPS:
        k, cond = reach(c, *key)
        place = lambda k=k: at(k, d)
        wires.arrive(z_id[key], place, cond)
        spread(key, place, place, cond)
        if key[1] > 0:
            for old in late:
                relay(*old)
            late = []
            yield
        late.append((key, cond))
    for old in late:
        relay(*old)
    yield
    for key in [(0, 0)] + STEPS:
        k, cond = (c, True) if key[0] == 0 else reach(c, *key)
        wires.arrive(e_id[key], lambda: at(k, d_e), cond)
        wires.arrive(f_id[key], lambda: at(k, (1 - y) * 2 + 1 - e), cond)
    fetch.wait()


def token_gather(wires, pos, src, at, half):
    t, c, y, e = pos
    d, d_e = y * 2 + e, y * 2 + 1 - e
    z_id = {key: wires.index() for key in STEPS}
    x_id = {key: wires.index() for key in STEPS}
    e_id = {key: wires.index() for key in STEPS}
    f_id = {key: wires.index() for key in STEPS}
    own = wires.index(), wires.index()
    here = wires.index(), wires.index()
    for way in (-1, 1):
        nxt = c - way
        wires.push(
            z_id[(1, way)], lambda: half(t), lambda: at(e, c, t), (t, nxt, d),
            (nxt >= 0) if way > 0 else (nxt <= 3),
        )
    for i in (0, 1):
        wires.push(own[i], lambda i=i: half(i), lambda i=i: at(e, c, i), (t, c, d_e))
    fetch = [wires.fetch(here[i], half(i), at(e, c, i)) for i in (0, 1)]
    yield

    def relay(key, cond):
        k = c + key[0] * key[1]
        place = lambda: at(e, k, 1 - t)
        wires.arrive(x_id[key], place, cond)
        wires.push(f_id[key], place, place, (t, c, d_e), cond)

    late = []
    for key in STEPS:
        k, cond = reach(c, *key)
        place = lambda k=k: at(e, k, t)
        wires.arrive(z_id[key], place, cond)
        s, sign = key
        if s < 3:
            nxt = c - sign
            ok = (nxt >= 0) if sign > 0 else (nxt <= 3)
            wires.push(z_id[(s + 1, sign)], place, place, (t, nxt, d), cond & ok)
        wires.push(x_id[key], place, place, (1 - t, c, d), cond)
        wires.push(e_id[key], place, place, (t, c, d_e), cond)
        if sign > 0:
            for old in late:
                relay(*old)
            late = []
            yield
        late.append((key, cond))
    for old in late:
        relay(*old)
    yield
    for i in (0, 1):
        wires.arrive(own[i], lambda i=i: at(1 - e, c, i))
    for key in STEPS:
        k, cond = reach(c, *key)
        wires.arrive(e_id[key], lambda: at(1 - e, k, t), cond)
        wires.arrive(f_id[key], lambda: at(1 - e, k, 1 - t), cond)
    for copy in fetch:
        copy.wait()


def unit_scatter(wires, pos, piece, place):
    t, c, y, e = pos
    me = c * 2 + e
    first = [wires.index() for _ in range(8)]
    second = [wires.index() for _ in range(8)]
    fetch = wires.fetch(first[0], piece(me), place(c, y * 2 + e))
    for i in range(1, 8):
        q = lax.rem(me + i, 8)
        wires.push(
            first[i], lambda q=q: piece(q), lambda: place(c, y * 2 + e), (t, q // 2, y * 2 + q % 2)
        )
    wires.push(
        second[0], lambda: piece(me), lambda: place(c, y * 2 + e), (t, c, (1 - y) * 2 + e)
    )
    yield
    for i in range(1, 8):
        q = lax.rem(me + 8 - i, 8)
        block = lambda q=q: place(q // 2, y * 2 + q % 2)
        wires.arrive(first[i], block)
        wires.push(second[i], block, block, (t, c, (1 - y) * 2 + e))
        yield
    yield
    for i in range(8):
        q = lax.rem(me + 8 - i, 8)
        wires.arrive(second[i], lambda q=q: place(q // 2, (1 - y) * 2 + q % 2))
    fetch.wait()


def run_all(parts):
    parts = list(parts)
    while parts:
        for part in list(parts):
            try:
                next(part)
            except StopIteration:
                parts.remove(part)


def rows(ref, start, size):
    return ref.at[pl.ds(pl.multiple_of(start, 16), size)]


def dot_nn(a, b):
    return lax.dot_general(a, b, (((1,), (0,)), ((), ())), preferred_element_type=jnp.float32)


def by_rows(count, width, act):
    step = max(16, 32768 // width)
    while count % step:
        step -= 16

    def body(i, carry):
        act(pl.ds(pl.multiple_of(i * step, step), step))
        return carry

    lax.fori_loop(0, count // step, body, 0)


ORDER = (3, 0, 2, 1)


def chain_sum(wires, pos, height, value, keep, came, extra, done):
    t, c, y, e = pos
    d = y * 2 + e
    wide = jnp.float32
    r_id = [wires.index() for _ in range(4)]
    l_id = [wires.index() for _ in range(4)]

    def stage(s):
        for edge, way, blocks, number in (
            (s, 1, range(3, s, -1), r_id), (3 - s, -1, range(0, 3 - s), l_id)
        ):
            here = c == edge
            for k in blocks:

                def act(k=k, number=number):
                    place = keep(k)
                    if s > 0:
                        wires.arrive(number[k], lambda: came.at[k])

                    def add(r):
                        total = value(k, r)
                        if s > 0:
                            total = total + came[k, r].astype(wide)
                        place[r] = total.astype(place.dtype)

                    by_rows(height, extra.shape[-1], add)

                pl.when(here)(act)
                target = extra if way < 0 and k == edge - 1 else came.at[k]
                wires.push(
                    number[k], lambda k=k: keep(k), lambda target=target: target,
                    (t, c + way, d), here,
                )

    def finish():
        for k in range(4):

            def act(k=k):
                if k > 0:
                    wires.arrive(r_id[k], lambda: came.at[k])
                if k < 3:
                    wires.arrive(l_id[k], lambda: extra)

                def add(r):
                    total = value(k, r)
                    if k > 0:
                        total = total + came[k, r].astype(wide)
                    if k < 3:
                        total = total + extra[r].astype(wide)
                    done(r, total)

                by_rows(height, extra.shape[-1], add)

            pl.when(c == k)(act)

    return stage, finish


def token_scatter(wires, pos, part, out, scratch, credit):
    t, c, y, e = pos
    near, own, x_in, came, extra = scratch
    wide = jnp.float32
    tokens, half = x_in.shape[1], x_in.shape[2]
    d_e = y * 2 + 1 - e
    e_id = [wires.index() for _ in range(4)]
    x_id = [wires.index() for _ in range(4)]
    last = wires.index()
    mine = pl.ds(pl.multiple_of(t * half, 128), half)
    other = pl.ds(pl.multiple_of((1 - t) * half, 128), half)

    def begin(k, f):
        return pl.multiple_of((k * 2 + f) * tokens, 16)

    pl.semaphore_wait(credit.at[0], 1)
    for k in ORDER:
        wires.push(
            e_id[k], lambda k=k: part.at[pl.ds(begin(k, 1 - e), tokens)],
            lambda k=k: near.at[k], (t, c, d_e),
        )
    fetch = [
        wires.fetch(wires.index(), part.at[pl.ds(begin(k, e), tokens)], own(k)) for k in range(4)
    ]
    yield
    pl.semaphore_wait(credit.at[1], 1)
    for k in ORDER:
        fetch[k].wait()
        wires.arrive(e_id[k], lambda: near.at[k])

        def away(r):
            total = own(k)[r, other].astype(wide) + near[k, r, other].astype(wide)
            near[k, r, other] = total.astype(near.dtype)

        by_rows(tokens, half, away)
        wires.push(
            x_id[k], lambda k=k: near.at[k, :, other], lambda k=k: x_in.at[k], (1 - t, c, y * 2 + e)
        )
    yield

    def value(k, r):
        return (
            own(k)[r, mine].astype(wide)
            + near[k, r, mine].astype(wide)
            + x_in[k, r].astype(wide)
        )

    def done(r, total):
        out[r, mine] = total.astype(out.dtype)

    stage, finish = chain_sum(
        wires, pos, tokens, value, lambda k: near.at[k, :, mine], came, extra, done
    )
    pl.when(c < 3)(lambda: pl.semaphore_wait(credit.at[2], 1))
    pl.when(c > 0)(lambda: pl.semaphore_wait(credit.at[3], 1))
    for k in ORDER:
        wires.arrive(x_id[k], lambda: x_in.at[k])
    for s in range(3):
        stage(s)
        yield
    finish()
    wires.push(last, lambda: out.at[:, mine], lambda: out.at[:, mine], (1 - t, c, y * 2 + e))
    yield
    wires.arrive(last, lambda: out.at[:, other])


def plane_scatter(wires, pos, out_block, own_block, height, scratch, done, straight=False):
    t, c, y, e = pos
    near, y_in, came, extra = scratch
    wide = jnp.float32
    d_y, d_e = (1 - y) * 2 + e, y * 2 + 1 - e
    e_id = {(k, f): wires.index() for f in range(2) for k in range(4)}
    y_id = [wires.index() for _ in range(4)]
    for f in range(2):
        yy = (1 - y) if f == 0 else y
        for k in ORDER:
            wires.push(
                e_id[k, f], lambda k=k, yy=yy: out_block(k, yy),
                lambda k=k, f=f: near.at[f * 4 + k], (t, c, d_e),
            )
    yield
    for k in ORDER:
        wires.arrive(e_id[k, 0], lambda: near.at[k])
        block = own_block(k, 1 - y)

        def away(r):
            total = block[r].astype(wide) + near[k, r].astype(wide)
            near[k, r] = total.astype(near.dtype)

        by_rows(height, extra.shape[-1], away)
        wires.push(y_id[k], lambda k=k: near.at[k], lambda k=k: y_in.at[k], (t, c, d_y))
        yield

    def block_value(k, r):
        block = own_block(k, y)
        return (
            block[r].astype(wide)
            + near[4 + k, r].astype(wide)
            + y_in[k, r].astype(wide)
        )

    def value(k, r):
        return (
            own_block(k, y)[r].astype(wide)
            + near[4 + k, r].astype(wide)
            + y_in[k, r].astype(wide)
        )

    if straight:
        s_id = [wires.index() for _ in range(4)]
        for far in (3, 1, 2):
            k = lax.rem(c + far, 4)
            wires.arrive(e_id[0, 1] + k, lambda: near.at[4 + k])
            wires.arrive(y_id[0] + k, lambda: y_in.at[k])

            def settle(r):
                near[4 + k, r] = block_value(k, r).astype(near.dtype)

            by_rows(height, extra.shape[-1], settle)
            wires.push(
                s_id[far], lambda k=k: near.at[4 + k], lambda far=far: came.at[far],
                (t, k, y * 2 + e),
            )
            yield
        wires.arrive(e_id[0, 1] + c, lambda: near.at[4 + c])
        wires.arrive(y_id[0] + c, lambda: y_in.at[c])
        for far in (3, 1, 2):
            wires.arrive(s_id[far], lambda: came.at[far])

        def add(r):
            total = block_value(c, r)
            for far in (1, 2, 3):
                total = total + came[far, r].astype(wide)
            done(r, total)

        by_rows(height, extra.shape[-1], add)
        return

    stage, finish = chain_sum(
        wires, pos, height, value, lambda k: near.at[4 + k], came, extra, done
    )
    for k in ORDER:
        wires.arrive(e_id[k, 1], lambda: near.at[4 + k])
        wires.arrive(y_id[k], lambda: y_in.at[k])
    for s in range(3):
        stage(s)
        yield
    finish()


def plane_scratch(shape):
    low = jnp.bfloat16
    return [
        pltpu.VMEM((8,) + shape, low),
        pltpu.VMEM((4,) + shape, low),
        pltpu.VMEM((4,) + shape, low),
        pltpu.VMEM(shape, low),
    ]


def unit_gather(wires, pos, grads, came, y_id, out):
    t, c, y, e = pos
    wide = jnp.float32
    units, lanes = came.shape[2], out.shape[2]
    me = c * 2 + e
    o_id = [wires.index() for _ in range(8)]
    here = pl.ds(pl.multiple_of(me * units, 16), units)
    fetch = []
    for far in (1, 2, 3, 0):
        k = lax.rem(c + far, 4)
        wires.arrive(y_id + k, lambda: came.at[k])
        where = pl.ds(pl.multiple_of((k * 2 + y) * 2 * lanes, 256), 2 * lanes)
        for m in range(3):

            def add(r):
                both = grads[m, r, where].astype(wide) + came[k, m, r].astype(wide)
                grads[m, r, where] = both.astype(grads.dtype)

            by_rows(units, 2 * lanes, add)
        for f in range(2):
            g = e if f == 0 else 1 - e
            src = lambda k=k, g=g: grads.at[
                :, pl.ds(0, units), pl.ds(pl.multiple_of(((k * 2 + y) * 2 + g) * lanes, 128), lanes)
            ]
            if far == 0 and f == 0:
                fetch.append(wires.fetch(wires.index(), src(), out.at[:, here]))
            else:
                wires.push(o_id[far * 2 + f], src, lambda: out.at[:, here], (t, k, y * 2 + g))
        yield
    for far in (1, 2, 3, 0):
        for f in range(2):
            if far == 0 and f == 0:
                continue
            k = lax.rem(c + 4 - far, 4)
            g = e if f == 0 else 1 - e
            wires.arrive(
                o_id[far * 2 + f],
                lambda: out.at[:, pl.ds(pl.multiple_of((k * 2 + g) * units, 16), units)],
            )
    fetch[0].wait()


def swap_halves(x):
    lane = lax.broadcasted_iota(jnp.int32, x.shape, 1)
    ahead, behind = pltpu.roll(x, x.shape[1] - 32, 1), pltpu.roll(x, 32, 1)
    return jnp.where(lax.rem(lane, 64) < 32, ahead, behind)


def head_probs(query, keys, allowed):
    scores = times_transposed(query, keys) * (HEAD_SIZE ** (-0.5))
    scores = jnp.where(allowed, scores, NEGATIVE)
    shifted = jnp.exp(scores - jnp.max(scores, axis=-1, keepdims=True))
    return shifted * (1.0 / jnp.sum(shifted, axis=-1, keepdims=True))


def norm_rows(upstream, inputs, gain):
    rms = lax.rsqrt(jnp.mean(inputs * inputs, axis=-1, keepdims=True) + EPS)
    gain_grad = jnp.sum(upstream * inputs * rms, axis=0, keepdims=True)
    scaled = upstream * gain
    inner = jnp.mean(scaled * inputs, axis=-1, keepdims=True)
    return rms * scaled - inputs * (rms * rms * rms * inner), gain_grad


def advance(parts, count=1):
    for _ in range(count):
        for part in list(parts):
            try:
                next(part)
            except StopIteration:
                parts.remove(part)


def pick(c, table):
    value = table[0]
    for i in range(1, 4):
        value = jnp.where(c == i, table[i], value)
    return value


NEAREST = ((0, 1, 2, 3), (1, 0, 2, 3), (2, 3, 1, 0), (3, 2, 1, 0))


def layer_kernel(
    lengths, states, gains, qkv, out_w, w3, gy, cosine, sine,
    layer_out, grad_states, g3_out, gq_out, go_out, gain_out, qkv_kept, part_b,
    send, recv, credit, qkv_all, out_all, gain_all, hidden, normed_one, q_rot, kv_all, mixed, gn_own,
    w3_all, gy_all, nt_all, act_t, part_g, stage_b, unit_in, kv_own, pair_out, pair_in, nt,
    near, x_in, came, grad_hidden, grad_low, branch, mixed_t, grad_mixed, gqkv, normed_t, gq_part,
    dk, dv, kv_part, kv_in, gains_sum, gain_in, *scratch,
):
    pos = position()
    t, c, y, e = pos
    low, wide = jnp.bfloat16, jnp.float32
    wires = Wires(send, recv)
    d = y * 2 + e
    me = c * 4 + d
    here, beside, over = (t, c, d), (t, c, y * 2 + 1 - e), (1 - t, c, d)
    peers = [(True, over)]
    for i in range(1, 16):
        q = lax.rem(me + i, 16)
        peers.append((True, (t, q // 4, lax.rem(q, 4))))
    greet(peers)
    tokens, width = states.shape
    half = width // 2
    block, n_all = qkv.shape
    n_query = q_rot.shape[1]
    n_key = (n_all - n_query) // 2
    lanes = out_w.shape[1]
    units = unit_in.shape[2]
    scaled = grad_hidden

    def lane_block(q, size=lanes):
        return pl.ds(pl.multiple_of(q * size, 128), size)

    gain_id = [wires.index() for _ in range(16)]
    for i in range(1, 16):
        q = lax.rem(me + i, 16)
        wires.push(
            gain_id[i], lambda: gains, lambda: gain_all.at[:, lane_block(me)],
            (t, q // 4, lax.rem(q, 4)),
        )
    fetch_gain = wires.fetch(wires.index(), gains, gain_all.at[:, lane_block(me)])
    g_qkv = [
        plane_gather(wires, pos, lambda: qkv, lambda k, f: rows(qkv_all, (k * 4 + f) * block, block))
    ]
    g_out = [
        plane_gather(
            wires, pos, lambda: out_w, lambda k, f: out_all.at[:, lane_block(k * 4 + f)]
        )
    ]
    g_unit = [
        unit_scatter(
            wires, pos,
            lambda q: w3.at[:, pl.ds(pl.multiple_of(q * units, 16), units)],
            lambda k, f: w3_all.at[:, pl.ds(0, units), lane_block(k * 4 + f)],
        )
    ]

    def spot(ref):
        return lambda f, k, h: ref.at[
            pl.ds(pl.multiple_of((k * 2 + f) * tokens, 16), tokens), lane_block(h, half)
        ]

    g_gy = [token_gather(wires, pos, None, spot(gy_all), lambda h: gy.at[:, lane_block(h, half)])]
    advance(g_qkv)
    advance(g_gy)
    w3_all[:, units:, :] = jnp.zeros_like(w3_all[:, units:, :])

    def scale_rows(r):
        x = states[r].astype(wide)
        scaled[r] = x * lax.rsqrt(jnp.mean(x * x, axis=-1, keepdims=True) + EPS)

    by_rows(tokens, width, scale_rows)
    advance(g_qkv)
    advance(g_out)
    advance(g_gy)
    advance(g_qkv)
    advance(g_out)
    advance(g_gy)
    advance(g_qkv)
    advance(g_out)
    advance(g_gy)
    while g_qkv:
        advance(g_qkv)
    fetch_gain.wait()
    for i in range(1, 16):
        q = lax.rem(me + 16 - i, 16)
        wires.arrive(gain_id[i], lambda: gain_all.at[:, lane_block(q)])
    gain_one = gain_all[...].astype(wide)[0:1]
    gain_two = gain_all[...].astype(wide)[1:2]

    save_qkv = wires.fetch(wires.index(), qkv_all, qkv_kept)

    def norm_one(r):
        normed_one[r] = (scaled[r] * gain_one).astype(low)

    by_rows(tokens, width, norm_one)

    def turned(x):
        return x * cosine[...] + swap_halves(x) * sine[...]

    tail = dot_nn(normed_one[...], qkv_all[:, n_query:])
    kv_own[:, :n_key] = turned(tail[:, :n_key]).astype(low)
    kv_own[:, n_key:] = tail[:, n_key:].astype(low)
    kv_all[pl.ds(pl.multiple_of(c * tokens, 16), tokens)] = kv_own[...]
    kv_id = [wires.index() for _ in range(3)]
    for i in range(3):
        k = lax.rem(c + i + 1, 4)
        wires.push(kv_id[i], lambda: kv_own, lambda: rows(kv_all, c * tokens, tokens), (t, k, d))
    advance(g_unit)

    def project(j, carry):
        where = pl.ds(pl.multiple_of(j * 256, 256), 256)
        two = dot_nn(normed_one[...], qkv_all[:, where])
        for h in range(2):
            slab = pl.ds(pl.multiple_of(j * 256 + h * 128, 128), 128)
            q_rot[:, slab] = turned(two[:, h * 128 : (h + 1) * 128]).astype(low)
        return carry

    lax.fori_loop(0, n_query // 256, project, 0)
    advance(g_out)
    for i in range(3):
        k = lax.rem(c + 3 - i, 4)
        wires.arrive(kv_id[i], lambda: rows(kv_all, k * tokens, tokens))
    q_pos = c * tokens + lax.broadcasted_iota(jnp.int32, (tokens, kv_all.shape[0]), 0)
    k_pos = lax.broadcasted_iota(jnp.int32, (tokens, kv_all.shape[0]), 1)
    allowed = (k_pos <= q_pos) & (k_pos < lengths[0])
    pairs = n_query // 256
    for g in range(2):
        keys = kv_all[:, g * HEAD_SIZE : (g + 1) * HEAD_SIZE]
        values = kv_all[:, n_key + g * HEAD_SIZE : n_key + (g + 1) * HEAD_SIZE]

        def pair(j, carry, g=g, keys=keys, values=values):
            slab = pl.ds(pl.multiple_of((g * pairs + j) * 128, 128), 128)
            q_two = q_rot[:, slab]
            both_heads = []
            for h in range(2):
                probs = head_probs(q_two[:, h * HEAD_SIZE : (h + 1) * HEAD_SIZE], keys, allowed)
                both_heads.append(dot_nn(probs.astype(low), values))
            mixed[:, slab] = jnp.concatenate(both_heads, axis=1).astype(low)
            return carry

        lax.fori_loop(0, pairs, pair, 0)
        if g == 0:
            advance(g_out)
    while g_out:
        advance(g_out)
    advance(g_unit)
    pair_id = [wires.index() for _ in range(4)]
    for i in range(4):
        for j in range(2):
            where = pl.ds(i * (width // 4) + j * (width // 8), width // 8)
            pair_out[:, where] = dot_nn(mixed[...], out_all[:, where]).astype(low)
        piece = pl.ds(i * (width // 4), width // 4)
        wires.push(pair_id[i], lambda p=piece: pair_out.at[:, p], lambda p=piece: pair_in.at[:, p], over)
    advance(g_unit, 2)
    for i in range(4):
        piece = pl.ds(i * (width // 4), width // 4)
        wires.arrive(pair_id[i], lambda: pair_in.at[:, piece])

    def norm_two(r):
        total = states[r].astype(wide) + (pair_out[r].astype(wide) + pair_in[r].astype(wide))
        hidden[r] = total
        factor = lax.rsqrt(jnp.mean(total * total, axis=-1, keepdims=True) + EPS)
        nt[r] = (total * factor * gain_two).astype(low)

    by_rows(tokens, width, norm_two)

    gathers = []
    for source, target in ((nt, nt_all),):
        at = spot(target)
        z_id, x_id, e_id, f_id = [[wires.index() for _ in range(4)][0] for _ in range(4)]
        gathers.append((at, z_id, x_id, e_id, f_id))
        own_half = lambda h, source=source: source.at[:, lane_block(h, half)]
        for i in (3, 1, 2):
            k = lax.rem(c + i, 4)
            wires.push(
                wires.index(), lambda own=own_half: own(t), lambda at=at: at(e, c, t), (t, k, d),
                lands=z_id + c,
            )
        wires.push(e_id + c, lambda own=own_half: own(t), lambda at=at: at(e, c, t), beside)
        wires.push(f_id + c, lambda own=own_half: own(1 - t), lambda at=at: at(e, c, 1 - t), beside)
    at_home = pl.ds(pl.multiple_of((c * 2 + e) * tokens, 16), tokens)
    nt_all[at_home] = nt[...]
    advance(g_unit, 4)
    while g_gy:
        advance(g_gy)

    def nearest(j):
        return pick(c, [sum_of(j, NEAREST[i]) for i in range(4)])

    def sum_of(j, order):
        value = order[0]
        for i in range(1, 4):
            value = jnp.where(j == i, order[i], value)
        return value

    def stage_one(j):
        k = nearest(j)
        for at, z_id, x_id, e_id, f_id in gathers:
            wires.arrive(z_id + k, lambda: at(e, k, t))
            wires.copy(x_id + k, at(e, k, t), at(e, k, t), over).start()
            wires.copy(e_id + k, at(e, k, t), at(e, k, t), beside).start()

    def stage_two(j):
        k = nearest(j)
        for at, z_id, x_id, e_id, f_id in gathers:

            def act():
                wires.arrive(x_id + k, lambda: at(e, k, 1 - t))
                wires.copy(f_id + k, at(e, k, 1 - t), at(e, k, 1 - t), beside).start()

            pl.when(j > 0)(act)
        for at, z_id, x_id, e_id, f_id in gathers:
            wires.arrive(e_id + k, lambda: at(1 - e, k, t))
            wires.arrive(f_id + k, lambda: at(1 - e, k, 1 - t))

    n_id = [wires.index() for _ in range(4)][0]
    r_id = [wires.index() for _ in range(4)][0]

    def part_rows(k, f):
        return part_g.at[pl.ds(pl.multiple_of((k * 2 + f) * tokens, 16), tokens)]

    mine, other = lane_block(t, half), lane_block(1 - t, half)

    def stage_three(j):
        k = nearest(j)
        wires.arrive(n_id + k, lambda: near.at[k])
        ours = part_rows(k, e)

        def away(r):
            total = ours[r, other].astype(wide) + near[k, r, other].astype(wide)
            near[k, r, other] = total.astype(low)

        by_rows(tokens, half, away)
        wires.copy(r_id + k, near.at[k, :, other], x_in.at[k], over).start()

    def kept(k, r):
        return (
            part_rows(k, e)[r, mine].astype(wide)
            + near[k, r, mine].astype(wide)
            + x_in[k, r].astype(wide)
        )

    s_id = [wires.index() for _ in range(4)][0]

    def stage_four(j):
        k = nearest(j)
        wires.arrive(r_id + k, lambda: x_in.at[k])

        def add(r):
            near[k, r, mine] = kept(k, r).astype(low)

        by_rows(tokens, half, add)
        i = lax.rem(k - c + 4, 4)
        wires.copy(s_id + i, near.at[k, :, mine], came.at[i - 1], (t, k, d)).start()

    padded = act_t.shape[0]
    act = qkv_all.at[pl.ds(0, tokens * 8), pl.ds(0, padded)]
    both = qkv_all.at[pl.ds(0, tokens * 8), pl.ds(padded, 2 * padded)]
    both_t = qkv_all.at[pl.ds(tokens * 8, 2 * padded), pl.ds(0, tokens * 8)]
    b_id = wires.index()

    def stored(k):
        where = pl.ds(pl.multiple_of(k * 2 * tokens, 16), 2 * tokens)
        return pltpu.make_async_copy(stage_b, part_b.at[where], wires.recv.at[b_id])

    def swiglu(j, carry):
        stage_two(j)
        k = nearest(j)
        where = pl.ds(pl.multiple_of(k * 2 * tokens, 16), 2 * tokens)
        x = nt_all[where]
        gate = times_transposed(x, w3_all[0])
        up = times_transposed(x, w3_all[1])
        grad_act = times_transposed(gy_all[where], w3_all[2])
        sigma = jax.nn.sigmoid(gate)
        swish = gate * sigma
        act[where] = (swish * up).astype(low)
        wide_units = gate.shape[1]
        both[where, :wide_units] = (
            grad_act * up * (sigma * (1.0 + gate * (1.0 - sigma)))
        ).astype(low)
        both[where, wide_units:] = (grad_act * swish).astype(low)
        for i in range(4):
            piece = slice(i * (width // 4), (i + 1) * (width // 4))
            part_g[where, piece] = (
                dot_nn(both[where, :wide_units], w3_all[0, :, piece])
                + dot_nn(both[where, wide_units:], w3_all[1, :, piece])
            ).astype(low)
        wires.copy(n_id + k, part_rows(k, 1 - e), near.at[k], beside).start()
        pl.when(j > 0)(lambda: stored(0).wait())
        for i in range(4):
            piece = slice(i * (width // 4), (i + 1) * (width // 4))
            stage_b[:, piece] = dot_nn(act[where], w3_all[2, :, piece]).astype(low)
        stored(k).start()
        pl.when(j > 0)(lambda: stage_three(j - 1))
        pl.when(j > 2)(lambda: stage_four(j - 2))
        return carry

    for j in range(1, 4):
        stage_one(j)
    while g_unit:
        advance(g_unit)
    save_qkv.wait()
    wires.drain()
    lax.fori_loop(0, 4, swiglu, 0)
    stored(0).wait()
    stage_three(3)
    for k in range(4):
        away = c != k
        for at, z_id, x_id, e_id, f_id in gathers:
            half_at = lambda h, k=k, at=at: at(e, k, h)
            wires.owe(x_id + k, lambda f=half_at: f(t), away)
            wires.owe(e_id + k, lambda f=half_at: f(t), away)
            wires.owe(f_id + k, lambda f=half_at: f(1 - t), away)
        wires.owe(n_id + k, lambda k=k: part_rows(k, 1 - e))
        wires.owe(r_id + k, lambda k=k: near.at[k, :, other])
    for i in (1, 2, 3):
        k = lax.rem(c + i, 4)
        wires.owe(s_id + i, lambda k=k: near.at[k, :, mine])
    stage_four(2)
    act_t[...] = act[...].T
    both_t[...] = both[...].T

    def unit_grads(k, yy):
        where = lane_block(k * 2 + yy, 256)
        two = dot_nn(both_t[...], nt_all[:, where]).astype(low)
        w3_all[0, :units, where] = two[:units]
        w3_all[1, :units, where] = two[padded : padded + units]
        w3_all[2, :units, where] = dot_nn(act_t[...], gy_all[:, where]).astype(low)[:units]

    u_id = [wires.index() for _ in range(4)][0]
    across = (t, c, (1 - y) * 2 + e)

    def half_grads(k):
        return w3_all.at[:, pl.ds(0, units), lane_block(k * 2 + 1 - y, 256)]

    def send_units(j, carry):
        k = lax.rem(c + 1 + j, 4)
        unit_grads(k, 1 - y)
        wires.copy(u_id + k, half_grads(k), unit_in.at[k], across).start()
        return carry

    lax.fori_loop(0, 2, send_units, 0)
    stage_four(3)
    lax.fori_loop(2, 4, send_units, 0)

    def keep_units(j, carry):
        unit_grads(lax.rem(c + 1 + j, 4), y)
        return carry

    lax.fori_loop(0, 2, keep_units, 0)
    g_unit = [unit_gather(wires, pos, w3_all, unit_in, u_id, g3_out)]
    owed, bulk = wires.sent, []
    wires.sent = bulk
    advance(g_unit)
    wires.sent = owed
    wires.arrive(r_id + c, lambda: x_in.at[c])
    for i in (3, 1, 2):
        wires.arrive(s_id + i, lambda: came.at[i - 1])

    def done(r):
        total = kept(c, r)
        for i in range(3):
            total = total + came[i, r].astype(wide)
        gn_own[r, mine] = total.astype(low)

    by_rows(tokens, half, done)
    last = wires.index()
    wires.push(last, lambda: gn_own.at[:, mine], lambda: gn_own.at[:, mine], over)
    lax.fori_loop(2, 4, keep_units, 0)
    wires.sent = bulk
    advance(g_unit)
    wires.sent = owed
    wires.arrive(last, lambda: gn_own.at[:, other])
    wires.sent = owed
    wires.drain()
    wires.sent = bulk
    for k in range(4):
        wires.owe(u_id + k, lambda k=k: half_grads(k))
    for i, cond, device in (
        (0, True, beside), (1, True, over), (2, c > 0, (t, c - 1, d)), (3, c < 3, (t, c + 1, d))
    ):
        only(
            cond,
            functools.partial(
                pl.semaphore_signal, credit.at[i], inc=1, device_id=device, device_id_type=MESH
            ),
        )
    load_qkv = wires.fetch(wires.index(), qkv_kept, qkv_all)
    s_q, s_k, s_o = scratch[:4], scratch[4:8], scratch[8:12]
    t_b = (
        near, lambda k: part_g.at[pl.ds(k * tokens, tokens)], x_in, came.at[pl.ds(0, 4)], came.at[4]
    )
    second = [token_scatter(wires, pos, part_b, branch, t_b, credit)]
    advance(second)
    mixed_t[...] = mixed[...].T
    normed_t[...] = normed_one[...].T
    gains_sum[...] = jnp.zeros_like(gains_sum)

    def norm_two_back(r):
        value, grad = norm_rows(gn_own[r].astype(wide), hidden[r], gain_two)
        home = pl.ds(pl.multiple_of((c * 2 + e) * tokens + r.start, 16), 16)
        total = gy_all[home].astype(wide) + value
        grad_hidden[r] = total
        grad_low[r] = total.astype(low)
        gains_sum[1:2] += grad

    by_rows(tokens, width, norm_two_back)
    advance(second)

    def out_grad(j, carry):
        where = pl.ds(pl.multiple_of(j * 2 * lanes, 256), 2 * lanes)
        nt_all[:, where] = dot_nn(mixed_t[...], grad_low[:, where]).astype(low)
        return carry

    lax.fori_loop(0, 8, out_grad, 0)
    outs = [
        plane_scatter(
            wires, pos,
            lambda k, yy: nt_all.at[:, lane_block(k * 4 + yy * 2 + 1 - e)],
            lambda k, yy: nt_all.at[:, lane_block(k * 4 + yy * 2 + e)],
            n_query, s_o, lambda r, v: go_out.__setitem__(r, v),
        )
    ]
    advance(outs)

    def mix_grad(j, carry):
        where = pl.ds(pl.multiple_of(j * 256, 256), 256)
        grad_mixed[:, where] = times_transposed(grad_low[...], out_all[where, :]).astype(low)
        return carry

    lax.fori_loop(0, n_query // 256, mix_grad, 0)
    advance(outs, 4)
    advance(g_unit)

    scale = HEAD_SIZE ** (-0.5)
    pairs = n_query // 256
    for g in range(2):
        keys = kv_all[:, g * HEAD_SIZE : (g + 1) * HEAD_SIZE]
        values = kv_all[:, n_key + g * HEAD_SIZE : n_key + (g + 1) * HEAD_SIZE]
        dk[...] = jnp.zeros_like(dk)
        dv[...] = jnp.zeros_like(dv)

        def pair(j, carry, g=g, keys=keys, values=values):
            slab = pl.ds(pl.multiple_of((g * pairs + j) * 128, 128), 128)
            q_two, m_two = q_rot[:, slab], grad_mixed[:, slab]
            both = []
            for h in range(2):
                query = q_two[:, h * HEAD_SIZE : (h + 1) * HEAD_SIZE]
                upstream = m_two[:, h * HEAD_SIZE : (h + 1) * HEAD_SIZE]
                probs = head_probs(query, keys, allowed)
                dprob = times_transposed(upstream, values)
                delta = jnp.sum(probs * dprob, axis=-1, keepdims=True)
                grad_scores = (probs * (dprob - delta)).astype(low)
                both.append(dot_nn(grad_scores, keys))
                dk[...] += transposed_times(grad_scores, query)
                dv[...] += transposed_times(probs.astype(low), upstream)
            grads = jnp.concatenate(both, axis=1) * scale
            back = grads * cosine[...] - swap_halves(grads) * sine[...]
            gqkv[:, slab] = back.astype(low)
            return carry

        lax.fori_loop(0, pairs, pair, 0)
        for k in range(4):
            block = slice(k * tokens, (k + 1) * tokens)
            kv_part[k, :, g * HEAD_SIZE : (g + 1) * HEAD_SIZE] = (dk[block] * scale).astype(low)
            kv_part[k, :, n_key + g * HEAD_SIZE : n_key + (g + 1) * HEAD_SIZE] = dv[block].astype(low)
    kvg_id = [wires.index() for _ in range(3)]
    for i in range(3):
        k = lax.rem(c + i + 1, 4)
        wires.push(kvg_id[i], lambda k=k: kv_part.at[k], lambda i=i: kv_in.at[i], (t, k, d))

    def q_block(place, i, where):
        return place.at[pl.ds(pl.multiple_of(i * lanes, 16), lanes), where]

    def q_grad(core, place, where):
        def step(i, carry):
            here = lane_block(i * 2 + core)
            q_block(place, i, where)[...] = dot_nn(normed_t[here, :], gqkv[:, where]).astype(low)
            return carry

        lax.fori_loop(0, 8, step, 0)

    def q_sums(where, scratches):
        def done(r, value):
            gq_out[r, where] = value

        return plane_scatter(
            wires, pos,
            lambda k, yy: q_block(gy_all, k * 2 + yy, where),
            lambda k, yy: q_block(gq_part, k * 2 + yy, where),
            gq_out.shape[0], scratches, done,
        )

    first, rest = slice(0, n_query), slice(n_query, n_query + 2 * n_key)
    q_grad(1 - e, gy_all, first)
    queries = [q_sums(first, s_q)]
    advance(queries)
    q_grad(e, gq_part, first)
    advance(queries, 4)
    advance(second)
    advance(g_unit)
    total = kv_part[c].astype(wide)
    for i in range(3):
        wires.arrive(kvg_id[i], lambda: kv_in.at[i])
        total = total + kv_in[i].astype(wide)
    key_grads = total[:, :n_key]
    key_grads = key_grads * cosine[...] - swap_halves(key_grads) * sine[...]
    gqkv[:, n_query : n_query + n_key] = key_grads.astype(low)
    gqkv[:, n_query + n_key :] = total[:, n_key:].astype(low)
    q_grad(1 - e, gy_all, rest)
    others = [q_sums(rest, s_k)]
    advance(others)
    q_grad(e, gq_part, rest)
    load_qkv.wait()

    def normed_grad(j, carry):
        where = pl.ds(pl.multiple_of(j * 256, 256), 256)
        pair_out[:, where] = times_transposed(gqkv[...], qkv_all[where, :]).astype(low)
        return carry

    lax.fori_loop(0, width // 256, normed_grad, 0)
    p_id = wires.index()
    wires.push(p_id, lambda: pair_out, lambda: pair_in, (1 - t, c, d))
    advance(others, 4)
    advance(second)
    advance(outs)
    advance(second)
    wires.arrive(p_id, lambda: pair_in)

    def norm_one_back(r):
        upstream = pair_out[r].astype(wide) + pair_in[r].astype(wide)
        value, grad = norm_rows(upstream, states[r].astype(wide), gain_one)
        grad_states[r] = grad_hidden[r] + value
        gains_sum[0:1] += grad

    by_rows(tokens, width, norm_one_back)
    g_id = [wires.index() for _ in range(16)]

    def gain_block(q):
        return gains_sum.at[:, pl.ds(pl.multiple_of(q * lanes, 128), lanes)]

    for i in range(1, 16):
        q = lax.rem(me + i, 16)
        wires.push(
            g_id[i], lambda q=q: gain_block(q), lambda i=i: gain_in.at[i],
            (t, q // 4, lax.rem(q, 4)),
        )
    advance(outs)
    advance(second)
    advance(others)
    advance(outs)
    advance(queries)
    advance(others)
    advance(outs)
    advance(queries)
    advance(others)
    advance(queries)
    advance(others)
    advance(queries)
    advance(second)
    while g_unit:
        advance(g_unit)

    def finish(r):
        layer_out[r] = (hidden[r] + branch[r].astype(wide)).astype(low)

    by_rows(tokens, width, finish)
    gain = gains_sum[:, pl.ds(pl.multiple_of(me * lanes, 128), lanes)]
    for i in range(1, 16):
        wires.arrive(g_id[i], lambda: gain_in.at[i])
        gain = gain + gain_in[i]
    gain_out[...] = gain
    wires.drain()


def layer_call(lengths, states, gains, qkv, out_w, w3, gy, cosine, sine):
    shape = jax.ShapeDtypeStruct
    low, wide = jnp.bfloat16, jnp.float32
    tokens, width = states.shape
    n_query, lanes = out_w.shape
    n_all = qkv.shape[1]
    n_rest = n_all - n_query
    units = w3.shape[1] // 8
    padded = -(-units // 128) * 128
    all_tokens, keys = tokens * 8, tokens * 4
    half = width // 2
    vm = pltpu.VMEM
    return pl.pallas_call(
        layer_kernel,
        name="layer",
        out_shape=(
            shape((tokens, width), low),
            shape((tokens, width), wide),
            shape((3, units * 8, lanes), low),
            shape((lanes, n_all), wide),
            shape((n_query, lanes), wide),
            shape((8, lanes), wide),
            shape((width, n_all), low),
            shape((all_tokens, width), low),
        ),
        in_specs=[pl.BlockSpec(memory_space=pltpu.MemorySpace.SMEM), pl.BlockSpec(memory_space=VMEM)]
        + [pl.BlockSpec(memory_space=HBM)] * 5
        + [pl.BlockSpec(memory_space=VMEM)] * 2,
        out_specs=[
            pl.BlockSpec(memory_space=VMEM),
            pl.BlockSpec(memory_space=VMEM),
            pl.BlockSpec(memory_space=HBM),
            pl.BlockSpec(memory_space=VMEM),
            pl.BlockSpec(memory_space=VMEM),
            pl.BlockSpec(memory_space=VMEM),
            pl.BlockSpec(memory_space=HBM),
            pl.BlockSpec(memory_space=HBM),
        ],
        scratch_shapes=[
            pltpu.SemaphoreType.DMA((320,)),
            pltpu.SemaphoreType.DMA((320,)),
            pltpu.SemaphoreType.REGULAR((4,)),
            vm((width, n_all), low),
            vm((n_query, width), low),
            vm((16, width), low),
            vm((tokens, width), wide),
            vm((tokens, width), low),
            vm((tokens, n_query), low),
            vm((keys, n_rest), low),
            vm((tokens, n_query), low),
            vm((tokens, width), low),
            vm((3, padded, width), low),
            vm((all_tokens, width), low),
            vm((all_tokens, width), low),
            vm((padded, all_tokens), low),
            vm((all_tokens, width), low),
            vm((2 * tokens, width), low),
            vm((4, 3, units, width // 8), low),
            vm((tokens, n_rest), low),
            vm((tokens, width), low),
            vm((tokens, width), low),
            vm((tokens, width), low),
            vm((4, tokens, width), low),
            vm((4, tokens, half), low),
            vm((5, tokens, half), low),
            vm((tokens, width), wide),
            vm((tokens, width), low),
            vm((tokens, width), low),
            vm((n_query, tokens), low),
            vm((tokens, n_query), low),
            vm((tokens, n_all), low),
            vm((width, tokens), low),
            vm((8 * lanes, n_all), low),
            vm((keys, HEAD_SIZE), wide),
            vm((keys, HEAD_SIZE), wide),
            vm((4, tokens, n_rest), low),
            vm((3, tokens, n_rest), low),
            vm((8, width), wide),
            vm((16, 8, lanes), wide),
        ]
        + plane_scratch((lanes, n_query))
        + plane_scratch((lanes, n_rest))
        + plane_scratch((n_query, lanes)),
        compiler_params=pltpu.CompilerParams(
            collective_id=1, has_side_effects=True, vmem_limit_bytes=63 << 20
        ),
    )(lengths, states, gains, qkv, out_w, w3, gy, cosine, sine)


def plane_shards(
    states, lengths, first_gain, w_query, key_matrix, value_matrix, w_out, second_gain,
    w_gate, w_up, w_down, cotangent,
):
    low, wide = jnp.bfloat16, jnp.float32
    tokens = states.shape[1]
    positions = lax.axis_index("ctx") * tokens + jnp.arange(tokens, dtype=jnp.int32)
    cosine, sine = rope_tables(positions, HEAD_SIZE // 2)
    lane = jnp.arange(2 * HEAD_SIZE)
    turn = jnp.where((lane % HEAD_SIZE) < HEAD_SIZE // 2, -1.0, 1.0)
    cosine = jnp.tile(cosine[:, 0], (1, 4))
    sine = jnp.tile(sine[:, 0], (1, 4)) * turn[None, :]
    valid = (positions < lengths[0])[:, None]
    grad_y = jnp.where(valid, cotangent[0], jnp.zeros((), low))
    n_query, n_key = w_query.shape[1], key_matrix.shape[1]
    lanes = w_out.shape[1]
    qkv = jnp.concatenate([w_query, key_matrix, value_matrix], axis=1)
    gains = jnp.concatenate(
        [first_gain[None], second_gain[None], jnp.zeros((14, lanes), low)], axis=0
    )
    w3 = jnp.stack([w_gate.T, w_up.T, w_down])
    layer_out, grad_states, g3, gq, go, gain, _, _ = layer_call(
        lengths, states[0], gains, qkv, w_out, w3, grad_y, cosine, sine
    )
    return (
        layer_out[None],
        grad_states[None],
        gain[0],
        gq[:, :n_query],
        gq[:, n_query : n_query + n_key],
        gq[:, n_query + n_key :],
        go,
        gain[1],
        g3[0].T.astype(wide),
        g3[1].T.astype(wide),
        g3[2].astype(wide),
    )


def fits(mesh):
    return dict(mesh.shape) == {"tensor": 2, "ctx": 4, "dp": 4}


def solution(mesh):
    placed = (
        P("dp", "ctx", None),
        P("dp"),
        P(("ctx", "dp")),
        P(("ctx", "dp"), "tensor"),
        P(("ctx", "dp"), "tensor"),
        P(("ctx", "dp"), "tensor"),
        P("tensor", ("ctx", "dp")),
        P(("ctx", "dp")),
        P(("ctx", "dp"), "tensor"),
        P(("ctx", "dp"), "tensor"),
        P("tensor", ("ctx", "dp")),
        P("dp", "ctx", None),
    )
    return jax.shard_map(
        plane_shards if fits(mesh) else shards,
        mesh=mesh,
        in_specs=placed,
        out_specs=(
            P("dp", "ctx", None),
            P("dp", "ctx", None),
            P(("ctx", "dp")),
            P(("ctx", "dp"), "tensor"),
            P(("ctx", "dp"), "tensor"),
            P(("ctx", "dp"), "tensor"),
            P("tensor", ("ctx", "dp")),
            P(("ctx", "dp")),
            P(("ctx", "dp"), "tensor"),
            P(("ctx", "dp"), "tensor"),
            P("tensor", ("ctx", "dp")),
        ),
        check_vma=False,
    )
```

```python
import functools

import jax
import jax.numpy as jnp
from jax import lax
from jax.experimental import pallas as pl
from jax.experimental.pallas import tpu as pltpu
from jax.sharding import PartitionSpec as P

HEAD_SIZE = 64


EPS = 1e-05
THETA = 10000.0
NEGATIVE = -1e30


def rope_tables(positions, half_width):
    inverse = jnp.exp(-jnp.log(THETA) * jnp.arange(half_width).astype(jnp.float32) / half_width)
    angles = positions.astype(jnp.float32)[:, None] * inverse[None, :]
    return (jnp.cos(angles)[:, None, :], jnp.sin(angles)[:, None, :])


def apply_rotation(vectors, cosine_table, sine_table):
    half_width = vectors.shape[-1] // 2
    first_half = vectors[..., :half_width]
    second_half = vectors[..., half_width:]
    return jnp.concatenate(
        [
            first_half * cosine_table - second_half * sine_table,
            second_half * cosine_table + first_half * sine_table,
        ],
        axis=-1,
    )


def rotate_back(grads, cosine_table, sine_table):
    half_width = grads.shape[-1] // 2
    first_half = grads[..., :half_width]
    second_half = grads[..., half_width:]
    return jnp.concatenate(
        [
            first_half * cosine_table + second_half * sine_table,
            second_half * cosine_table - first_half * sine_table,
        ],
        axis=-1,
    )


def times_transposed(left, right):
    return lax.dot_general(
        left, right, (((1,), (1,)), ((), ())), preferred_element_type=jnp.float32
    )


def transposed_times(left, right):
    return lax.dot_general(
        left, right, (((0,), (0,)), ((), ())), preferred_element_type=jnp.float32
    )


def norm_back(upstream, inputs, inverse_rms, gain):
    scaled = upstream * gain
    gain_grad = jnp.sum(upstream * inputs * inverse_rms, axis=0)
    inner = jnp.mean(scaled * inputs, axis=-1, keepdims=True)
    return (inverse_rms * scaled - inputs * inverse_rms**3 * inner, gain_grad)


def shards(
    states,
    lengths,
    first_gain,
    w_query,
    key_matrix,
    value_matrix,
    w_out,
    second_gain,
    w_gate,
    w_up,
    w_down,
    cotangent,
):
    low_type = jnp.bfloat16
    wide_type = jnp.float32
    gathered = (
        lax.all_gather(first_gain, ("ctx", "dp"), axis=0, tiled=True),
        lax.all_gather(w_query, ("ctx", "dp"), axis=0, tiled=True),
        lax.all_gather(key_matrix, ("ctx", "dp"), axis=0, tiled=True),
        lax.all_gather(value_matrix, ("ctx", "dp"), axis=0, tiled=True),
        lax.all_gather(w_out, ("ctx", "dp"), axis=1, tiled=True),
        lax.all_gather(second_gain, ("ctx", "dp"), axis=0, tiled=True),
        lax.all_gather(w_gate, ("ctx", "dp"), axis=0, tiled=True),
        lax.all_gather(w_up, ("ctx", "dp"), axis=0, tiled=True),
        lax.all_gather(w_down, ("ctx", "dp"), axis=1, tiled=True),
    )
    (
        gain_one,
        full_query,
        full_key,
        full_value,
        full_out,
        gain_two,
        full_gate,
        full_up,
        full_down,
    ) = gathered
    gain_one = gain_one.astype(wide_type)
    gain_two = gain_two.astype(wide_type)
    tokens = states.shape[1]
    inputs = states[0].astype(wide_type)
    seq_length = lengths[0]
    first_pos = lax.axis_index("ctx") * tokens
    positions = first_pos + jnp.arange(tokens, dtype=jnp.int32)
    cosine_table, sine_table = rope_tables(positions, HEAD_SIZE // 2)
    heads = full_query.shape[1] // HEAD_SIZE
    kv_heads = full_key.shape[1] // HEAD_SIZE
    group_factor = heads // kv_heads
    scale = HEAD_SIZE ** (-0.5)
    rms_one = lax.rsqrt(jnp.mean(inputs * inputs, axis=-1, keepdims=True) + EPS)
    first_normed = (inputs * rms_one * gain_one).astype(low_type)
    query_rows = jnp.dot(first_normed, full_query, preferred_element_type=wide_type)
    fresh_keys = jnp.dot(first_normed, full_key, preferred_element_type=wide_type)
    values_new = jnp.dot(first_normed, full_value, preferred_element_type=wide_type)
    query_rotated = (
        apply_rotation(query_rows.reshape(tokens, heads, HEAD_SIZE), cosine_table, sine_table)
        .astype(low_type)
        .reshape(tokens, kv_heads, group_factor, HEAD_SIZE)
    )
    key_rot = (
        apply_rotation(fresh_keys.reshape(tokens, kv_heads, HEAD_SIZE), cosine_table, sine_table)
        .astype(low_type)
        .reshape(tokens, kv_heads * HEAD_SIZE)
    )
    value_lower = values_new.astype(low_type)
    keys_all, values_all = (
        lax.all_gather(key_rot, "ctx", axis=0, tiled=True),
        lax.all_gather(value_lower, "ctx", axis=0, tiled=True),
    )
    total_keys = keys_all.shape[0]
    key_block = min(512, total_keys)
    block_count = total_keys // key_block

    def block_scores(begin_at):
        key_piece = lax.dynamic_slice_in_dim(keys_all, begin_at, key_block, 0).reshape(
            key_block, kv_heads, HEAD_SIZE
        )
        value_piece = lax.dynamic_slice_in_dim(values_all, begin_at, key_block, 0).reshape(
            key_block, kv_heads, HEAD_SIZE
        )
        scores = (
            jnp.einsum("qkgd,pkd->kgqp", query_rotated, key_piece, preferred_element_type=wide_type)
            * scale
        )
        key_pos = begin_at + jnp.arange(key_block, dtype=jnp.int32)
        allowed = (key_pos[None, :] <= positions[:, None]) & (key_pos[None, :] < seq_length)
        return (jnp.where(allowed, scores, NEGATIVE), key_piece, value_piece)

    def max_pass(index, carry):
        running, total = carry
        scores = block_scores(index * key_block)[0]
        newest = jnp.maximum(running, jnp.max(scores, axis=-1))
        total = total * jnp.exp(running - newest) + jnp.sum(
            jnp.exp(scores - newest[..., None]), axis=-1
        )
        return (newest, total)

    start_max = jnp.full((kv_heads, group_factor, tokens), NEGATIVE, wide_type)
    running, total = lax.fori_loop(0, block_count, max_pass, (start_max, jnp.zeros_like(start_max)))
    log_total = running + jnp.log(total)

    def mix_pass(index, carry):
        scores, key_piece, value_piece = block_scores(index * key_block)
        weights = jnp.exp(scores - log_total[..., None]).astype(low_type)
        return carry + jnp.einsum(
            "kgqp,pkd->qkgd", weights, value_piece, preferred_element_type=wide_type
        )

    mixed = lax.fori_loop(
        0, block_count, mix_pass, jnp.zeros((tokens, kv_heads, group_factor, HEAD_SIZE), wide_type)
    )
    mixed_low = mixed.reshape(tokens, heads * HEAD_SIZE).astype(low_type)
    attention = lax.psum(jnp.dot(mixed_low, full_out, preferred_element_type=wide_type), "tensor")
    hidden = inputs + attention
    rms_two = lax.rsqrt(jnp.mean(hidden * hidden, axis=-1, keepdims=True) + EPS)
    normed_two = (hidden * rms_two * gain_two).astype(low_type)
    gate = jnp.dot(normed_two, full_gate, preferred_element_type=wide_type)
    up_proj = jnp.dot(normed_two, full_up, preferred_element_type=wide_type)
    sigma = jax.nn.sigmoid(gate)
    swish = gate * sigma
    activated = (swish * up_proj).astype(low_type)
    branch = lax.psum(
        jnp.dot(activated, full_down, preferred_element_type=wide_type).astype(jnp.bfloat16),
        "tensor",
    ).astype(jnp.float32)
    layer_out = (hidden + branch).astype(low_type)
    valid = (positions < seq_length)[:, None]
    grad_y = jnp.where(valid, cotangent[0].astype(wide_type), 0.0)
    grad_y_low = grad_y.astype(low_type)
    grad_down = transposed_times(activated, grad_y_low)
    grad_act = times_transposed(grad_y_low, full_down)
    grad_gate_low = (grad_act * up_proj * (sigma * (1.0 + gate * (1.0 - sigma)))).astype(low_type)
    grad_up_low = (grad_act * swish).astype(low_type)
    grad_gate = transposed_times(normed_two, grad_gate_low)
    grad_up = transposed_times(normed_two, grad_up_low)
    grad_normed_two = lax.psum(
        times_transposed(grad_gate_low, full_gate) + times_transposed(grad_up_low, full_up),
        "tensor",
    )
    norm_part, grad_gain_two = norm_back(grad_normed_two, hidden, rms_two, gain_two)
    grad_hidden = grad_y + norm_part
    grad_hidden_low = grad_hidden.astype(low_type)
    grad_out = transposed_times(mixed_low, grad_hidden_low)
    grad_mixed = (
        times_transposed(grad_hidden_low, full_out)
        .astype(low_type)
        .reshape(tokens, kv_heads, group_factor, HEAD_SIZE)
    )

    def delta_pass(index, carry):
        scores, key_piece, value_piece = block_scores(index * key_block)
        probs = jnp.exp(scores - log_total[..., None])
        dprob = jnp.einsum(
            "qkgd,pkd->kgqp", grad_mixed, value_piece, preferred_element_type=wide_type
        )
        return carry + jnp.sum(probs * dprob, axis=-1)

    delta = lax.fori_loop(
        0, block_count, delta_pass, jnp.zeros((kv_heads, group_factor, tokens), wide_type)
    )

    def grad_pass(index, carry):
        grad_queries, key_grads, value_grads = carry
        begin_at = index * key_block
        scores, key_piece, value_piece = block_scores(begin_at)
        probs = jnp.exp(scores - log_total[..., None])
        dprob = jnp.einsum(
            "qkgd,pkd->kgqp", grad_mixed, value_piece, preferred_element_type=wide_type
        )
        grad_scores = (probs * (dprob - delta[..., None])).astype(low_type)
        grad_queries = (
            grad_queries
            + jnp.einsum("kgqp,pkd->qkgd", grad_scores, key_piece, preferred_element_type=wide_type)
            * scale
        )
        key_part = (
            jnp.einsum(
                "kgqp,qkgd->pkd", grad_scores, query_rotated, preferred_element_type=wide_type
            )
            * scale
        )
        value_part = jnp.einsum(
            "kgqp,qkgd->pkd", probs.astype(low_type), grad_mixed, preferred_element_type=wide_type
        )
        key_grads = lax.dynamic_update_slice_in_dim(
            key_grads, key_part.reshape(key_block, kv_heads * HEAD_SIZE), begin_at, 0
        )
        value_grads = lax.dynamic_update_slice_in_dim(
            value_grads, value_part.reshape(key_block, kv_heads * HEAD_SIZE), begin_at, 0
        )
        return (grad_queries, key_grads, value_grads)

    empty_keys = jnp.zeros((total_keys, kv_heads * HEAD_SIZE), wide_type)
    start_state = (
        jnp.zeros((tokens, kv_heads, group_factor, HEAD_SIZE), wide_type),
        empty_keys,
        empty_keys,
    )
    grad_queries, key_grads, value_grads = lax.fori_loop(0, block_count, grad_pass, start_state)
    key_local, value_local = (
        lax.psum_scatter(key_grads, "ctx", scatter_dimension=0, tiled=True),
        lax.psum_scatter(value_grads, "ctx", scatter_dimension=0, tiled=True),
    )
    grad_query_low = (
        rotate_back(grad_queries.reshape(tokens, heads, HEAD_SIZE), cosine_table, sine_table)
        .reshape(tokens, heads * HEAD_SIZE)
        .astype(low_type)
    )
    grad_key_low = (
        rotate_back(key_local.reshape(tokens, kv_heads, HEAD_SIZE), cosine_table, sine_table)
        .reshape(tokens, kv_heads * HEAD_SIZE)
        .astype(low_type)
    )
    grad_value_low = value_local.astype(low_type)
    grad_query = transposed_times(first_normed, grad_query_low)
    grad_key = transposed_times(first_normed, grad_key_low)
    grad_value = transposed_times(first_normed, grad_value_low)
    grad_normed_one = lax.psum(
        (
            times_transposed(grad_query_low, full_query)
            + times_transposed(grad_key_low, full_key)
            + times_transposed(grad_value_low, full_value)
        ).astype(jnp.bfloat16),
        "tensor",
    ).astype(jnp.float32)
    first_part, grad_gain_one = norm_back(grad_normed_one, inputs, rms_one, gain_one)
    grad_states = grad_hidden + first_part
    summed = tuple(
        (
            lax.psum_scatter(grad_gain_one, ("ctx", "dp"), scatter_dimension=0, tiled=True),
            lax.psum_scatter(grad_query, ("ctx", "dp"), scatter_dimension=0, tiled=True),
            lax.psum_scatter(grad_key, ("ctx", "dp"), scatter_dimension=0, tiled=True),
            lax.psum_scatter(grad_value, ("ctx", "dp"), scatter_dimension=0, tiled=True),
            lax.psum_scatter(grad_out, ("ctx", "dp"), scatter_dimension=1, tiled=True),
            lax.psum_scatter(grad_gain_two, ("ctx", "dp"), scatter_dimension=0, tiled=True),
            lax.psum_scatter(grad_gate, ("ctx", "dp"), scatter_dimension=0, tiled=True),
            lax.psum_scatter(grad_up, ("ctx", "dp"), scatter_dimension=0, tiled=True),
            lax.psum_scatter(grad_down, ("ctx", "dp"), scatter_dimension=1, tiled=True),
        )
    )
    return (
        layer_out[None],
        grad_states[None],
        summed[0],
        summed[1],
        summed[2],
        summed[3],
        summed[4],
        summed[5],
        summed[6],
        summed[7],
        summed[8],
    )


MESH = pl.DeviceIdType.MESH
HBM = pltpu.MemorySpace.HBM
VMEM = pltpu.MemorySpace.VMEM
STEPS = [(1, -1), (1, 1), (2, -1), (2, 1), (3, -1), (3, 1)]


def position():
    t, c, d = lax.axis_index("tensor"), lax.axis_index("ctx"), lax.axis_index("dp")
    return t, c, d // 2, d % 2


def only(cond, act):
    if cond is True:
        act()
    else:
        pl.when(cond)(act)


class Wires:
    def __init__(self, send, recv):
        self.send, self.recv, self.used, self.sent = send, recv, 0, []

    def index(self):
        self.used += 1
        return self.used - 1

    def copy(self, i, src, dst, device, lands=None):
        return pltpu.make_async_remote_copy(
            src_ref=src,
            dst_ref=dst,
            send_sem=self.send.at[i],
            recv_sem=self.recv.at[i if lands is None else lands],
            device_id=device,
            device_id_type=MESH,
        )

    def push(self, i, src, dst, device, cond=True, lands=None):
        only(cond, lambda: self.copy(i, src(), dst(), device, lands).start())
        self.sent.append((cond, lambda: self.copy(i, src(), dst(), device).wait_send()))

    def owe(self, i, src, cond=True):
        self.sent.append((cond, lambda: self.copy(i, src(), src(), position_id()).wait_send()))

    def arrive(self, i, dst, cond=True):
        def act():
            place = dst()
            self.copy(i, place, place, position_id()).wait_recv()

        only(cond, act)

    def local(self, i, src, dst):
        def make():
            return pltpu.make_async_copy(src(), dst(), self.send.at[i])

        make().start()
        self.sent.append((True, lambda: make().wait()))

    def fetch(self, i, src, dst):
        copy = pltpu.make_async_copy(src, dst, self.recv.at[i])
        copy.start()
        return copy

    def drain(self):
        for cond, act in self.sent:
            only(cond, act)
        self.sent = []


def position_id():
    t, c, y, e = position()
    return (t, c, y * 2 + e)


def greet(peers):
    barrier = pltpu.get_barrier_semaphore()
    count = 0
    for cond, device in peers:
        only(
            cond,
            functools.partial(
                pl.semaphore_signal, barrier, inc=1, device_id=device, device_id_type=MESH
            ),
        )
        count = count + (1 if cond is True else cond.astype(jnp.int32))
    pl.semaphore_wait(barrier, count)


def around(pos, chain=True, x=False, y=False, core=True, row=False):
    t, c, yy, e = pos
    d = yy * 2 + e
    peers = []
    if chain:
        peers += [(c < 3, (t, c + 1, d)), (c > 0, (t, c - 1, d))]
    if x:
        peers.append((True, (1 - t, c, d)))
    if y:
        peers.append((True, (t, c, (1 - yy) * 2 + e)))
    if core:
        peers.append((True, (t, c, yy * 2 + 1 - e)))
    return peers


def reach(c, s, sign):
    k = c + sign * s
    return k, ((k >= 0) if sign < 0 else (k <= 3))


def plane_gather(wires, pos, src, at):
    t, c, y, e = pos
    d, d_y, d_e = y * 2 + e, (1 - y) * 2 + e, y * 2 + 1 - e
    z_id = {key: wires.index() for key in STEPS}
    y_id = {key: wires.index() for key in [(0, 0)] + STEPS}
    e_id = {key: wires.index() for key in [(0, 0)] + STEPS}
    f_id = {key: wires.index() for key in [(0, 0)] + STEPS}
    fetch = wires.fetch(wires.index(), src(), at(c, d))

    def spread(key, block, place, cond):
        s, sign = key
        if s < 3:
            for way in ((-1, 1) if s == 0 else (sign,)):
                nxt = c - way
                here = (nxt >= 0) if way > 0 else (nxt <= 3)
                wires.push(
                    z_id[(s + 1, way)], block, place, (t, nxt, d),
                    here if cond is True else (cond & here),
                )
        wires.push(y_id[key], block, place, (t, c, d_y), cond)
        wires.push(e_id[key], block, place, (t, c, d_e), cond)

    def relay(key, cond):
        k = c + key[0] * key[1]
        place = lambda: at(k, d_y)
        wires.arrive(y_id[key], place, cond)
        wires.push(f_id[key], place, place, (t, c, d_e), cond)

    spread((0, 0), src, lambda: at(c, d), True)
    yield
    late = [((0, 0), True)]
    for key in STEPS:
        k, cond = reach(c, *key)
        place = lambda k=k: at(k, d)
        wires.arrive(z_id[key], place, cond)
        spread(key, place, place, cond)
        if key[1] > 0:
            for old in late:
                relay(*old)
            late = []
            yield
        late.append((key, cond))
    for old in late:
        relay(*old)
    yield
    for key in [(0, 0)] + STEPS:
        k, cond = (c, True) if key[0] == 0 else reach(c, *key)
        wires.arrive(e_id[key], lambda: at(k, d_e), cond)
        wires.arrive(f_id[key], lambda: at(k, (1 - y) * 2 + 1 - e), cond)
    fetch.wait()


def token_gather(wires, pos, src, at, half):
    t, c, y, e = pos
    d, d_e = y * 2 + e, y * 2 + 1 - e
    z_id = {key: wires.index() for key in STEPS}
    x_id = {key: wires.index() for key in STEPS}
    e_id = {key: wires.index() for key in STEPS}
    f_id = {key: wires.index() for key in STEPS}
    own = wires.index(), wires.index()
    here = wires.index(), wires.index()
    for way in (-1, 1):
        nxt = c - way
        wires.push(
            z_id[(1, way)], lambda: half(t), lambda: at(e, c, t), (t, nxt, d),
            (nxt >= 0) if way > 0 else (nxt <= 3),
        )
    for i in (0, 1):
        wires.push(own[i], lambda i=i: half(i), lambda i=i: at(e, c, i), (t, c, d_e))
    fetch = [wires.fetch(here[i], half(i), at(e, c, i)) for i in (0, 1)]
    yield

    def relay(key, cond):
        k = c + key[0] * key[1]
        place = lambda: at(e, k, 1 - t)
        wires.arrive(x_id[key], place, cond)
        wires.push(f_id[key], place, place, (t, c, d_e), cond)

    late = []
    for key in STEPS:
        k, cond = reach(c, *key)
        place = lambda k=k: at(e, k, t)
        wires.arrive(z_id[key], place, cond)
        s, sign = key
        if s < 3:
            nxt = c - sign
            ok = (nxt >= 0) if sign > 0 else (nxt <= 3)
            wires.push(z_id[(s + 1, sign)], place, place, (t, nxt, d), cond & ok)
        wires.push(x_id[key], place, place, (1 - t, c, d), cond)
        wires.push(e_id[key], place, place, (t, c, d_e), cond)
        if sign > 0:
            for old in late:
                relay(*old)
            late = []
            yield
        late.append((key, cond))
    for old in late:
        relay(*old)
    yield
    for i in (0, 1):
        wires.arrive(own[i], lambda i=i: at(1 - e, c, i))
    for key in STEPS:
        k, cond = reach(c, *key)
        wires.arrive(e_id[key], lambda: at(1 - e, k, t), cond)
        wires.arrive(f_id[key], lambda: at(1 - e, k, 1 - t), cond)
    for copy in fetch:
        copy.wait()


def unit_scatter(wires, pos, piece, place):
    t, c, y, e = pos
    me = c * 2 + e
    first = [wires.index() for _ in range(8)]
    second = [wires.index() for _ in range(8)]
    fetch = wires.fetch(first[0], piece(me), place(c, y * 2 + e))
    for i in range(1, 8):
        q = lax.rem(me + i, 8)
        wires.push(
            first[i], lambda q=q: piece(q), lambda: place(c, y * 2 + e), (t, q // 2, y * 2 + q % 2)
        )
    wires.push(
        second[0], lambda: piece(me), lambda: place(c, y * 2 + e), (t, c, (1 - y) * 2 + e)
    )
    yield
    for i in range(1, 8):
        q = lax.rem(me + 8 - i, 8)
        block = lambda q=q: place(q // 2, y * 2 + q % 2)
        wires.arrive(first[i], block)
        wires.push(second[i], block, block, (t, c, (1 - y) * 2 + e))
        yield
    yield
    for i in range(8):
        q = lax.rem(me + 8 - i, 8)
        wires.arrive(second[i], lambda q=q: place(q // 2, (1 - y) * 2 + q % 2))
    fetch.wait()


def run_all(parts):
    parts = list(parts)
    while parts:
        for part in list(parts):
            try:
                next(part)
            except StopIteration:
                parts.remove(part)


def rows(ref, start, size):
    return ref.at[pl.ds(pl.multiple_of(start, 16), size)]


def dot_nn(a, b):
    return lax.dot_general(a, b, (((1,), (0,)), ((), ())), preferred_element_type=jnp.float32)


def by_rows(count, width, act):
    step = max(16, 32768 // width)
    while count % step:
        step -= 16

    def body(i, carry):
        act(pl.ds(pl.multiple_of(i * step, step), step))
        return carry

    lax.fori_loop(0, count // step, body, 0)


ORDER = (3, 0, 2, 1)


def chain_sum(wires, pos, height, value, keep, came, extra, done):
    t, c, y, e = pos
    d = y * 2 + e
    wide = jnp.float32
    r_id = [wires.index() for _ in range(4)]
    l_id = [wires.index() for _ in range(4)]

    def stage(s):
        for edge, way, blocks, number in (
            (s, 1, range(3, s, -1), r_id), (3 - s, -1, range(0, 3 - s), l_id)
        ):
            here = c == edge
            for k in blocks:

                def act(k=k, number=number):
                    place = keep(k)
                    if s > 0:
                        wires.arrive(number[k], lambda: came.at[k])

                    def add(r):
                        total = value(k, r)
                        if s > 0:
                            total = total + came[k, r].astype(wide)
                        place[r] = total.astype(place.dtype)

                    by_rows(height, extra.shape[-1], add)

                pl.when(here)(act)
                target = extra if way < 0 and k == edge - 1 else came.at[k]
                wires.push(
                    number[k], lambda k=k: keep(k), lambda target=target: target,
                    (t, c + way, d), here,
                )

    def finish():
        for k in range(4):

            def act(k=k):
                if k > 0:
                    wires.arrive(r_id[k], lambda: came.at[k])
                if k < 3:
                    wires.arrive(l_id[k], lambda: extra)

                def add(r):
                    total = value(k, r)
                    if k > 0:
                        total = total + came[k, r].astype(wide)
                    if k < 3:
                        total = total + extra[r].astype(wide)
                    done(r, total)

                by_rows(height, extra.shape[-1], add)

            pl.when(c == k)(act)

    return stage, finish


def token_scatter(wires, pos, part, out, scratch, credit):
    t, c, y, e = pos
    near, own, x_in, came, extra = scratch
    wide = jnp.float32
    tokens, half = x_in.shape[1], x_in.shape[2]
    d_e = y * 2 + 1 - e
    e_id = [wires.index() for _ in range(4)]
    x_id = [wires.index() for _ in range(4)]
    last = wires.index()
    mine = pl.ds(pl.multiple_of(t * half, 128), half)
    other = pl.ds(pl.multiple_of((1 - t) * half, 128), half)

    def begin(k, f):
        return pl.multiple_of((k * 2 + f) * tokens, 16)

    pl.semaphore_wait(credit.at[0], 1)
    for k in ORDER:
        wires.push(
            e_id[k], lambda k=k: part.at[pl.ds(begin(k, 1 - e), tokens)],
            lambda k=k: near.at[k], (t, c, d_e),
        )
    fetch = [
        wires.fetch(wires.index(), part.at[pl.ds(begin(k, e), tokens)], own(k)) for k in range(4)
    ]
    yield
    pl.semaphore_wait(credit.at[1], 1)
    for k in ORDER:
        fetch[k].wait()
        wires.arrive(e_id[k], lambda: near.at[k])

        def away(r):
            total = own(k)[r, other].astype(wide) + near[k, r, other].astype(wide)
            near[k, r, other] = total.astype(near.dtype)

        by_rows(tokens, half, away)
        wires.push(
            x_id[k], lambda k=k: near.at[k, :, other], lambda k=k: x_in.at[k], (1 - t, c, y * 2 + e)
        )
    yield

    def value(k, r):
        return (
            own(k)[r, mine].astype(wide)
            + near[k, r, mine].astype(wide)
            + x_in[k, r].astype(wide)
        )

    def done(r, total):
        out[r, mine] = total.astype(out.dtype)

    stage, finish = chain_sum(
        wires, pos, tokens, value, lambda k: near.at[k, :, mine], came, extra, done
    )
    pl.when(c < 3)(lambda: pl.semaphore_wait(credit.at[2], 1))
    pl.when(c > 0)(lambda: pl.semaphore_wait(credit.at[3], 1))
    for k in ORDER:
        wires.arrive(x_id[k], lambda: x_in.at[k])
    for s in range(3):
        stage(s)
        yield
    finish()
    wires.push(last, lambda: out.at[:, mine], lambda: out.at[:, mine], (1 - t, c, y * 2 + e))
    yield
    wires.arrive(last, lambda: out.at[:, other])


def plane_scatter(wires, pos, out_block, own_block, height, scratch, done, straight=False):
    t, c, y, e = pos
    near, y_in, came, extra = scratch
    wide = jnp.float32
    d_y, d_e = (1 - y) * 2 + e, y * 2 + 1 - e
    e_id = {(k, f): wires.index() for f in range(2) for k in range(4)}
    y_id = [wires.index() for _ in range(4)]
    for f in range(2):
        yy = (1 - y) if f == 0 else y
        for k in ORDER:
            wires.push(
                e_id[k, f], lambda k=k, yy=yy: out_block(k, yy),
                lambda k=k, f=f: near.at[f * 4 + k], (t, c, d_e),
            )
    yield
    for k in ORDER:
        wires.arrive(e_id[k, 0], lambda: near.at[k])
        block = own_block(k, 1 - y)

        def away(r):
            total = block[r].astype(wide) + near[k, r].astype(wide)
            near[k, r] = total.astype(near.dtype)

        by_rows(height, extra.shape[-1], away)
        wires.push(y_id[k], lambda k=k: near.at[k], lambda k=k: y_in.at[k], (t, c, d_y))
        yield

    def block_value(k, r):
        block = own_block(k, y)
        return (
            block[r].astype(wide)
            + near[4 + k, r].astype(wide)
            + y_in[k, r].astype(wide)
        )

    def value(k, r):
        return (
            own_block(k, y)[r].astype(wide)
            + near[4 + k, r].astype(wide)
            + y_in[k, r].astype(wide)
        )

    if straight:
        s_id = [wires.index() for _ in range(4)]
        for far in (3, 1, 2):
            k = lax.rem(c + far, 4)
            wires.arrive(e_id[0, 1] + k, lambda: near.at[4 + k])
            wires.arrive(y_id[0] + k, lambda: y_in.at[k])

            def settle(r):
                near[4 + k, r] = block_value(k, r).astype(near.dtype)

            by_rows(height, extra.shape[-1], settle)
            wires.push(
                s_id[far], lambda k=k: near.at[4 + k], lambda far=far: came.at[far],
                (t, k, y * 2 + e),
            )
            yield
        wires.arrive(e_id[0, 1] + c, lambda: near.at[4 + c])
        wires.arrive(y_id[0] + c, lambda: y_in.at[c])
        for far in (3, 1, 2):
            wires.arrive(s_id[far], lambda: came.at[far])

        def add(r):
            total = block_value(c, r)
            for far in (1, 2, 3):
                total = total + came[far, r].astype(wide)
            done(r, total)

        by_rows(height, extra.shape[-1], add)
        return

    stage, finish = chain_sum(
        wires, pos, height, value, lambda k: near.at[4 + k], came, extra, done
    )
    for k in ORDER:
        wires.arrive(e_id[k, 1], lambda: near.at[4 + k])
        wires.arrive(y_id[k], lambda: y_in.at[k])
    for s in range(3):
        stage(s)
        yield
    finish()


def plane_scratch(shape):
    low = jnp.bfloat16
    return [
        pltpu.VMEM((8,) + shape, low),
        pltpu.VMEM((4,) + shape, low),
        pltpu.VMEM((4,) + shape, low),
        pltpu.VMEM(shape, low),
    ]


def unit_gather(wires, pos, grads, came, y_id, out):
    t, c, y, e = pos
    wide = jnp.float32
    units, lanes = came.shape[2], out.shape[2]
    me = c * 2 + e
    o_id = [wires.index() for _ in range(8)]
    here = pl.ds(pl.multiple_of(me * units, 16), units)
    fetch = []
    for far in (2, 1, 3, 0):
        k = lax.rem(c + far, 4)
        wires.arrive(y_id + k, lambda: came.at[k])
        where = pl.ds(pl.multiple_of((k * 2 + y) * 2 * lanes, 256), 2 * lanes)
        for m in range(3):

            def add(r):
                both = grads[m, r, where].astype(wide) + came[k, m, r].astype(wide)
                grads[m, r, where] = both.astype(grads.dtype)

            by_rows(units, 2 * lanes, add)
        for f in range(2):
            g = e if f == 0 else 1 - e
            src = lambda k=k, g=g: grads.at[
                :, pl.ds(0, units), pl.ds(pl.multiple_of(((k * 2 + y) * 2 + g) * lanes, 128), lanes)
            ]
            if far == 0 and f == 0:
                fetch.append(wires.fetch(wires.index(), src(), out.at[:, here]))
            else:
                wires.push(o_id[far * 2 + f], src, lambda: out.at[:, here], (t, k, y * 2 + g))
        yield
    for far in (1, 2, 3, 0):
        for f in range(2):
            if far == 0 and f == 0:
                continue
            k = lax.rem(c + 4 - far, 4)
            g = e if f == 0 else 1 - e
            wires.arrive(
                o_id[far * 2 + f],
                lambda: out.at[:, pl.ds(pl.multiple_of((k * 2 + g) * units, 16), units)],
            )
    fetch[0].wait()


def swap_halves(x):
    lane = lax.broadcasted_iota(jnp.int32, x.shape, 1)
    ahead, behind = pltpu.roll(x, x.shape[1] - 32, 1), pltpu.roll(x, 32, 1)
    return jnp.where(lax.rem(lane, 64) < 32, ahead, behind)


def head_probs(query, keys, allowed):
    scores = times_transposed(query, keys) * (HEAD_SIZE ** (-0.5))
    scores = jnp.where(allowed, scores, NEGATIVE)
    shifted = jnp.exp(scores - jnp.max(scores, axis=-1, keepdims=True))
    return shifted * (1.0 / jnp.sum(shifted, axis=-1, keepdims=True))


def norm_rows(upstream, inputs, gain):
    rms = lax.rsqrt(jnp.mean(inputs * inputs, axis=-1, keepdims=True) + EPS)
    gain_grad = jnp.sum(upstream * inputs * rms, axis=0, keepdims=True)
    scaled = upstream * gain
    inner = jnp.mean(scaled * inputs, axis=-1, keepdims=True)
    return rms * scaled - inputs * (rms * rms * rms * inner), gain_grad


def advance(parts, count=1):
    for _ in range(count):
        for part in list(parts):
            try:
                next(part)
            except StopIteration:
                parts.remove(part)


def pick(c, table):
    value = table[0]
    for i in range(1, 4):
        value = jnp.where(c == i, table[i], value)
    return value


NEAREST = ((0, 1, 2, 3), (1, 0, 2, 3), (2, 3, 1, 0), (3, 2, 1, 0))


def layer_kernel(
    lengths, states, gains, qkv, out_w, w3, gy, cosine, sine,
    layer_out, grad_states, g3_out, gq_out, go_out, gain_out, qkv_kept, part_b,
    send, recv, credit, qkv_all, out_all, gain_all, hidden, normed_one, q_rot, kv_all, mixed, gn_own,
    w3_all, gy_all, nt_all, act_t, part_g, stage_b, unit_in, kv_own, pair_out, pair_in, nt,
    near, x_in, came, grad_hidden, grad_low, branch, mixed_t, grad_mixed, gqkv, normed_t, gq_part,
    dk, dv, kv_part, kv_in, gains_sum, gain_in, *scratch,
):
    pos = position()
    t, c, y, e = pos
    low, wide = jnp.bfloat16, jnp.float32
    wires = Wires(send, recv)
    d = y * 2 + e
    me = c * 4 + d
    here, beside, over = (t, c, d), (t, c, y * 2 + 1 - e), (1 - t, c, d)
    peers = [(True, over)]
    for i in range(1, 16):
        q = lax.rem(me + i, 16)
        peers.append((True, (t, q // 4, lax.rem(q, 4))))
    greet(peers)
    tokens, width = states.shape
    half = width // 2
    block, n_all = qkv.shape
    n_query = q_rot.shape[1]
    n_key = (n_all - n_query) // 2
    lanes = out_w.shape[1]
    units = unit_in.shape[2]
    scaled = grad_hidden

    def lane_block(q, size=lanes):
        return pl.ds(pl.multiple_of(q * size, 128), size)

    gain_id = [wires.index() for _ in range(16)]
    for i in range(1, 16):
        q = lax.rem(me + i, 16)
        wires.push(
            gain_id[i], lambda: gains, lambda: gain_all.at[:, lane_block(me)],
            (t, q // 4, lax.rem(q, 4)),
        )
    fetch_gain = wires.fetch(wires.index(), gains, gain_all.at[:, lane_block(me)])
    g_qkv = [
        plane_gather(wires, pos, lambda: qkv, lambda k, f: rows(qkv_all, (k * 4 + f) * block, block))
    ]
    g_out = [
        plane_gather(
            wires, pos, lambda: out_w, lambda k, f: out_all.at[:, lane_block(k * 4 + f)]
        )
    ]
    g_unit = [
        unit_scatter(
            wires, pos,
            lambda q: w3.at[:, pl.ds(pl.multiple_of(q * units, 16), units)],
            lambda k, f: w3_all.at[:, pl.ds(0, units), lane_block(k * 4 + f)],
        )
    ]

    def spot(ref):
        return lambda f, k, h: ref.at[
            pl.ds(pl.multiple_of((k * 2 + f) * tokens, 16), tokens), lane_block(h, half)
        ]

    g_gy = [token_gather(wires, pos, None, spot(gy_all), lambda h: gy.at[:, lane_block(h, half)])]
    advance(g_qkv)
    advance(g_gy)
    w3_all[:, units:, :] = jnp.zeros_like(w3_all[:, units:, :])

    def scale_rows(r):
        x = states[r].astype(wide)
        scaled[r] = x * lax.rsqrt(jnp.mean(x * x, axis=-1, keepdims=True) + EPS)

    by_rows(tokens, width, scale_rows)
    advance(g_qkv)
    advance(g_out)
    advance(g_gy)
    advance(g_qkv)
    advance(g_out)
    advance(g_gy)
    advance(g_qkv)
    advance(g_out)
    advance(g_gy)
    while g_qkv:
        advance(g_qkv)
    fetch_gain.wait()
    for i in range(1, 16):
        q = lax.rem(me + 16 - i, 16)
        wires.arrive(gain_id[i], lambda: gain_all.at[:, lane_block(q)])
    gain_one = gain_all[...].astype(wide)[0:1]
    gain_two = gain_all[...].astype(wide)[1:2]

    save_qkv = wires.fetch(wires.index(), qkv_all, qkv_kept)

    def norm_one(r):
        normed_one[r] = (scaled[r] * gain_one).astype(low)

    by_rows(tokens, width, norm_one)

    def turned(x):
        return x * cosine[...] + swap_halves(x) * sine[...]

    tail = dot_nn(normed_one[...], qkv_all[:, n_query:])
    kv_own[:, :n_key] = turned(tail[:, :n_key]).astype(low)
    kv_own[:, n_key:] = tail[:, n_key:].astype(low)
    kv_all[pl.ds(pl.multiple_of(c * tokens, 16), tokens)] = kv_own[...]
    kv_id = [wires.index() for _ in range(3)]
    for i in range(3):
        k = lax.rem(c + i + 1, 4)
        wires.push(kv_id[i], lambda: kv_own, lambda: rows(kv_all, c * tokens, tokens), (t, k, d))
    advance(g_unit)

    def project(j, carry):
        where = pl.ds(pl.multiple_of(j * 256, 256), 256)
        two = dot_nn(normed_one[...], qkv_all[:, where])
        for h in range(2):
            slab = pl.ds(pl.multiple_of(j * 256 + h * 128, 128), 128)
            q_rot[:, slab] = turned(two[:, h * 128 : (h + 1) * 128]).astype(low)
        return carry

    lax.fori_loop(0, n_query // 256, project, 0)
    advance(g_out)
    for i in range(3):
        k = lax.rem(c + 3 - i, 4)
        wires.arrive(kv_id[i], lambda: rows(kv_all, k * tokens, tokens))
    q_pos = c * tokens + lax.broadcasted_iota(jnp.int32, (tokens, kv_all.shape[0]), 0)
    k_pos = lax.broadcasted_iota(jnp.int32, (tokens, kv_all.shape[0]), 1)
    allowed = (k_pos <= q_pos) & (k_pos < lengths[0])
    pairs = n_query // 256
    for g in range(2):
        keys = kv_all[:, g * HEAD_SIZE : (g + 1) * HEAD_SIZE]
        values = kv_all[:, n_key + g * HEAD_SIZE : n_key + (g + 1) * HEAD_SIZE]

        def pair(j, carry, g=g, keys=keys, values=values):
            slab = pl.ds(pl.multiple_of((g * pairs + j) * 128, 128), 128)
            q_two = q_rot[:, slab]
            both_heads = []
            for h in range(2):
                probs = head_probs(q_two[:, h * HEAD_SIZE : (h + 1) * HEAD_SIZE], keys, allowed)
                both_heads.append(dot_nn(probs.astype(low), values))
            mixed[:, slab] = jnp.concatenate(both_heads, axis=1).astype(low)
            return carry

        lax.fori_loop(0, pairs, pair, 0)
        if g == 0:
            advance(g_out)
    while g_out:
        advance(g_out)
    advance(g_unit)
    pair_id = [wires.index() for _ in range(4)]
    for i in range(4):
        for j in range(2):
            where = pl.ds(i * (width // 4) + j * (width // 8), width // 8)
            pair_out[:, where] = dot_nn(mixed[...], out_all[:, where]).astype(low)
        piece = pl.ds(i * (width // 4), width // 4)
        wires.push(pair_id[i], lambda p=piece: pair_out.at[:, p], lambda p=piece: pair_in.at[:, p], over)
    advance(g_unit, 2)
    for i in range(4):
        piece = pl.ds(i * (width // 4), width // 4)
        wires.arrive(pair_id[i], lambda: pair_in.at[:, piece])

    def norm_two(r):
        total = states[r].astype(wide) + (pair_out[r].astype(wide) + pair_in[r].astype(wide))
        hidden[r] = total
        factor = lax.rsqrt(jnp.mean(total * total, axis=-1, keepdims=True) + EPS)
        nt[r] = (total * factor * gain_two).astype(low)

    by_rows(tokens, width, norm_two)

    gathers = []
    for source, target in ((nt, nt_all),):
        at = spot(target)
        z_id, x_id, e_id, f_id = [[wires.index() for _ in range(4)][0] for _ in range(4)]
        gathers.append((at, z_id, x_id, e_id, f_id))
        own_half = lambda h, source=source: source.at[:, lane_block(h, half)]
        for i in (3, 1, 2):
            k = lax.rem(c + i, 4)
            wires.push(
                wires.index(), lambda own=own_half: own(t), lambda at=at: at(e, c, t), (t, k, d),
                lands=z_id + c,
            )
        wires.push(e_id + c, lambda own=own_half: own(t), lambda at=at: at(e, c, t), beside)
        wires.push(f_id + c, lambda own=own_half: own(1 - t), lambda at=at: at(e, c, 1 - t), beside)
    at_home = pl.ds(pl.multiple_of((c * 2 + e) * tokens, 16), tokens)
    nt_all[at_home] = nt[...]
    advance(g_unit, 4)
    while g_gy:
        advance(g_gy)

    def nearest(j):
        return pick(c, [sum_of(j, NEAREST[i]) for i in range(4)])

    def sum_of(j, order):
        value = order[0]
        for i in range(1, 4):
            value = jnp.where(j == i, order[i], value)
        return value

    def stage_one(j):
        k = nearest(j)
        for at, z_id, x_id, e_id, f_id in gathers:
            wires.arrive(z_id + k, lambda: at(e, k, t))
            wires.copy(x_id + k, at(e, k, t), at(e, k, t), over).start()
            wires.copy(e_id + k, at(e, k, t), at(e, k, t), beside).start()

    def stage_two(j):
        k = nearest(j)
        for at, z_id, x_id, e_id, f_id in gathers:

            def act():
                wires.arrive(x_id + k, lambda: at(e, k, 1 - t))
                wires.copy(f_id + k, at(e, k, 1 - t), at(e, k, 1 - t), beside).start()

            pl.when(j > 0)(act)
        for at, z_id, x_id, e_id, f_id in gathers:
            wires.arrive(e_id + k, lambda: at(1 - e, k, t))
            wires.arrive(f_id + k, lambda: at(1 - e, k, 1 - t))

    n_id = [wires.index() for _ in range(4)][0]
    r_id = [wires.index() for _ in range(4)][0]

    def part_rows(k, f):
        return part_g.at[pl.ds(pl.multiple_of((k * 2 + f) * tokens, 16), tokens)]

    mine, other = lane_block(t, half), lane_block(1 - t, half)

    def stage_three(j):
        k = nearest(j)
        wires.arrive(n_id + k, lambda: near.at[k])
        ours = part_rows(k, e)

        def away(r):
            total = ours[r, other].astype(wide) + near[k, r, other].astype(wide)
            near[k, r, other] = total.astype(low)

        by_rows(tokens, half, away)
        wires.copy(r_id + k, near.at[k, :, other], x_in.at[k], over).start()

    def kept(k, r):
        return (
            part_rows(k, e)[r, mine].astype(wide)
            + near[k, r, mine].astype(wide)
            + x_in[k, r].astype(wide)
        )

    s_id = [wires.index() for _ in range(4)][0]

    def stage_four(j):
        k = nearest(j)
        wires.arrive(r_id + k, lambda: x_in.at[k])

        def add(r):
            near[k, r, mine] = kept(k, r).astype(low)

        by_rows(tokens, half, add)
        i = lax.rem(k - c + 4, 4)
        wires.copy(s_id + i, near.at[k, :, mine], came.at[i - 1], (t, k, d)).start()

    padded = act_t.shape[0]
    act = qkv_all.at[pl.ds(0, tokens * 8), pl.ds(0, padded)]
    both = qkv_all.at[pl.ds(0, tokens * 8), pl.ds(padded, 2 * padded)]
    both_t = qkv_all.at[pl.ds(tokens * 8, 2 * padded), pl.ds(0, tokens * 8)]
    b_id = wires.index()

    def stored(k):
        where = pl.ds(pl.multiple_of(k * 2 * tokens, 16), 2 * tokens)
        return pltpu.make_async_copy(stage_b, part_b.at[where], wires.recv.at[b_id])

    def swiglu(j, carry):
        stage_two(j)
        k = nearest(j)
        where = pl.ds(pl.multiple_of(k * 2 * tokens, 16), 2 * tokens)
        x = nt_all[where]
        gate = times_transposed(x, w3_all[0])
        up = times_transposed(x, w3_all[1])
        grad_act = times_transposed(gy_all[where], w3_all[2])
        sigma = jax.nn.sigmoid(gate)
        swish = gate * sigma
        act[where] = (swish * up).astype(low)
        wide_units = gate.shape[1]
        both[where, :wide_units] = (
            grad_act * up * (sigma * (1.0 + gate * (1.0 - sigma)))
        ).astype(low)
        both[where, wide_units:] = (grad_act * swish).astype(low)
        for i in range(4):
            piece = slice(i * (width // 4), (i + 1) * (width // 4))
            part_g[where, piece] = (
                dot_nn(both[where, :wide_units], w3_all[0, :, piece])
                + dot_nn(both[where, wide_units:], w3_all[1, :, piece])
            ).astype(low)
        wires.copy(n_id + k, part_rows(k, 1 - e), near.at[k], beside).start()
        pl.when(j > 0)(lambda: stored(0).wait())
        for i in range(4):
            piece = slice(i * (width // 4), (i + 1) * (width // 4))
            stage_b[:, piece] = dot_nn(act[where], w3_all[2, :, piece]).astype(low)
        stored(k).start()
        pl.when(j > 0)(lambda: stage_three(j - 1))
        pl.when(j > 2)(lambda: stage_four(j - 2))
        return carry

    for j in range(1, 4):
        stage_one(j)
    while g_unit:
        advance(g_unit)
    save_qkv.wait()
    wires.drain()
    lax.fori_loop(0, 4, swiglu, 0)
    stored(0).wait()
    stage_three(3)
    for k in range(4):
        away = c != k
        for at, z_id, x_id, e_id, f_id in gathers:
            half_at = lambda h, k=k, at=at: at(e, k, h)
            wires.owe(x_id + k, lambda f=half_at: f(t), away)
            wires.owe(e_id + k, lambda f=half_at: f(t), away)
            wires.owe(f_id + k, lambda f=half_at: f(1 - t), away)
        wires.owe(n_id + k, lambda k=k: part_rows(k, 1 - e))
        wires.owe(r_id + k, lambda k=k: near.at[k, :, other])
    for i in (1, 2, 3):
        k = lax.rem(c + i, 4)
        wires.owe(s_id + i, lambda k=k: near.at[k, :, mine])
    stage_four(2)
    act_t[...] = act[...].T
    both_t[...] = both[...].T

    def unit_grads(k, yy):
        where = lane_block(k * 2 + yy, 256)
        two = dot_nn(both_t[...], nt_all[:, where]).astype(low)
        w3_all[0, :units, where] = two[:units]
        w3_all[1, :units, where] = two[padded : padded + units]
        w3_all[2, :units, where] = dot_nn(act_t[...], gy_all[:, where]).astype(low)[:units]

    u_id = [wires.index() for _ in range(4)][0]
    across = (t, c, (1 - y) * 2 + e)

    def half_grads(k):
        return w3_all.at[:, pl.ds(0, units), lane_block(k * 2 + 1 - y, 256)]

    def send_units(j, carry):
        k = lax.rem(c + pick(j, (2, 1, 3, 0)), 4)
        unit_grads(k, 1 - y)
        wires.copy(u_id + k, half_grads(k), unit_in.at[k], across).start()
        return carry

    lax.fori_loop(0, 2, send_units, 0)
    stage_four(3)
    lax.fori_loop(2, 4, send_units, 0)

    def keep_units(j, carry):
        unit_grads(lax.rem(c + pick(j, (2, 1, 3, 0)), 4), y)
        return carry

    lax.fori_loop(0, 2, keep_units, 0)
    g_unit = [unit_gather(wires, pos, w3_all, unit_in, u_id, g3_out)]
    owed, bulk = wires.sent, []
    wires.sent = bulk
    advance(g_unit)
    wires.sent = owed
    wires.arrive(r_id + c, lambda: x_in.at[c])
    for i in (3, 1, 2):
        wires.arrive(s_id + i, lambda: came.at[i - 1])

    def done(r):
        total = kept(c, r)
        for i in range(3):
            total = total + came[i, r].astype(wide)
        gn_own[r, mine] = total.astype(low)

    by_rows(tokens, half, done)
    last = wires.index()
    wires.push(last, lambda: gn_own.at[:, mine], lambda: gn_own.at[:, mine], over)
    lax.fori_loop(2, 4, keep_units, 0)
    wires.sent = bulk
    advance(g_unit)
    wires.sent = owed
    wires.arrive(last, lambda: gn_own.at[:, other])
    wires.sent = owed
    wires.drain()
    wires.sent = bulk
    for k in range(4):
        wires.owe(u_id + k, lambda k=k: half_grads(k))
    for i, cond, device in (
        (0, True, beside), (1, True, over), (2, c > 0, (t, c - 1, d)), (3, c < 3, (t, c + 1, d))
    ):
        only(
            cond,
            functools.partial(
                pl.semaphore_signal, credit.at[i], inc=1, device_id=device, device_id_type=MESH
            ),
        )
    load_qkv = wires.fetch(wires.index(), qkv_kept, qkv_all)
    s_q, s_k, s_o = scratch[:4], scratch[4:8], scratch[8:12]
    t_b = (
        near, lambda k: part_g.at[pl.ds(k * tokens, tokens)], x_in, came.at[pl.ds(0, 4)], came.at[4]
    )
    second = [token_scatter(wires, pos, part_b, branch, t_b, credit)]
    advance(second)
    mixed_t[...] = mixed[...].T
    normed_t[...] = normed_one[...].T
    gains_sum[...] = jnp.zeros_like(gains_sum)

    def norm_two_back(r):
        value, grad = norm_rows(gn_own[r].astype(wide), hidden[r], gain_two)
        home = pl.ds(pl.multiple_of((c * 2 + e) * tokens + r.start, 16), 16)
        total = gy_all[home].astype(wide) + value
        grad_hidden[r] = total
        grad_low[r] = total.astype(low)
        gains_sum[1:2] += grad

    by_rows(tokens, width, norm_two_back)
    advance(second)

    def out_grad(j, carry):
        where = pl.ds(pl.multiple_of(j * 2 * lanes, 256), 2 * lanes)
        nt_all[:, where] = dot_nn(mixed_t[...], grad_low[:, where]).astype(low)
        return carry

    lax.fori_loop(0, 8, out_grad, 0)
    outs = [
        plane_scatter(
            wires, pos,
            lambda k, yy: nt_all.at[:, lane_block(k * 4 + yy * 2 + 1 - e)],
            lambda k, yy: nt_all.at[:, lane_block(k * 4 + yy * 2 + e)],
            n_query, s_o, lambda r, v: go_out.__setitem__(r, v),
        )
    ]
    advance(outs)

    def mix_grad(j, carry):
        where = pl.ds(pl.multiple_of(j * 256, 256), 256)
        grad_mixed[:, where] = times_transposed(grad_low[...], out_all[where, :]).astype(low)
        return carry

    lax.fori_loop(0, n_query // 256, mix_grad, 0)
    advance(outs, 4)
    advance(g_unit)

    scale = HEAD_SIZE ** (-0.5)
    pairs = n_query // 256
    for g in range(2):
        keys = kv_all[:, g * HEAD_SIZE : (g + 1) * HEAD_SIZE]
        values = kv_all[:, n_key + g * HEAD_SIZE : n_key + (g + 1) * HEAD_SIZE]
        dk[...] = jnp.zeros_like(dk)
        dv[...] = jnp.zeros_like(dv)

        def pair(j, carry, g=g, keys=keys, values=values):
            slab = pl.ds(pl.multiple_of((g * pairs + j) * 128, 128), 128)
            q_two, m_two = q_rot[:, slab], grad_mixed[:, slab]
            both = []
            for h in range(2):
                query = q_two[:, h * HEAD_SIZE : (h + 1) * HEAD_SIZE]
                upstream = m_two[:, h * HEAD_SIZE : (h + 1) * HEAD_SIZE]
                probs = head_probs(query, keys, allowed)
                dprob = times_transposed(upstream, values)
                delta = jnp.sum(probs * dprob, axis=-1, keepdims=True)
                grad_scores = (probs * (dprob - delta)).astype(low)
                both.append(dot_nn(grad_scores, keys))
                dk[...] += transposed_times(grad_scores, query)
                dv[...] += transposed_times(probs.astype(low), upstream)
            grads = jnp.concatenate(both, axis=1) * scale
            back = grads * cosine[...] - swap_halves(grads) * sine[...]
            gqkv[:, slab] = back.astype(low)
            return carry

        lax.fori_loop(0, pairs, pair, 0)
        for k in range(4):
            block = slice(k * tokens, (k + 1) * tokens)
            kv_part[k, :, g * HEAD_SIZE : (g + 1) * HEAD_SIZE] = (dk[block] * scale).astype(low)
            kv_part[k, :, n_key + g * HEAD_SIZE : n_key + (g + 1) * HEAD_SIZE] = dv[block].astype(low)
    kvg_id = [wires.index() for _ in range(3)]
    for i in range(3):
        k = lax.rem(c + i + 1, 4)
        wires.push(kvg_id[i], lambda k=k: kv_part.at[k], lambda i=i: kv_in.at[i], (t, k, d))

    def q_block(place, i, where):
        return place.at[pl.ds(pl.multiple_of(i * lanes, 16), lanes), where]

    def q_grad(core, place, where):
        def step(i, carry):
            here = lane_block(i * 2 + core)
            q_block(place, i, where)[...] = dot_nn(normed_t[here, :], gqkv[:, where]).astype(low)
            return carry

        lax.fori_loop(0, 8, step, 0)

    def q_sums(where, scratches):
        def done(r, value):
            gq_out[r, where] = value

        return plane_scatter(
            wires, pos,
            lambda k, yy: q_block(gy_all, k * 2 + yy, where),
            lambda k, yy: q_block(gq_part, k * 2 + yy, where),
            gq_out.shape[0], scratches, done,
        )

    first, rest = slice(0, n_query), slice(n_query, n_query + 2 * n_key)
    q_grad(1 - e, gy_all, first)
    queries = [q_sums(first, s_q)]
    advance(queries)
    q_grad(e, gq_part, first)
    advance(queries, 4)
    advance(second)
    advance(g_unit)
    total = kv_part[c].astype(wide)
    for i in range(3):
        wires.arrive(kvg_id[i], lambda: kv_in.at[i])
        total = total + kv_in[i].astype(wide)
    key_grads = total[:, :n_key]
    key_grads = key_grads * cosine[...] - swap_halves(key_grads) * sine[...]
    gqkv[:, n_query : n_query + n_key] = key_grads.astype(low)
    gqkv[:, n_query + n_key :] = total[:, n_key:].astype(low)
    q_grad(1 - e, gy_all, rest)
    others = [q_sums(rest, s_k)]
    advance(others)
    q_grad(e, gq_part, rest)
    load_qkv.wait()

    def normed_grad(j, carry):
        where = pl.ds(pl.multiple_of(j * 256, 256), 256)
        pair_out[:, where] = times_transposed(gqkv[...], qkv_all[where, :]).astype(low)
        return carry

    lax.fori_loop(0, width // 256, normed_grad, 0)
    p_id = wires.index()
    wires.push(p_id, lambda: pair_out, lambda: pair_in, (1 - t, c, d))
    advance(others, 4)
    advance(second)
    advance(outs)
    advance(second)
    wires.arrive(p_id, lambda: pair_in)

    def norm_one_back(r):
        upstream = pair_out[r].astype(wide) + pair_in[r].astype(wide)
        value, grad = norm_rows(upstream, states[r].astype(wide), gain_one)
        grad_states[r] = grad_hidden[r] + value
        gains_sum[0:1] += grad

    by_rows(tokens, width, norm_one_back)
    g_id = [wires.index() for _ in range(16)]

    def gain_block(q):
        return gains_sum.at[:, pl.ds(pl.multiple_of(q * lanes, 128), lanes)]

    for i in range(1, 16):
        q = lax.rem(me + i, 16)
        wires.push(
            g_id[i], lambda q=q: gain_block(q), lambda i=i: gain_in.at[i],
            (t, q // 4, lax.rem(q, 4)),
        )
    advance(outs)
    advance(second)
    advance(others)
    advance(outs)
    advance(queries)
    advance(others)
    advance(outs)
    advance(queries)
    advance(others)
    advance(queries)
    advance(others)
    advance(queries)
    advance(second)
    while g_unit:
        advance(g_unit)

    def finish(r):
        layer_out[r] = (hidden[r] + branch[r].astype(wide)).astype(low)

    by_rows(tokens, width, finish)
    gain = gains_sum[:, pl.ds(pl.multiple_of(me * lanes, 128), lanes)]
    for i in range(1, 16):
        wires.arrive(g_id[i], lambda: gain_in.at[i])
        gain = gain + gain_in[i]
    gain_out[...] = gain
    wires.drain()


def layer_call(lengths, states, gains, qkv, out_w, w3, gy, cosine, sine):
    shape = jax.ShapeDtypeStruct
    low, wide = jnp.bfloat16, jnp.float32
    tokens, width = states.shape
    n_query, lanes = out_w.shape
    n_all = qkv.shape[1]
    n_rest = n_all - n_query
    units = w3.shape[1] // 8
    padded = -(-units // 128) * 128
    all_tokens, keys = tokens * 8, tokens * 4
    half = width // 2
    vm = pltpu.VMEM
    return pl.pallas_call(
        layer_kernel,
        name="layer",
        out_shape=(
            shape((tokens, width), low),
            shape((tokens, width), wide),
            shape((3, units * 8, lanes), low),
            shape((lanes, n_all), wide),
            shape((n_query, lanes), wide),
            shape((8, lanes), wide),
            shape((width, n_all), low),
            shape((all_tokens, width), low),
        ),
        in_specs=[pl.BlockSpec(memory_space=pltpu.MemorySpace.SMEM), pl.BlockSpec(memory_space=VMEM)]
        + [pl.BlockSpec(memory_space=HBM)] * 5
        + [pl.BlockSpec(memory_space=VMEM)] * 2,
        out_specs=[
            pl.BlockSpec(memory_space=VMEM),
            pl.BlockSpec(memory_space=VMEM),
            pl.BlockSpec(memory_space=HBM),
            pl.BlockSpec(memory_space=VMEM),
            pl.BlockSpec(memory_space=VMEM),
            pl.BlockSpec(memory_space=VMEM),
            pl.BlockSpec(memory_space=HBM),
            pl.BlockSpec(memory_space=HBM),
        ],
        scratch_shapes=[
            pltpu.SemaphoreType.DMA((320,)),
            pltpu.SemaphoreType.DMA((320,)),
            pltpu.SemaphoreType.REGULAR((4,)),
            vm((width, n_all), low),
            vm((n_query, width), low),
            vm((16, width), low),
            vm((tokens, width), wide),
            vm((tokens, width), low),
            vm((tokens, n_query), low),
            vm((keys, n_rest), low),
            vm((tokens, n_query), low),
            vm((tokens, width), low),
            vm((3, padded, width), low),
            vm((all_tokens, width), low),
            vm((all_tokens, width), low),
            vm((padded, all_tokens), low),
            vm((all_tokens, width), low),
            vm((2 * tokens, width), low),
            vm((4, 3, units, width // 8), low),
            vm((tokens, n_rest), low),
            vm((tokens, width), low),
            vm((tokens, width), low),
            vm((tokens, width), low),
            vm((4, tokens, width), low),
            vm((4, tokens, half), low),
            vm((5, tokens, half), low),
            vm((tokens, width), wide),
            vm((tokens, width), low),
            vm((tokens, width), low),
            vm((n_query, tokens), low),
            vm((tokens, n_query), low),
            vm((tokens, n_all), low),
            vm((width, tokens), low),
            vm((8 * lanes, n_all), low),
            vm((keys, HEAD_SIZE), wide),
            vm((keys, HEAD_SIZE), wide),
            vm((4, tokens, n_rest), low),
            vm((3, tokens, n_rest), low),
            vm((8, width), wide),
            vm((16, 8, lanes), wide),
        ]
        + plane_scratch((lanes, n_query))
        + plane_scratch((lanes, n_rest))
        + plane_scratch((n_query, lanes)),
        compiler_params=pltpu.CompilerParams(
            collective_id=1, has_side_effects=True, vmem_limit_bytes=63 << 20
        ),
    )(lengths, states, gains, qkv, out_w, w3, gy, cosine, sine)


def plane_shards(
    states, lengths, first_gain, w_query, key_matrix, value_matrix, w_out, second_gain,
    w_gate, w_up, w_down, cotangent,
):
    low, wide = jnp.bfloat16, jnp.float32
    tokens = states.shape[1]
    positions = lax.axis_index("ctx") * tokens + jnp.arange(tokens, dtype=jnp.int32)
    cosine, sine = rope_tables(positions, HEAD_SIZE // 2)
    lane = jnp.arange(2 * HEAD_SIZE)
    turn = jnp.where((lane % HEAD_SIZE) < HEAD_SIZE // 2, -1.0, 1.0)
    cosine = jnp.tile(cosine[:, 0], (1, 4))
    sine = jnp.tile(sine[:, 0], (1, 4)) * turn[None, :]
    valid = (positions < lengths[0])[:, None]
    grad_y = jnp.where(valid, cotangent[0], jnp.zeros((), low))
    n_query, n_key = w_query.shape[1], key_matrix.shape[1]
    lanes = w_out.shape[1]
    qkv = jnp.concatenate([w_query, key_matrix, value_matrix], axis=1)
    gains = jnp.concatenate(
        [first_gain[None], second_gain[None], jnp.zeros((14, lanes), low)], axis=0
    )
    w3 = jnp.stack([w_gate.T, w_up.T, w_down])
    layer_out, grad_states, g3, gq, go, gain, _, _ = layer_call(
        lengths, states[0], gains, qkv, w_out, w3, grad_y, cosine, sine
    )
    return (
        layer_out[None],
        grad_states[None],
        gain[0],
        gq[:, :n_query],
        gq[:, n_query : n_query + n_key],
        gq[:, n_query + n_key :],
        go,
        gain[1],
        g3[0].T.astype(wide),
        g3[1].T.astype(wide),
        g3[2].astype(wide),
    )


def fits(mesh):
    return dict(mesh.shape) == {"tensor": 2, "ctx": 4, "dp": 4}


def solution(mesh):
    placed = (
        P("dp", "ctx", None),
        P("dp"),
        P(("ctx", "dp")),
        P(("ctx", "dp"), "tensor"),
        P(("ctx", "dp"), "tensor"),
        P(("ctx", "dp"), "tensor"),
        P("tensor", ("ctx", "dp")),
        P(("ctx", "dp")),
        P(("ctx", "dp"), "tensor"),
        P(("ctx", "dp"), "tensor"),
        P("tensor", ("ctx", "dp")),
        P("dp", "ctx", None),
    )
    return jax.shard_map(
        plane_shards if fits(mesh) else shards,
        mesh=mesh,
        in_specs=placed,
        out_specs=(
            P("dp", "ctx", None),
            P("dp", "ctx", None),
            P(("ctx", "dp")),
            P(("ctx", "dp"), "tensor"),
            P(("ctx", "dp"), "tensor"),
            P(("ctx", "dp"), "tensor"),
            P("tensor", ("ctx", "dp")),
            P(("ctx", "dp")),
            P(("ctx", "dp"), "tensor"),
            P(("ctx", "dp"), "tensor"),
            P("tensor", ("ctx", "dp")),
        ),
        check_vma=False,
    )
```

```python
import functools

import jax
import jax.numpy as jnp
from jax import lax
from jax.experimental import pallas as pl
from jax.experimental.pallas import tpu as pltpu
from jax.sharding import PartitionSpec as P

HEAD_SIZE = 64


EPS = 1e-05
THETA = 10000.0
NEGATIVE = -1e30


def rope_tables(positions, half_width):
    inverse = jnp.exp(-jnp.log(THETA) * jnp.arange(half_width).astype(jnp.float32) / half_width)
    angles = positions.astype(jnp.float32)[:, None] * inverse[None, :]
    return (jnp.cos(angles)[:, None, :], jnp.sin(angles)[:, None, :])


def apply_rotation(vectors, cosine_table, sine_table):
    half_width = vectors.shape[-1] // 2
    first_half = vectors[..., :half_width]
    second_half = vectors[..., half_width:]
    return jnp.concatenate(
        [
            first_half * cosine_table - second_half * sine_table,
            second_half * cosine_table + first_half * sine_table,
        ],
        axis=-1,
    )


def rotate_back(grads, cosine_table, sine_table):
    half_width = grads.shape[-1] // 2
    first_half = grads[..., :half_width]
    second_half = grads[..., half_width:]
    return jnp.concatenate(
        [
            first_half * cosine_table + second_half * sine_table,
            second_half * cosine_table - first_half * sine_table,
        ],
        axis=-1,
    )


def times_transposed(left, right):
    return lax.dot_general(
        left, right, (((1,), (1,)), ((), ())), preferred_element_type=jnp.float32
    )


def transposed_times(left, right):
    return lax.dot_general(
        left, right, (((0,), (0,)), ((), ())), preferred_element_type=jnp.float32
    )


def norm_back(upstream, inputs, inverse_rms, gain):
    scaled = upstream * gain
    gain_grad = jnp.sum(upstream * inputs * inverse_rms, axis=0)
    inner = jnp.mean(scaled * inputs, axis=-1, keepdims=True)
    return (inverse_rms * scaled - inputs * inverse_rms**3 * inner, gain_grad)


def shards(
    states,
    lengths,
    first_gain,
    w_query,
    key_matrix,
    value_matrix,
    w_out,
    second_gain,
    w_gate,
    w_up,
    w_down,
    cotangent,
):
    low_type = jnp.bfloat16
    wide_type = jnp.float32
    gathered = (
        lax.all_gather(first_gain, ("ctx", "dp"), axis=0, tiled=True),
        lax.all_gather(w_query, ("ctx", "dp"), axis=0, tiled=True),
        lax.all_gather(key_matrix, ("ctx", "dp"), axis=0, tiled=True),
        lax.all_gather(value_matrix, ("ctx", "dp"), axis=0, tiled=True),
        lax.all_gather(w_out, ("ctx", "dp"), axis=1, tiled=True),
        lax.all_gather(second_gain, ("ctx", "dp"), axis=0, tiled=True),
        lax.all_gather(w_gate, ("ctx", "dp"), axis=0, tiled=True),
        lax.all_gather(w_up, ("ctx", "dp"), axis=0, tiled=True),
        lax.all_gather(w_down, ("ctx", "dp"), axis=1, tiled=True),
    )
    (
        gain_one,
        full_query,
        full_key,
        full_value,
        full_out,
        gain_two,
        full_gate,
        full_up,
        full_down,
    ) = gathered
    gain_one = gain_one.astype(wide_type)
    gain_two = gain_two.astype(wide_type)
    tokens = states.shape[1]
    inputs = states[0].astype(wide_type)
    seq_length = lengths[0]
    first_pos = lax.axis_index("ctx") * tokens
    positions = first_pos + jnp.arange(tokens, dtype=jnp.int32)
    cosine_table, sine_table = rope_tables(positions, HEAD_SIZE // 2)
    heads = full_query.shape[1] // HEAD_SIZE
    kv_heads = full_key.shape[1] // HEAD_SIZE
    group_factor = heads // kv_heads
    scale = HEAD_SIZE ** (-0.5)
    rms_one = lax.rsqrt(jnp.mean(inputs * inputs, axis=-1, keepdims=True) + EPS)
    first_normed = (inputs * rms_one * gain_one).astype(low_type)
    query_rows = jnp.dot(first_normed, full_query, preferred_element_type=wide_type)
    fresh_keys = jnp.dot(first_normed, full_key, preferred_element_type=wide_type)
    values_new = jnp.dot(first_normed, full_value, preferred_element_type=wide_type)
    query_rotated = (
        apply_rotation(query_rows.reshape(tokens, heads, HEAD_SIZE), cosine_table, sine_table)
        .astype(low_type)
        .reshape(tokens, kv_heads, group_factor, HEAD_SIZE)
    )
    key_rot = (
        apply_rotation(fresh_keys.reshape(tokens, kv_heads, HEAD_SIZE), cosine_table, sine_table)
        .astype(low_type)
        .reshape(tokens, kv_heads * HEAD_SIZE)
    )
    value_lower = values_new.astype(low_type)
    keys_all, values_all = (
        lax.all_gather(key_rot, "ctx", axis=0, tiled=True),
        lax.all_gather(value_lower, "ctx", axis=0, tiled=True),
    )
    total_keys = keys_all.shape[0]
    key_block = min(512, total_keys)
    block_count = total_keys // key_block

    def block_scores(begin_at):
        key_piece = lax.dynamic_slice_in_dim(keys_all, begin_at, key_block, 0).reshape(
            key_block, kv_heads, HEAD_SIZE
        )
        value_piece = lax.dynamic_slice_in_dim(values_all, begin_at, key_block, 0).reshape(
            key_block, kv_heads, HEAD_SIZE
        )
        scores = (
            jnp.einsum("qkgd,pkd->kgqp", query_rotated, key_piece, preferred_element_type=wide_type)
            * scale
        )
        key_pos = begin_at + jnp.arange(key_block, dtype=jnp.int32)
        allowed = (key_pos[None, :] <= positions[:, None]) & (key_pos[None, :] < seq_length)
        return (jnp.where(allowed, scores, NEGATIVE), key_piece, value_piece)

    def max_pass(index, carry):
        running, total = carry
        scores = block_scores(index * key_block)[0]
        newest = jnp.maximum(running, jnp.max(scores, axis=-1))
        total = total * jnp.exp(running - newest) + jnp.sum(
            jnp.exp(scores - newest[..., None]), axis=-1
        )
        return (newest, total)

    start_max = jnp.full((kv_heads, group_factor, tokens), NEGATIVE, wide_type)
    running, total = lax.fori_loop(0, block_count, max_pass, (start_max, jnp.zeros_like(start_max)))
    log_total = running + jnp.log(total)

    def mix_pass(index, carry):
        scores, key_piece, value_piece = block_scores(index * key_block)
        weights = jnp.exp(scores - log_total[..., None]).astype(low_type)
        return carry + jnp.einsum(
            "kgqp,pkd->qkgd", weights, value_piece, preferred_element_type=wide_type
        )

    mixed = lax.fori_loop(
        0, block_count, mix_pass, jnp.zeros((tokens, kv_heads, group_factor, HEAD_SIZE), wide_type)
    )
    mixed_low = mixed.reshape(tokens, heads * HEAD_SIZE).astype(low_type)
    attention = lax.psum(jnp.dot(mixed_low, full_out, preferred_element_type=wide_type), "tensor")
    hidden = inputs + attention
    rms_two = lax.rsqrt(jnp.mean(hidden * hidden, axis=-1, keepdims=True) + EPS)
    normed_two = (hidden * rms_two * gain_two).astype(low_type)
    gate = jnp.dot(normed_two, full_gate, preferred_element_type=wide_type)
    up_proj = jnp.dot(normed_two, full_up, preferred_element_type=wide_type)
    sigma = jax.nn.sigmoid(gate)
    swish = gate * sigma
    activated = (swish * up_proj).astype(low_type)
    branch = lax.psum(
        jnp.dot(activated, full_down, preferred_element_type=wide_type).astype(jnp.bfloat16),
        "tensor",
    ).astype(jnp.float32)
    layer_out = (hidden + branch).astype(low_type)
    valid = (positions < seq_length)[:, None]
    grad_y = jnp.where(valid, cotangent[0].astype(wide_type), 0.0)
    grad_y_low = grad_y.astype(low_type)
    grad_down = transposed_times(activated, grad_y_low)
    grad_act = times_transposed(grad_y_low, full_down)
    grad_gate_low = (grad_act * up_proj * (sigma * (1.0 + gate * (1.0 - sigma)))).astype(low_type)
    grad_up_low = (grad_act * swish).astype(low_type)
    grad_gate = transposed_times(normed_two, grad_gate_low)
    grad_up = transposed_times(normed_two, grad_up_low)
    grad_normed_two = lax.psum(
        times_transposed(grad_gate_low, full_gate) + times_transposed(grad_up_low, full_up),
        "tensor",
    )
    norm_part, grad_gain_two = norm_back(grad_normed_two, hidden, rms_two, gain_two)
    grad_hidden = grad_y + norm_part
    grad_hidden_low = grad_hidden.astype(low_type)
    grad_out = transposed_times(mixed_low, grad_hidden_low)
    grad_mixed = (
        times_transposed(grad_hidden_low, full_out)
        .astype(low_type)
        .reshape(tokens, kv_heads, group_factor, HEAD_SIZE)
    )

    def delta_pass(index, carry):
        scores, key_piece, value_piece = block_scores(index * key_block)
        probs = jnp.exp(scores - log_total[..., None])
        dprob = jnp.einsum(
            "qkgd,pkd->kgqp", grad_mixed, value_piece, preferred_element_type=wide_type
        )
        return carry + jnp.sum(probs * dprob, axis=-1)

    delta = lax.fori_loop(
        0, block_count, delta_pass, jnp.zeros((kv_heads, group_factor, tokens), wide_type)
    )

    def grad_pass(index, carry):
        grad_queries, key_grads, value_grads = carry
        begin_at = index * key_block
        scores, key_piece, value_piece = block_scores(begin_at)
        probs = jnp.exp(scores - log_total[..., None])
        dprob = jnp.einsum(
            "qkgd,pkd->kgqp", grad_mixed, value_piece, preferred_element_type=wide_type
        )
        grad_scores = (probs * (dprob - delta[..., None])).astype(low_type)
        grad_queries = (
            grad_queries
            + jnp.einsum("kgqp,pkd->qkgd", grad_scores, key_piece, preferred_element_type=wide_type)
            * scale
        )
        key_part = (
            jnp.einsum(
                "kgqp,qkgd->pkd", grad_scores, query_rotated, preferred_element_type=wide_type
            )
            * scale
        )
        value_part = jnp.einsum(
            "kgqp,qkgd->pkd", probs.astype(low_type), grad_mixed, preferred_element_type=wide_type
        )
        key_grads = lax.dynamic_update_slice_in_dim(
            key_grads, key_part.reshape(key_block, kv_heads * HEAD_SIZE), begin_at, 0
        )
        value_grads = lax.dynamic_update_slice_in_dim(
            value_grads, value_part.reshape(key_block, kv_heads * HEAD_SIZE), begin_at, 0
        )
        return (grad_queries, key_grads, value_grads)

    empty_keys = jnp.zeros((total_keys, kv_heads * HEAD_SIZE), wide_type)
    start_state = (
        jnp.zeros((tokens, kv_heads, group_factor, HEAD_SIZE), wide_type),
        empty_keys,
        empty_keys,
    )
    grad_queries, key_grads, value_grads = lax.fori_loop(0, block_count, grad_pass, start_state)
    key_local, value_local = (
        lax.psum_scatter(key_grads, "ctx", scatter_dimension=0, tiled=True),
        lax.psum_scatter(value_grads, "ctx", scatter_dimension=0, tiled=True),
    )
    grad_query_low = (
        rotate_back(grad_queries.reshape(tokens, heads, HEAD_SIZE), cosine_table, sine_table)
        .reshape(tokens, heads * HEAD_SIZE)
        .astype(low_type)
    )
    grad_key_low = (
        rotate_back(key_local.reshape(tokens, kv_heads, HEAD_SIZE), cosine_table, sine_table)
        .reshape(tokens, kv_heads * HEAD_SIZE)
        .astype(low_type)
    )
    grad_value_low = value_local.astype(low_type)
    grad_query = transposed_times(first_normed, grad_query_low)
    grad_key = transposed_times(first_normed, grad_key_low)
    grad_value = transposed_times(first_normed, grad_value_low)
    grad_normed_one = lax.psum(
        (
            times_transposed(grad_query_low, full_query)
            + times_transposed(grad_key_low, full_key)
            + times_transposed(grad_value_low, full_value)
        ).astype(jnp.bfloat16),
        "tensor",
    ).astype(jnp.float32)
    first_part, grad_gain_one = norm_back(grad_normed_one, inputs, rms_one, gain_one)
    grad_states = grad_hidden + first_part
    summed = tuple(
        (
            lax.psum_scatter(grad_gain_one, ("ctx", "dp"), scatter_dimension=0, tiled=True),
            lax.psum_scatter(grad_query, ("ctx", "dp"), scatter_dimension=0, tiled=True),
            lax.psum_scatter(grad_key, ("ctx", "dp"), scatter_dimension=0, tiled=True),
            lax.psum_scatter(grad_value, ("ctx", "dp"), scatter_dimension=0, tiled=True),
            lax.psum_scatter(grad_out, ("ctx", "dp"), scatter_dimension=1, tiled=True),
            lax.psum_scatter(grad_gain_two, ("ctx", "dp"), scatter_dimension=0, tiled=True),
            lax.psum_scatter(grad_gate, ("ctx", "dp"), scatter_dimension=0, tiled=True),
            lax.psum_scatter(grad_up, ("ctx", "dp"), scatter_dimension=0, tiled=True),
            lax.psum_scatter(grad_down, ("ctx", "dp"), scatter_dimension=1, tiled=True),
        )
    )
    return (
        layer_out[None],
        grad_states[None],
        summed[0],
        summed[1],
        summed[2],
        summed[3],
        summed[4],
        summed[5],
        summed[6],
        summed[7],
        summed[8],
    )


MESH = pl.DeviceIdType.MESH
HBM = pltpu.MemorySpace.HBM
VMEM = pltpu.MemorySpace.VMEM
STEPS = [(1, -1), (1, 1), (2, -1), (2, 1), (3, -1), (3, 1)]


def position():
    t, c, d = lax.axis_index("tensor"), lax.axis_index("ctx"), lax.axis_index("dp")
    return t, c, d // 2, d % 2


def only(cond, act):
    if cond is True:
        act()
    else:
        pl.when(cond)(act)


class Wires:
    def __init__(self, send, recv):
        self.send, self.recv, self.used, self.sent = send, recv, 0, []

    def index(self):
        self.used += 1
        return self.used - 1

    def copy(self, i, src, dst, device, lands=None):
        return pltpu.make_async_remote_copy(
            src_ref=src,
            dst_ref=dst,
            send_sem=self.send.at[i],
            recv_sem=self.recv.at[i if lands is None else lands],
            device_id=device,
            device_id_type=MESH,
        )

    def push(self, i, src, dst, device, cond=True, lands=None):
        only(cond, lambda: self.copy(i, src(), dst(), device, lands).start())
        self.sent.append((cond, lambda: self.copy(i, src(), dst(), device).wait_send()))

    def owe(self, i, src, cond=True):
        self.sent.append((cond, lambda: self.copy(i, src(), src(), position_id()).wait_send()))

    def arrive(self, i, dst, cond=True):
        def act():
            place = dst()
            self.copy(i, place, place, position_id()).wait_recv()

        only(cond, act)

    def local(self, i, src, dst):
        def make():
            return pltpu.make_async_copy(src(), dst(), self.send.at[i])

        make().start()
        self.sent.append((True, lambda: make().wait()))

    def fetch(self, i, src, dst):
        copy = pltpu.make_async_copy(src, dst, self.recv.at[i])
        copy.start()
        return copy

    def drain(self):
        for cond, act in self.sent:
            only(cond, act)
        self.sent = []


def position_id():
    t, c, y, e = position()
    return (t, c, y * 2 + e)


def greet(peers):
    barrier = pltpu.get_barrier_semaphore()
    count = 0
    for cond, device in peers:
        only(
            cond,
            functools.partial(
                pl.semaphore_signal, barrier, inc=1, device_id=device, device_id_type=MESH
            ),
        )
        count = count + (1 if cond is True else cond.astype(jnp.int32))
    pl.semaphore_wait(barrier, count)


def around(pos, chain=True, x=False, y=False, core=True, row=False):
    t, c, yy, e = pos
    d = yy * 2 + e
    peers = []
    if chain:
        peers += [(c < 3, (t, c + 1, d)), (c > 0, (t, c - 1, d))]
    if x:
        peers.append((True, (1 - t, c, d)))
    if y:
        peers.append((True, (t, c, (1 - yy) * 2 + e)))
    if core:
        peers.append((True, (t, c, yy * 2 + 1 - e)))
    return peers


def reach(c, s, sign):
    k = c + sign * s
    return k, ((k >= 0) if sign < 0 else (k <= 3))


def plane_gather(wires, pos, src, at):
    t, c, y, e = pos
    d, d_y, d_e = y * 2 + e, (1 - y) * 2 + e, y * 2 + 1 - e
    z_id = {key: wires.index() for key in STEPS}
    y_id = {key: wires.index() for key in [(0, 0)] + STEPS}
    e_id = {key: wires.index() for key in [(0, 0)] + STEPS}
    f_id = {key: wires.index() for key in [(0, 0)] + STEPS}
    fetch = wires.fetch(wires.index(), src(), at(c, d))

    def spread(key, block, place, cond):
        s, sign = key
        if s < 3:
            for way in ((-1, 1) if s == 0 else (sign,)):
                nxt = c - way
                here = (nxt >= 0) if way > 0 else (nxt <= 3)
                wires.push(
                    z_id[(s + 1, way)], block, place, (t, nxt, d),
                    here if cond is True else (cond & here),
                )
        wires.push(y_id[key], block, place, (t, c, d_y), cond)
        wires.push(e_id[key], block, place, (t, c, d_e), cond)

    def relay(key, cond):
        k = c + key[0] * key[1]
        place = lambda: at(k, d_y)
        wires.arrive(y_id[key], place, cond)
        wires.push(f_id[key], place, place, (t, c, d_e), cond)

    spread((0, 0), src, lambda: at(c, d), True)
    yield
    late = [((0, 0), True)]
    for key in STEPS:
        k, cond = reach(c, *key)
        place = lambda k=k: at(k, d)
        wires.arrive(z_id[key], place, cond)
        spread(key, place, place, cond)
        if key[1] > 0:
            for old in late:
                relay(*old)
            late = []
            yield
        late.append((key, cond))
    for old in late:
        relay(*old)
    yield
    for key in [(0, 0)] + STEPS:
        k, cond = (c, True) if key[0] == 0 else reach(c, *key)
        wires.arrive(e_id[key], lambda: at(k, d_e), cond)
        wires.arrive(f_id[key], lambda: at(k, (1 - y) * 2 + 1 - e), cond)
    fetch.wait()


def token_gather(wires, pos, src, at, half):
    t, c, y, e = pos
    d, d_e = y * 2 + e, y * 2 + 1 - e
    z_id = {key: wires.index() for key in STEPS}
    x_id = {key: wires.index() for key in STEPS}
    e_id = {key: wires.index() for key in STEPS}
    f_id = {key: wires.index() for key in STEPS}
    own = wires.index(), wires.index()
    here = wires.index(), wires.index()
    for way in (-1, 1):
        nxt = c - way
        wires.push(
            z_id[(1, way)], lambda: half(t), lambda: at(e, c, t), (t, nxt, d),
            (nxt >= 0) if way > 0 else (nxt <= 3),
        )
    for i in (0, 1):
        wires.push(own[i], lambda i=i: half(i), lambda i=i: at(e, c, i), (t, c, d_e))
    fetch = [wires.fetch(here[i], half(i), at(e, c, i)) for i in (0, 1)]
    yield

    def relay(key, cond):
        k = c + key[0] * key[1]
        place = lambda: at(e, k, 1 - t)
        wires.arrive(x_id[key], place, cond)
        wires.push(f_id[key], place, place, (t, c, d_e), cond)

    late = []
    for key in STEPS:
        k, cond = reach(c, *key)
        place = lambda k=k: at(e, k, t)
        wires.arrive(z_id[key], place, cond)
        s, sign = key
        if s < 3:
            nxt = c - sign
            ok = (nxt >= 0) if sign > 0 else (nxt <= 3)
            wires.push(z_id[(s + 1, sign)], place, place, (t, nxt, d), cond & ok)
        wires.push(x_id[key], place, place, (1 - t, c, d), cond)
        wires.push(e_id[key], place, place, (t, c, d_e), cond)
        if sign > 0:
            for old in late:
                relay(*old)
            late = []
            yield
        late.append((key, cond))
    for old in late:
        relay(*old)
    yield
    for i in (0, 1):
        wires.arrive(own[i], lambda i=i: at(1 - e, c, i))
    for key in STEPS:
        k, cond = reach(c, *key)
        wires.arrive(e_id[key], lambda: at(1 - e, k, t), cond)
        wires.arrive(f_id[key], lambda: at(1 - e, k, 1 - t), cond)
    for copy in fetch:
        copy.wait()


def unit_scatter(wires, pos, piece, place):
    t, c, y, e = pos
    me = c * 2 + e
    first = [wires.index() for _ in range(8)]
    second = [wires.index() for _ in range(8)]
    fetch = wires.fetch(first[0], piece(me), place(c, y * 2 + e))
    for i in range(1, 8):
        q = lax.rem(me + i, 8)
        wires.push(
            first[i], lambda q=q: piece(q), lambda: place(c, y * 2 + e), (t, q // 2, y * 2 + q % 2)
        )
    wires.push(
        second[0], lambda: piece(me), lambda: place(c, y * 2 + e), (t, c, (1 - y) * 2 + e)
    )
    yield
    for i in range(1, 8):
        q = lax.rem(me + 8 - i, 8)
        block = lambda q=q: place(q // 2, y * 2 + q % 2)
        wires.arrive(first[i], block)
        wires.push(second[i], block, block, (t, c, (1 - y) * 2 + e))
        yield
    yield
    for i in range(8):
        q = lax.rem(me + 8 - i, 8)
        wires.arrive(second[i], lambda q=q: place(q // 2, (1 - y) * 2 + q % 2))
    fetch.wait()


def run_all(parts):
    parts = list(parts)
    while parts:
        for part in list(parts):
            try:
                next(part)
            except StopIteration:
                parts.remove(part)


def rows(ref, start, size):
    return ref.at[pl.ds(pl.multiple_of(start, 16), size)]


def dot_nn(a, b):
    return lax.dot_general(a, b, (((1,), (0,)), ((), ())), preferred_element_type=jnp.float32)


def by_rows(count, width, act):
    step = max(16, 32768 // width)
    while count % step:
        step -= 16

    def body(i, carry):
        act(pl.ds(pl.multiple_of(i * step, step), step))
        return carry

    lax.fori_loop(0, count // step, body, 0)


ORDER = (3, 0, 2, 1)


def chain_sum(wires, pos, height, value, keep, came, extra, done):
    t, c, y, e = pos
    d = y * 2 + e
    wide = jnp.float32
    r_id = [wires.index() for _ in range(4)]
    l_id = [wires.index() for _ in range(4)]

    def stage(s):
        for edge, way, blocks, number in (
            (s, 1, range(3, s, -1), r_id), (3 - s, -1, range(0, 3 - s), l_id)
        ):
            here = c == edge
            for k in blocks:

                def act(k=k, number=number):
                    place = keep(k)
                    if s > 0:
                        wires.arrive(number[k], lambda: came.at[k])

                    def add(r):
                        total = value(k, r)
                        if s > 0:
                            total = total + came[k, r].astype(wide)
                        place[r] = total.astype(place.dtype)

                    by_rows(height, extra.shape[-1], add)

                pl.when(here)(act)
                target = extra if way < 0 and k == edge - 1 else came.at[k]
                wires.push(
                    number[k], lambda k=k: keep(k), lambda target=target: target,
                    (t, c + way, d), here,
                )

    def finish():
        for k in range(4):

            def act(k=k):
                if k > 0:
                    wires.arrive(r_id[k], lambda: came.at[k])
                if k < 3:
                    wires.arrive(l_id[k], lambda: extra)

                def add(r):
                    total = value(k, r)
                    if k > 0:
                        total = total + came[k, r].astype(wide)
                    if k < 3:
                        total = total + extra[r].astype(wide)
                    done(r, total)

                by_rows(height, extra.shape[-1], add)

            pl.when(c == k)(act)

    return stage, finish


def token_scatter(wires, pos, part, out, scratch, credit):
    t, c, y, e = pos
    near, own, x_in, came, extra = scratch
    wide = jnp.float32
    tokens, half = x_in.shape[1], x_in.shape[2]
    d_e = y * 2 + 1 - e
    e_id = [wires.index() for _ in range(4)]
    x_id = [wires.index() for _ in range(4)]
    last = wires.index()
    mine = pl.ds(pl.multiple_of(t * half, 128), half)
    other = pl.ds(pl.multiple_of((1 - t) * half, 128), half)

    def begin(k, f):
        return pl.multiple_of((k * 2 + f) * tokens, 16)

    pl.semaphore_wait(credit.at[0], 1)
    for k in ORDER:
        wires.push(
            e_id[k], lambda k=k: part.at[pl.ds(begin(k, 1 - e), tokens)],
            lambda k=k: near.at[k], (t, c, d_e),
        )
    fetch = [
        wires.fetch(wires.index(), part.at[pl.ds(begin(k, e), tokens)], own(k)) for k in range(4)
    ]
    yield
    pl.semaphore_wait(credit.at[1], 1)
    for k in ORDER:
        fetch[k].wait()
        wires.arrive(e_id[k], lambda: near.at[k])

        def away(r):
            total = own(k)[r, other].astype(wide) + near[k, r, other].astype(wide)
            near[k, r, other] = total.astype(near.dtype)

        by_rows(tokens, half, away)
        wires.push(
            x_id[k], lambda k=k: near.at[k, :, other], lambda k=k: x_in.at[k], (1 - t, c, y * 2 + e)
        )
    yield

    def value(k, r):
        return (
            own(k)[r, mine].astype(wide)
            + near[k, r, mine].astype(wide)
            + x_in[k, r].astype(wide)
        )

    def done(r, total):
        out[r, mine] = total.astype(out.dtype)

    stage, finish = chain_sum(
        wires, pos, tokens, value, lambda k: near.at[k, :, mine], came, extra, done
    )
    pl.when(c < 3)(lambda: pl.semaphore_wait(credit.at[2], 1))
    pl.when(c > 0)(lambda: pl.semaphore_wait(credit.at[3], 1))
    for k in ORDER:
        wires.arrive(x_id[k], lambda: x_in.at[k])
    for s in range(3):
        stage(s)
        yield
    finish()
    wires.push(last, lambda: out.at[:, mine], lambda: out.at[:, mine], (1 - t, c, y * 2 + e))
    yield
    wires.arrive(last, lambda: out.at[:, other])


def plane_scatter(wires, pos, out_block, own_block, height, scratch, done, straight=False):
    t, c, y, e = pos
    near, y_in, came, extra = scratch
    wide = jnp.float32
    d_y, d_e = (1 - y) * 2 + e, y * 2 + 1 - e
    e_id = {(k, f): wires.index() for f in range(2) for k in range(4)}
    y_id = [wires.index() for _ in range(4)]
    for f in range(2):
        yy = (1 - y) if f == 0 else y
        for k in ORDER:
            wires.push(
                e_id[k, f], lambda k=k, yy=yy: out_block(k, yy),
                lambda k=k, f=f: near.at[f * 4 + k], (t, c, d_e),
            )
    yield
    for k in ORDER:
        wires.arrive(e_id[k, 0], lambda: near.at[k])
        block = own_block(k, 1 - y)

        def away(r):
            total = block[r].astype(wide) + near[k, r].astype(wide)
            near[k, r] = total.astype(near.dtype)

        by_rows(height, extra.shape[-1], away)
        wires.push(y_id[k], lambda k=k: near.at[k], lambda k=k: y_in.at[k], (t, c, d_y))
        yield

    def block_value(k, r):
        block = own_block(k, y)
        return (
            block[r].astype(wide)
            + near[4 + k, r].astype(wide)
            + y_in[k, r].astype(wide)
        )

    def value(k, r):
        return (
            own_block(k, y)[r].astype(wide)
            + near[4 + k, r].astype(wide)
            + y_in[k, r].astype(wide)
        )

    if straight:
        s_id = [wires.index() for _ in range(4)]
        for far in (3, 1, 2):
            k = lax.rem(c + far, 4)
            wires.arrive(e_id[0, 1] + k, lambda: near.at[4 + k])
            wires.arrive(y_id[0] + k, lambda: y_in.at[k])

            def settle(r):
                near[4 + k, r] = block_value(k, r).astype(near.dtype)

            by_rows(height, extra.shape[-1], settle)
            wires.push(
                s_id[far], lambda k=k: near.at[4 + k], lambda far=far: came.at[far],
                (t, k, y * 2 + e),
            )
            yield
        wires.arrive(e_id[0, 1] + c, lambda: near.at[4 + c])
        wires.arrive(y_id[0] + c, lambda: y_in.at[c])
        for far in (3, 1, 2):
            wires.arrive(s_id[far], lambda: came.at[far])

        def add(r):
            total = block_value(c, r)
            for far in (1, 2, 3):
                total = total + came[far, r].astype(wide)
            done(r, total)

        by_rows(height, extra.shape[-1], add)
        return

    stage, finish = chain_sum(
        wires, pos, height, value, lambda k: near.at[4 + k], came, extra, done
    )
    for k in ORDER:
        wires.arrive(e_id[k, 1], lambda: near.at[4 + k])
        wires.arrive(y_id[k], lambda: y_in.at[k])
    for s in range(3):
        stage(s)
        yield
    finish()


def plane_scratch(shape):
    low = jnp.bfloat16
    return [
        pltpu.VMEM((8,) + shape, low),
        pltpu.VMEM((4,) + shape, low),
        pltpu.VMEM((4,) + shape, low),
        pltpu.VMEM(shape, low),
    ]


def unit_gather(wires, pos, grads, came, y_id, out):
    t, c, y, e = pos
    wide = jnp.float32
    units, lanes = came.shape[2], out.shape[2]
    me = c * 2 + e
    o_id = [wires.index() for _ in range(8)]
    here = pl.ds(pl.multiple_of(me * units, 16), units)
    fetch = []
    for far in (2, 3, 1, 0):
        k = lax.rem(c + far, 4)
        wires.arrive(y_id + k, lambda: came.at[k])
        where = pl.ds(pl.multiple_of((k * 2 + y) * 2 * lanes, 256), 2 * lanes)
        for m in range(3):

            def add(r):
                both = grads[m, r, where].astype(wide) + came[k, m, r].astype(wide)
                grads[m, r, where] = both.astype(grads.dtype)

            by_rows(units, 2 * lanes, add)
        for f in range(2):
            g = e if f == 0 else 1 - e
            src = lambda k=k, g=g: grads.at[
                :, pl.ds(0, units), pl.ds(pl.multiple_of(((k * 2 + y) * 2 + g) * lanes, 128), lanes)
            ]
            if far == 0 and f == 0:
                fetch.append(wires.fetch(wires.index(), src(), out.at[:, here]))
            else:
                wires.push(o_id[far * 2 + f], src, lambda: out.at[:, here], (t, k, y * 2 + g))
        yield
    for far in (1, 2, 3, 0):
        for f in range(2):
            if far == 0 and f == 0:
                continue
            k = lax.rem(c + 4 - far, 4)
            g = e if f == 0 else 1 - e
            wires.arrive(
                o_id[far * 2 + f],
                lambda: out.at[:, pl.ds(pl.multiple_of((k * 2 + g) * units, 16), units)],
            )
    fetch[0].wait()


def swap_halves(x):
    lane = lax.broadcasted_iota(jnp.int32, x.shape, 1)
    ahead, behind = pltpu.roll(x, x.shape[1] - 32, 1), pltpu.roll(x, 32, 1)
    return jnp.where(lax.rem(lane, 64) < 32, ahead, behind)


def head_probs(query, keys, allowed):
    scores = times_transposed(query, keys) * (HEAD_SIZE ** (-0.5))
    scores = jnp.where(allowed, scores, NEGATIVE)
    shifted = jnp.exp(scores - jnp.max(scores, axis=-1, keepdims=True))
    return shifted * (1.0 / jnp.sum(shifted, axis=-1, keepdims=True))


def norm_rows(upstream, inputs, gain):
    rms = lax.rsqrt(jnp.mean(inputs * inputs, axis=-1, keepdims=True) + EPS)
    gain_grad = jnp.sum(upstream * inputs * rms, axis=0, keepdims=True)
    scaled = upstream * gain
    inner = jnp.mean(scaled * inputs, axis=-1, keepdims=True)
    return rms * scaled - inputs * (rms * rms * rms * inner), gain_grad


def advance(parts, count=1):
    for _ in range(count):
        for part in list(parts):
            try:
                next(part)
            except StopIteration:
                parts.remove(part)


def pick(c, table):
    value = table[0]
    for i in range(1, 4):
        value = jnp.where(c == i, table[i], value)
    return value


NEAREST = ((0, 1, 2, 3), (1, 0, 2, 3), (2, 3, 1, 0), (3, 2, 1, 0))


def layer_kernel(
    lengths, states, gains, qkv, out_w, w3, gy, cosine, sine,
    layer_out, grad_states, g3_out, gq_out, gk_out, gv_out, go_out, gain_out, qkv_kept, part_b,
    send, recv, credit, qkv_all, out_all, gain_all, hidden, normed_one, q_rot, kv_all, mixed, gn_own,
    w3_all, gy_all, nt_all, act_t, part_g, stage_b, unit_in, kv_own, pair_out, pair_in, nt,
    near, x_in, came, grad_hidden, grad_low, branch, mixed_t, grad_mixed, gqkv, normed_t, gq_part,
    dk, dv, kv_part, kv_in, gains_sum, gain_in, *scratch,
):
    pos = position()
    t, c, y, e = pos
    low, wide = jnp.bfloat16, jnp.float32
    wires = Wires(send, recv)
    d = y * 2 + e
    me = c * 4 + d
    here, beside, over = (t, c, d), (t, c, y * 2 + 1 - e), (1 - t, c, d)
    peers = [(True, over)]
    for i in range(1, 16):
        q = lax.rem(me + i, 16)
        peers.append((True, (t, q // 4, lax.rem(q, 4))))
    greet(peers)
    tokens, width = states.shape
    half = width // 2
    block, n_all = qkv.shape
    n_query = q_rot.shape[1]
    n_key = (n_all - n_query) // 2
    lanes = out_w.shape[1]
    units = unit_in.shape[2]
    scaled = grad_hidden

    def lane_block(q, size=lanes):
        return pl.ds(pl.multiple_of(q * size, 128), size)

    gain_id = [wires.index() for _ in range(16)]
    for i in range(1, 16):
        q = lax.rem(me + i, 16)
        wires.push(
            gain_id[i], lambda: gains, lambda: gain_all.at[:, lane_block(me)],
            (t, q // 4, lax.rem(q, 4)),
        )
    fetch_gain = wires.fetch(wires.index(), gains, gain_all.at[:, lane_block(me)])
    g_qkv = [
        plane_gather(wires, pos, lambda: qkv, lambda k, f: rows(qkv_all, (k * 4 + f) * block, block))
    ]
    g_out = [
        plane_gather(
            wires, pos, lambda: out_w, lambda k, f: out_all.at[:, lane_block(k * 4 + f)]
        )
    ]
    g_unit = [
        unit_scatter(
            wires, pos,
            lambda q: w3.at[:, pl.ds(pl.multiple_of(q * units, 16), units)],
            lambda k, f: w3_all.at[:, pl.ds(0, units), lane_block(k * 4 + f)],
        )
    ]

    def spot(ref):
        return lambda f, k, h: ref.at[
            pl.ds(pl.multiple_of((k * 2 + f) * tokens, 16), tokens), lane_block(h, half)
        ]

    g_gy = [token_gather(wires, pos, None, spot(gy_all), lambda h: gy.at[:, lane_block(h, half)])]
    advance(g_qkv)
    advance(g_gy)
    w3_all[:, units:, :] = jnp.zeros_like(w3_all[:, units:, :])

    def scale_rows(r):
        x = states[r].astype(wide)
        scaled[r] = x * lax.rsqrt(jnp.mean(x * x, axis=-1, keepdims=True) + EPS)

    by_rows(tokens, width, scale_rows)
    advance(g_qkv)
    advance(g_out)
    advance(g_gy)
    advance(g_qkv)
    advance(g_out)
    advance(g_gy)
    advance(g_qkv)
    advance(g_out)
    advance(g_gy)
    while g_qkv:
        advance(g_qkv)
    fetch_gain.wait()
    for i in range(1, 16):
        q = lax.rem(me + 16 - i, 16)
        wires.arrive(gain_id[i], lambda: gain_all.at[:, lane_block(q)])
    gain_one = gain_all[...].astype(wide)[0:1]
    gain_two = gain_all[...].astype(wide)[1:2]

    save_qkv = wires.fetch(wires.index(), qkv_all, qkv_kept)

    def norm_one(r):
        normed_one[r] = (scaled[r] * gain_one).astype(low)

    by_rows(tokens, width, norm_one)

    def turned(x):
        return x * cosine[...] + swap_halves(x) * sine[...]

    tail = dot_nn(normed_one[...], qkv_all[:, n_query:])
    kv_own[:, :n_key] = turned(tail[:, :n_key]).astype(low)
    kv_own[:, n_key:] = tail[:, n_key:].astype(low)
    kv_all[pl.ds(pl.multiple_of(c * tokens, 16), tokens)] = kv_own[...]
    kv_id = [wires.index() for _ in range(3)]
    for i in range(3):
        k = lax.rem(c + i + 1, 4)
        wires.push(kv_id[i], lambda: kv_own, lambda: rows(kv_all, c * tokens, tokens), (t, k, d))
    advance(g_unit)

    def project(j, carry):
        where = pl.ds(pl.multiple_of(j * 256, 256), 256)
        two = dot_nn(normed_one[...], qkv_all[:, where])
        for h in range(2):
            slab = pl.ds(pl.multiple_of(j * 256 + h * 128, 128), 128)
            q_rot[:, slab] = turned(two[:, h * 128 : (h + 1) * 128]).astype(low)
        return carry

    lax.fori_loop(0, n_query // 256, project, 0)
    advance(g_out)
    for i in range(3):
        k = lax.rem(c + 3 - i, 4)
        wires.arrive(kv_id[i], lambda: rows(kv_all, k * tokens, tokens))
    q_pos = c * tokens + lax.broadcasted_iota(jnp.int32, (tokens, kv_all.shape[0]), 0)
    k_pos = lax.broadcasted_iota(jnp.int32, (tokens, kv_all.shape[0]), 1)
    allowed = (k_pos <= q_pos) & (k_pos < lengths[0])
    pairs = n_query // 256
    for g in range(2):
        keys = kv_all[:, g * HEAD_SIZE : (g + 1) * HEAD_SIZE]
        values = kv_all[:, n_key + g * HEAD_SIZE : n_key + (g + 1) * HEAD_SIZE]

        def pair(j, carry, g=g, keys=keys, values=values):
            slab = pl.ds(pl.multiple_of((g * pairs + j) * 128, 128), 128)
            q_two = q_rot[:, slab]
            both_heads = []
            for h in range(2):
                probs = head_probs(q_two[:, h * HEAD_SIZE : (h + 1) * HEAD_SIZE], keys, allowed)
                both_heads.append(dot_nn(probs.astype(low), values))
            mixed[:, slab] = jnp.concatenate(both_heads, axis=1).astype(low)
            return carry

        lax.fori_loop(0, pairs, pair, 0)
        if g == 0:
            advance(g_out)
    while g_out:
        advance(g_out)
    advance(g_unit)
    pair_id = [wires.index() for _ in range(4)]
    for i in range(4):
        for j in range(2):
            where = pl.ds(i * (width // 4) + j * (width // 8), width // 8)
            pair_out[:, where] = dot_nn(mixed[...], out_all[:, where]).astype(low)
        piece = pl.ds(i * (width // 4), width // 4)
        wires.push(pair_id[i], lambda p=piece: pair_out.at[:, p], lambda p=piece: pair_in.at[:, p], over)
    advance(g_unit, 2)
    for i in range(4):
        piece = pl.ds(i * (width // 4), width // 4)
        wires.arrive(pair_id[i], lambda: pair_in.at[:, piece])

    def norm_two(r):
        total = states[r].astype(wide) + (pair_out[r].astype(wide) + pair_in[r].astype(wide))
        hidden[r] = total
        factor = lax.rsqrt(jnp.mean(total * total, axis=-1, keepdims=True) + EPS)
        nt[r] = (total * factor * gain_two).astype(low)

    by_rows(tokens, width, norm_two)

    gathers = []
    for source, target in ((nt, nt_all),):
        at = spot(target)
        z_id, x_id, e_id, f_id = [[wires.index() for _ in range(4)][0] for _ in range(4)]
        gathers.append((at, z_id, x_id, e_id, f_id))
        own_half = lambda h, source=source: source.at[:, lane_block(h, half)]
        for i in (3, 1, 2):
            k = lax.rem(c + i, 4)
            wires.push(
                wires.index(), lambda own=own_half: own(t), lambda at=at: at(e, c, t), (t, k, d),
                lands=z_id + c,
            )
        wires.push(e_id + c, lambda own=own_half: own(t), lambda at=at: at(e, c, t), beside)
        wires.push(f_id + c, lambda own=own_half: own(1 - t), lambda at=at: at(e, c, 1 - t), beside)
    at_home = pl.ds(pl.multiple_of((c * 2 + e) * tokens, 16), tokens)
    nt_all[at_home] = nt[...]
    advance(g_unit, 4)
    while g_gy:
        advance(g_gy)

    def nearest(j):
        return pick(c, [sum_of(j, NEAREST[i]) for i in range(4)])

    def sum_of(j, order):
        value = order[0]
        for i in range(1, 4):
            value = jnp.where(j == i, order[i], value)
        return value

    def stage_one(j):
        k = nearest(j)
        for at, z_id, x_id, e_id, f_id in gathers:
            wires.arrive(z_id + k, lambda: at(e, k, t))
            wires.copy(x_id + k, at(e, k, t), at(e, k, t), over).start()
            wires.copy(e_id + k, at(e, k, t), at(e, k, t), beside).start()

    def stage_two(j):
        k = nearest(j)
        for at, z_id, x_id, e_id, f_id in gathers:

            def act():
                wires.arrive(x_id + k, lambda: at(e, k, 1 - t))
                wires.copy(f_id + k, at(e, k, 1 - t), at(e, k, 1 - t), beside).start()

            pl.when(j > 0)(act)
        for at, z_id, x_id, e_id, f_id in gathers:
            wires.arrive(e_id + k, lambda: at(1 - e, k, t))
            wires.arrive(f_id + k, lambda: at(1 - e, k, 1 - t))

    n_id = [wires.index() for _ in range(4)][0]
    r_id = [wires.index() for _ in range(4)][0]

    def part_rows(k, f):
        return part_g.at[pl.ds(pl.multiple_of((k * 2 + f) * tokens, 16), tokens)]

    mine, other = lane_block(t, half), lane_block(1 - t, half)

    def stage_three(j):
        k = nearest(j)
        wires.arrive(n_id + k, lambda: near.at[k])
        ours = part_rows(k, e)

        def away(r):
            total = ours[r, other].astype(wide) + near[k, r, other].astype(wide)
            near[k, r, other] = total.astype(low)

        by_rows(tokens, half, away)
        wires.copy(r_id + k, near.at[k, :, other], x_in.at[k], over).start()

    def kept(k, r):
        return (
            part_rows(k, e)[r, mine].astype(wide)
            + near[k, r, mine].astype(wide)
            + x_in[k, r].astype(wide)
        )

    s_id = [wires.index() for _ in range(4)][0]

    def stage_four(j):
        k = nearest(j)
        wires.arrive(r_id + k, lambda: x_in.at[k])

        def add(r):
            near[k, r, mine] = kept(k, r).astype(low)

        by_rows(tokens, half, add)
        i = lax.rem(k - c + 4, 4)
        wires.copy(s_id + i, near.at[k, :, mine], came.at[i - 1], (t, k, d)).start()

    padded = act_t.shape[0]
    act = qkv_all.at[pl.ds(0, tokens * 8), pl.ds(0, padded)]
    both = qkv_all.at[pl.ds(0, tokens * 8), pl.ds(padded, 2 * padded)]
    both_t = qkv_all.at[pl.ds(tokens * 8, 2 * padded), pl.ds(0, tokens * 8)]
    b_id = wires.index()

    def stored(k):
        where = pl.ds(pl.multiple_of(k * 2 * tokens, 16), 2 * tokens)
        return pltpu.make_async_copy(stage_b, part_b.at[where], wires.recv.at[b_id])

    def swiglu(j, carry):
        stage_two(j)
        k = nearest(j)
        where = pl.ds(pl.multiple_of(k * 2 * tokens, 16), 2 * tokens)
        x = nt_all[where]
        gate = times_transposed(x, w3_all[0])
        up = times_transposed(x, w3_all[1])
        grad_act = times_transposed(gy_all[where], w3_all[2])
        sigma = jax.nn.sigmoid(gate)
        swish = gate * sigma
        act[where] = (swish * up).astype(low)
        wide_units = gate.shape[1]
        both[where, :wide_units] = (
            grad_act * up * (sigma * (1.0 + gate * (1.0 - sigma)))
        ).astype(low)
        both[where, wide_units:] = (grad_act * swish).astype(low)
        for i in range(4):
            piece = slice(i * (width // 4), (i + 1) * (width // 4))
            part_g[where, piece] = (
                dot_nn(both[where, :wide_units], w3_all[0, :, piece])
                + dot_nn(both[where, wide_units:], w3_all[1, :, piece])
            ).astype(low)
        wires.copy(n_id + k, part_rows(k, 1 - e), near.at[k], beside).start()
        pl.when(j > 0)(lambda: stored(0).wait())
        for i in range(4):
            piece = slice(i * (width // 4), (i + 1) * (width // 4))
            stage_b[:, piece] = dot_nn(act[where], w3_all[2, :, piece]).astype(low)
        stored(k).start()
        pl.when(j > 0)(lambda: stage_three(j - 1))
        pl.when(j > 2)(lambda: stage_four(j - 2))
        return carry

    for j in range(1, 4):
        stage_one(j)
    while g_unit:
        advance(g_unit)
    save_qkv.wait()
    wires.drain()
    lax.fori_loop(0, 4, swiglu, 0)
    stored(0).wait()
    stage_three(3)
    for k in range(4):
        away = c != k
        for at, z_id, x_id, e_id, f_id in gathers:
            half_at = lambda h, k=k, at=at: at(e, k, h)
            wires.owe(x_id + k, lambda f=half_at: f(t), away)
            wires.owe(e_id + k, lambda f=half_at: f(t), away)
            wires.owe(f_id + k, lambda f=half_at: f(1 - t), away)
        wires.owe(n_id + k, lambda k=k: part_rows(k, 1 - e))
        wires.owe(r_id + k, lambda k=k: near.at[k, :, other])
    for i in (1, 2, 3):
        k = lax.rem(c + i, 4)
        wires.owe(s_id + i, lambda k=k: near.at[k, :, mine])
    stage_four(2)
    act_t[...] = act[...].T
    both_t[...] = both[...].T

    def unit_grads(k, yy):
        where = lane_block(k * 2 + yy, 256)
        two = dot_nn(both_t[...], nt_all[:, where]).astype(low)
        w3_all[0, :units, where] = two[:units]
        w3_all[1, :units, where] = two[padded : padded + units]
        w3_all[2, :units, where] = dot_nn(act_t[...], gy_all[:, where]).astype(low)[:units]

    u_id = [wires.index() for _ in range(4)][0]
    across = (t, c, (1 - y) * 2 + e)

    def half_grads(k):
        return w3_all.at[:, pl.ds(0, units), lane_block(k * 2 + 1 - y, 256)]

    def send_units(j, carry):
        k = lax.rem(c + pick(j, (2, 3, 1, 0)), 4)
        unit_grads(k, 1 - y)
        wires.copy(u_id + k, half_grads(k), unit_in.at[k], across).start()
        return carry

    lax.fori_loop(0, 2, send_units, 0)
    stage_four(3)
    lax.fori_loop(2, 4, send_units, 0)

    def keep_units(j, carry):
        unit_grads(lax.rem(c + pick(j, (2, 3, 1, 0)), 4), y)
        return carry

    lax.fori_loop(0, 2, keep_units, 0)
    g_unit = [unit_gather(wires, pos, w3_all, unit_in, u_id, g3_out)]
    owed, bulk = wires.sent, []
    wires.sent = bulk
    advance(g_unit)
    wires.sent = owed
    wires.arrive(r_id + c, lambda: x_in.at[c])
    for i in (3, 1, 2):
        wires.arrive(s_id + i, lambda: came.at[i - 1])

    def done(r):
        total = kept(c, r)
        for i in range(3):
            total = total + came[i, r].astype(wide)
        gn_own[r, mine] = total.astype(low)

    by_rows(tokens, half, done)
    last = wires.index()
    wires.push(last, lambda: gn_own.at[:, mine], lambda: gn_own.at[:, mine], over)
    lax.fori_loop(2, 4, keep_units, 0)
    wires.sent = bulk
    advance(g_unit)
    wires.sent = owed
    wires.arrive(last, lambda: gn_own.at[:, other])
    wires.sent = owed
    wires.drain()
    wires.sent = bulk
    for k in range(4):
        wires.owe(u_id + k, lambda k=k: half_grads(k))
    for i, cond, device in (
        (0, True, beside), (1, True, over), (2, c > 0, (t, c - 1, d)), (3, c < 3, (t, c + 1, d))
    ):
        only(
            cond,
            functools.partial(
                pl.semaphore_signal, credit.at[i], inc=1, device_id=device, device_id_type=MESH
            ),
        )
    load_qkv = wires.fetch(wires.index(), qkv_kept, qkv_all)
    s_q, s_k, s_o = scratch[:4], scratch[4:8], scratch[8:12]
    t_b = (
        near, lambda k: part_g.at[pl.ds(k * tokens, tokens)], x_in, came.at[pl.ds(0, 4)], came.at[4]
    )
    second = [token_scatter(wires, pos, part_b, branch, t_b, credit)]
    advance(second)
    mixed_t[...] = mixed[...].T
    normed_t[...] = normed_one[...].T
    gains_sum[...] = jnp.zeros_like(gains_sum)

    def norm_two_back(r):
        value, grad = norm_rows(gn_own[r].astype(wide), hidden[r], gain_two)
        home = pl.ds(pl.multiple_of((c * 2 + e) * tokens + r.start, 16), 16)
        total = gy_all[home].astype(wide) + value
        grad_hidden[r] = total
        grad_low[r] = total.astype(low)
        gains_sum[1:2] += grad

    by_rows(tokens, width, norm_two_back)
    advance(second)

    def out_grad(j, carry):
        where = pl.ds(pl.multiple_of(j * 2 * lanes, 256), 2 * lanes)
        nt_all[:, where] = dot_nn(mixed_t[...], grad_low[:, where]).astype(low)
        return carry

    lax.fori_loop(0, 8, out_grad, 0)
    outs = [
        plane_scatter(
            wires, pos,
            lambda k, yy: nt_all.at[:, lane_block(k * 4 + yy * 2 + 1 - e)],
            lambda k, yy: nt_all.at[:, lane_block(k * 4 + yy * 2 + e)],
            n_query, s_o, lambda r, v: go_out.__setitem__(r, v),
        )
    ]
    advance(outs)

    def mix_grad(j, carry):
        where = pl.ds(pl.multiple_of(j * 256, 256), 256)
        grad_mixed[:, where] = times_transposed(grad_low[...], out_all[where, :]).astype(low)
        return carry

    lax.fori_loop(0, n_query // 256, mix_grad, 0)
    advance(outs, 4)
    advance(g_unit)

    scale = HEAD_SIZE ** (-0.5)
    pairs = n_query // 256
    for g in range(2):
        keys = kv_all[:, g * HEAD_SIZE : (g + 1) * HEAD_SIZE]
        values = kv_all[:, n_key + g * HEAD_SIZE : n_key + (g + 1) * HEAD_SIZE]
        dk[...] = jnp.zeros_like(dk)
        dv[...] = jnp.zeros_like(dv)

        def pair(j, carry, g=g, keys=keys, values=values):
            slab = pl.ds(pl.multiple_of((g * pairs + j) * 128, 128), 128)
            q_two, m_two = q_rot[:, slab], grad_mixed[:, slab]
            both = []
            for h in range(2):
                query = q_two[:, h * HEAD_SIZE : (h + 1) * HEAD_SIZE]
                upstream = m_two[:, h * HEAD_SIZE : (h + 1) * HEAD_SIZE]
                probs = head_probs(query, keys, allowed)
                dprob = times_transposed(upstream, values)
                delta = jnp.sum(probs * dprob, axis=-1, keepdims=True)
                grad_scores = (probs * (dprob - delta)).astype(low)
                both.append(dot_nn(grad_scores, keys))
                dk[...] += transposed_times(grad_scores, query)
                dv[...] += transposed_times(probs.astype(low), upstream)
            grads = jnp.concatenate(both, axis=1) * scale
            back = grads * cosine[...] - swap_halves(grads) * sine[...]
            gqkv[:, slab] = back.astype(low)
            return carry

        lax.fori_loop(0, pairs, pair, 0)
        for k in range(4):
            block = slice(k * tokens, (k + 1) * tokens)
            kv_part[k, :, g * HEAD_SIZE : (g + 1) * HEAD_SIZE] = (dk[block] * scale).astype(low)
            kv_part[k, :, n_key + g * HEAD_SIZE : n_key + (g + 1) * HEAD_SIZE] = dv[block].astype(low)
    kvg_id = [wires.index() for _ in range(3)]
    for i in range(3):
        k = lax.rem(c + i + 1, 4)
        wires.push(kvg_id[i], lambda k=k: kv_part.at[k], lambda i=i: kv_in.at[i], (t, k, d))

    def q_block(place, i, where):
        return place.at[pl.ds(pl.multiple_of(i * lanes, 16), lanes), where]

    def q_grad(core, place, where):
        def step(i, carry):
            here = lane_block(i * 2 + core)
            q_block(place, i, where)[...] = dot_nn(normed_t[here, :], gqkv[:, where]).astype(low)
            return carry

        lax.fori_loop(0, 8, step, 0)

    def q_sums(where, scratches, done):
        return plane_scatter(
            wires, pos,
            lambda k, yy: q_block(gy_all, k * 2 + yy, where),
            lambda k, yy: q_block(gq_part, k * 2 + yy, where),
            gq_out.shape[0], scratches, done,
        )

    def done_first(r, value):
        gq_out[r] = value

    def done_rest(r, value):
        gk_out[r] = value[:, :n_key]
        gv_out[r] = value[:, n_key:]

    first, rest = slice(0, n_query), slice(n_query, n_query + 2 * n_key)
    q_grad(1 - e, gy_all, first)
    queries = [q_sums(first, s_q, done_first)]
    advance(queries)
    q_grad(e, gq_part, first)
    advance(queries, 4)
    advance(second)
    advance(g_unit)
    total = kv_part[c].astype(wide)
    for i in range(3):
        wires.arrive(kvg_id[i], lambda: kv_in.at[i])
        total = total + kv_in[i].astype(wide)
    key_grads = total[:, :n_key]
    key_grads = key_grads * cosine[...] - swap_halves(key_grads) * sine[...]
    gqkv[:, n_query : n_query + n_key] = key_grads.astype(low)
    gqkv[:, n_query + n_key :] = total[:, n_key:].astype(low)
    q_grad(1 - e, gy_all, rest)
    others = [q_sums(rest, s_k, done_rest)]
    advance(others)
    q_grad(e, gq_part, rest)
    load_qkv.wait()

    def normed_grad(j, carry):
        where = pl.ds(pl.multiple_of(j * 256, 256), 256)
        pair_out[:, where] = times_transposed(gqkv[...], qkv_all[where, :]).astype(low)
        return carry

    lax.fori_loop(0, width // 256, normed_grad, 0)
    p_id = wires.index()
    wires.push(p_id, lambda: pair_out, lambda: pair_in, (1 - t, c, d))
    advance(others, 4)
    advance(second)
    advance(outs)
    advance(second)
    wires.arrive(p_id, lambda: pair_in)

    def norm_one_back(r):
        upstream = pair_out[r].astype(wide) + pair_in[r].astype(wide)
        value, grad = norm_rows(upstream, states[r].astype(wide), gain_one)
        grad_states[r] = grad_hidden[r] + value
        gains_sum[0:1] += grad

    by_rows(tokens, width, norm_one_back)
    g_id = [wires.index() for _ in range(16)]

    def gain_block(q):
        return gains_sum.at[:, pl.ds(pl.multiple_of(q * lanes, 128), lanes)]

    for i in range(1, 16):
        q = lax.rem(me + i, 16)
        wires.push(
            g_id[i], lambda q=q: gain_block(q), lambda i=i: gain_in.at[i],
            (t, q // 4, lax.rem(q, 4)),
        )
    advance(outs)
    advance(second)
    advance(others)
    advance(outs)
    advance(queries)
    advance(others)
    advance(outs)
    advance(queries)
    advance(others)
    advance(queries)
    advance(others)
    advance(queries)
    advance(second)
    while g_unit:
        advance(g_unit)

    def finish(r):
        layer_out[r] = (hidden[r] + branch[r].astype(wide)).astype(low)

    by_rows(tokens, width, finish)
    gain = gains_sum[:, pl.ds(pl.multiple_of(me * lanes, 128), lanes)]
    for i in range(1, 16):
        wires.arrive(g_id[i], lambda: gain_in.at[i])
        gain = gain + gain_in[i]
    gain_out[...] = gain
    wires.drain()


def layer_call(lengths, states, gains, qkv, out_w, w3, gy, cosine, sine):
    shape = jax.ShapeDtypeStruct
    low, wide = jnp.bfloat16, jnp.float32
    tokens, width = states.shape
    n_query, lanes = out_w.shape
    n_all = qkv.shape[1]
    n_rest = n_all - n_query
    units = w3.shape[1] // 8
    padded = -(-units // 128) * 128
    all_tokens, keys = tokens * 8, tokens * 4
    half = width // 2
    vm = pltpu.VMEM
    return pl.pallas_call(
        layer_kernel,
        name="layer",
        out_shape=(
            shape((tokens, width), low),
            shape((tokens, width), wide),
            shape((3, units * 8, lanes), low),
            shape((lanes, n_query), wide),
            shape((lanes, n_rest // 2), wide),
            shape((lanes, n_rest // 2), wide),
            shape((n_query, lanes), wide),
            shape((8, lanes), wide),
            shape((width, n_all), low),
            shape((all_tokens, width), low),
        ),
        in_specs=[pl.BlockSpec(memory_space=pltpu.MemorySpace.SMEM), pl.BlockSpec(memory_space=VMEM)]
        + [pl.BlockSpec(memory_space=HBM)] * 5
        + [pl.BlockSpec(memory_space=VMEM)] * 2,
        out_specs=[pl.BlockSpec(memory_space=VMEM)] * 2
        + [pl.BlockSpec(memory_space=HBM)]
        + [pl.BlockSpec(memory_space=VMEM)] * 5
        + [pl.BlockSpec(memory_space=HBM)] * 2,
        scratch_shapes=[
            pltpu.SemaphoreType.DMA((320,)),
            pltpu.SemaphoreType.DMA((320,)),
            pltpu.SemaphoreType.REGULAR((4,)),
            vm((width, n_all), low),
            vm((n_query, width), low),
            vm((16, width), low),
            vm((tokens, width), wide),
            vm((tokens, width), low),
            vm((tokens, n_query), low),
            vm((keys, n_rest), low),
            vm((tokens, n_query), low),
            vm((tokens, width), low),
            vm((3, padded, width), low),
            vm((all_tokens, width), low),
            vm((all_tokens, width), low),
            vm((padded, all_tokens), low),
            vm((all_tokens, width), low),
            vm((2 * tokens, width), low),
            vm((4, 3, units, width // 8), low),
            vm((tokens, n_rest), low),
            vm((tokens, width), low),
            vm((tokens, width), low),
            vm((tokens, width), low),
            vm((4, tokens, width), low),
            vm((4, tokens, half), low),
            vm((5, tokens, half), low),
            vm((tokens, width), wide),
            vm((tokens, width), low),
            vm((tokens, width), low),
            vm((n_query, tokens), low),
            vm((tokens, n_query), low),
            vm((tokens, n_all), low),
            vm((width, tokens), low),
            vm((8 * lanes, n_all), low),
            vm((keys, HEAD_SIZE), wide),
            vm((keys, HEAD_SIZE), wide),
            vm((4, tokens, n_rest), low),
            vm((3, tokens, n_rest), low),
            vm((8, width), wide),
            vm((16, 8, lanes), wide),
        ]
        + plane_scratch((lanes, n_query))
        + plane_scratch((lanes, n_rest))
        + plane_scratch((n_query, lanes)),
        compiler_params=pltpu.CompilerParams(
            collective_id=1, has_side_effects=True, vmem_limit_bytes=63 << 20
        ),
    )(lengths, states, gains, qkv, out_w, w3, gy, cosine, sine)


def plane_shards(
    states, lengths, first_gain, w_query, key_matrix, value_matrix, w_out, second_gain,
    w_gate, w_up, w_down, cotangent,
):
    low, wide = jnp.bfloat16, jnp.float32
    tokens = states.shape[1]
    positions = lax.axis_index("ctx") * tokens + jnp.arange(tokens, dtype=jnp.int32)
    cosine, sine = rope_tables(positions, HEAD_SIZE // 2)
    lane = jnp.arange(2 * HEAD_SIZE)
    turn = jnp.where((lane % HEAD_SIZE) < HEAD_SIZE // 2, -1.0, 1.0)
    cosine = jnp.tile(cosine[:, 0], (1, 4))
    sine = jnp.tile(sine[:, 0], (1, 4)) * turn[None, :]
    valid = (positions < lengths[0])[:, None]
    grad_y = jnp.where(valid, cotangent[0], jnp.zeros((), low))
    lanes = w_out.shape[1]
    qkv = jnp.concatenate([w_query, key_matrix, value_matrix], axis=1)
    gains = jnp.concatenate(
        [first_gain[None], second_gain[None], jnp.zeros((14, lanes), low)], axis=0
    )
    w3 = jnp.stack([w_gate.T, w_up.T, w_down])
    layer_out, grad_states, g3, gq, gk, gv, go, gain, _, _ = layer_call(
        lengths, states[0], gains, qkv, w_out, w3, grad_y, cosine, sine
    )
    return (
        layer_out[None],
        grad_states[None],
        gain[0],
        gq,
        gk,
        gv,
        go,
        gain[1],
        g3[0].T.astype(wide),
        g3[1].T.astype(wide),
        g3[2].astype(wide),
    )


def fits(mesh):
    return dict(mesh.shape) == {"tensor": 2, "ctx": 4, "dp": 4}


def solution(mesh):
    placed = (
        P("dp", "ctx", None),
        P("dp"),
        P(("ctx", "dp")),
        P(("ctx", "dp"), "tensor"),
        P(("ctx", "dp"), "tensor"),
        P(("ctx", "dp"), "tensor"),
        P("tensor", ("ctx", "dp")),
        P(("ctx", "dp")),
        P(("ctx", "dp"), "tensor"),
        P(("ctx", "dp"), "tensor"),
        P("tensor", ("ctx", "dp")),
        P("dp", "ctx", None),
    )
    return jax.shard_map(
        plane_shards if fits(mesh) else shards,
        mesh=mesh,
        in_specs=placed,
        out_specs=(
            P("dp", "ctx", None),
            P("dp", "ctx", None),
            P(("ctx", "dp")),
            P(("ctx", "dp"), "tensor"),
            P(("ctx", "dp"), "tensor"),
            P(("ctx", "dp"), "tensor"),
            P("tensor", ("ctx", "dp")),
            P(("ctx", "dp")),
            P(("ctx", "dp"), "tensor"),
            P(("ctx", "dp"), "tensor"),
            P("tensor", ("ctx", "dp")),
        ),
        check_vma=False,
    )
```
